32 devices in a mesh: row: 8 (over z, y), col: 4 (over x, core).
Axes of the slice: x: 2, y: 2, z: 4, core: 2. Of those that a mesh axis runs over, the one named last changes fastest.
Arguments:
- panel: float32 [8, 8, 256, 256], P(None, 'row', None, 'col'), may hold values from -0.1875 to 0.1875
- slab: bfloat16 [8, 8, 256, 4, 4, 256], P(None, 'row', None, None, 'col'), may hold values from -6 to 6
- cotangent: bfloat16 [8, 8, 256, 4, 4, 256], P(None, 'row', None, None, 'col'), may hold values from -0.0625 to 0.0625
- inverse: float32 [256, 256], replicated, may hold values from -2 to 8, as said below
Outputs:
- updated: bfloat16 [8, 8, 256, 4, 4, 256], P(None, 'row', None, None, 'col')
- grad_panel: float32 [8, 8, 256, 256], P(None, 'row', None, 'col')
- grad_inverse: float32 [256, 256], P(None, 'col')
The draws below stay inside these ranges and needn't reach their ends.
Inputs may be any that keep to these rules, and one draw needn't show every extreme that they name: `inverse`: lower triangular; diagonal entries between 4 and 8.
All inputs are finite; a program needn't handle non-finite values.
Results may differ from the reference program's by a relative error of at most 0.015.
Values may be sent and summed in bfloat16 or wider, within the bound.
No kernel may reach another device: no remote copies, remote signals or barrier semaphores. Data moves between devices by JAX's collectives and lax.ppermute only.
A program may use at most 128 MiB of HBM per device.

```python
import jax
import jax.numpy as jnp
from jax import lax

TILE = 256
TR_DEV = 8
TC_DEV = 4
N_ROW = 8
N_COL = 4


def draw_inverse(key, part):
    key_diag = jax.random.fold_in(key, 11)
    key_off = jax.random.fold_in(key, 12)
    diag_vals = jax.random.uniform(key_diag, (TILE,), jnp.float32, 4.0, 8.0)
    off_vals = jnp.clip(0.25 * jax.random.normal(key_off, (TILE, TILE), jnp.float32), -1.5, 1.5)
    lower = jnp.tril(off_vals, -1)
    return (lower + jnp.diag(diag_vals)).astype(jnp.float32)


def level_of(key, extent, shards, least, largest):
    factor_of, own = 1.0, jax.random.fold_in(key, 6)
    for position, parts in shards:
        steps = jnp.exp(jax.random.uniform(jax.random.fold_in(own, position), (parts,), jnp.float32, least / len(shards), largest / len(shards)))
        factor_of = factor_of * jnp.repeat(steps, extent[position] // parts).reshape([-1 if axis == position else 1 for axis in range(len(extent))])
    return factor_of


def noise(rng, extent, deviation, bound, cuts=(), kind=jnp.bfloat16):
    level = level_of(rng, extent, cuts, -0.22, 0.18) if cuts else 1.0
    result = jax.random.normal(rng, extent, jnp.float32) * deviation * level
    return jnp.minimum(jnp.maximum(result, -bound), bound).astype(kind)


def setup_inputs(seed: int = 0) -> dict:
    streams_of = jax.random.split(jax.random.key(seed), 5)
    panel = noise(streams_of[0], (TR_DEV, N_ROW, TILE, TILE), 0.03, 0.1875, ((1, 8), (3, 4)), jnp.float32)
    slab = noise(streams_of[1], (TR_DEV, N_ROW, TILE, TC_DEV, N_COL, TILE), 1.0, 6.0, ((1, 8), (4, 4)))
    cotangent = noise(streams_of[2], (TR_DEV, N_ROW, TILE, TC_DEV, N_COL, TILE), 0.01, 0.0625, ((1, 8), (4, 4)))
    inverse = draw_inverse(jax.random.fold_in(streams_of[4], 71), 0)
    return {"panel": panel, "slab": slab, "cotangent": cotangent, "inverse": inverse}


def reference(panel, slab, cotangent, inverse):
    row_count = TR_DEV * N_ROW * TILE
    slab_width = TC_DEV * N_COL * TILE
    highest = lax.Precision.HIGHEST
    panel_rows = panel.reshape(row_count, TILE)
    factor = jnp.dot(panel_rows, inverse.T, precision=highest, preferred_element_type=jnp.float32)
    rounded = factor.astype(jnp.bfloat16)
    top_rows = rounded[:slab_width]
    slab_rows = slab.reshape(row_count, slab_width)
    product = jnp.dot(rounded, top_rows.T, preferred_element_type=jnp.float32)
    updated = (slab_rows.astype(jnp.float32) - product).astype(jnp.bfloat16)
    cot_rows = cotangent.reshape(row_count, slab_width)
    factor_grad = -jnp.dot(cot_rows, top_rows, preferred_element_type=jnp.float32)
    slab_grad = -jnp.dot(cot_rows.T, rounded, preferred_element_type=jnp.float32)
    factor_grad = factor_grad.at[:slab_width].add(slab_grad)
    grad_panel = jnp.dot(factor_grad, inverse, precision=highest, preferred_element_type=jnp.float32)
    grad_inverse = jnp.dot(factor_grad.T, panel_rows, precision=highest, preferred_element_type=jnp.float32)
    return updated.reshape(slab.shape), grad_panel.reshape(panel.shape), grad_inverse
```

```python
import jax
import jax.numpy as jnp
from jax import lax
from jax.sharding import PartitionSpec as P

BOTH = ("row", "col")
F32 = jnp.float32
BF16 = jnp.bfloat16


def bits_of(count):
    return [1 << b for b in reversed(range(count.bit_length() - 1))]


def swap_order(pieces, index, bit, axis):
    return jnp.where((index & bit) != 0, jnp.flip(pieces, axis), pieces)


def relative_order(pieces, index, count):
    rest = pieces.shape[1:]
    bits = bits_of(count)
    split = pieces.reshape((2,) * len(bits) + rest)
    for axis, bit in enumerate(bits):
        split = swap_order(split, index, bit, axis)
    return split.reshape(pieces.shape)


def per_device(panel, slab, cotangent, inverse):
    tiles, _, tile, strip = panel.shape
    slab_tiles = slab.shape[3]
    n_row = lax.axis_size("row")
    n_col = lax.axis_size("col")
    groups = n_row // n_col
    slots = slab_tiles // groups
    row = lax.axis_index("row")
    col = lax.axis_index("col")
    group, rho = row // n_col, row % n_col
    highest = lax.Precision.HIGHEST

    def permute_row(value, bit):
        return lax.ppermute(value, "row", [(i, i ^ bit) for i in range(n_row)])

    def permute_col(value, bit):
        return lax.ppermute(value, "col", [(i, i ^ bit) for i in range(n_col)])

    def transpose(value):
        pairs = []
        for m in range(groups):
            for a in range(n_col):
                for b in range(n_col):
                    pairs.append(((m * n_col + a) * n_col + b, (m * n_col + b) * n_col + a))
        return lax.ppermute(value, BOTH, pairs)

    def dot(a, b, dims, precision=None):
        return lax.dot_general(a, b, (dims, ((), ())), precision=precision, preferred_element_type=F32)

    own = panel.reshape(tiles, tile, strip).transpose(0, 2, 1).astype(BF16)
    top = transpose(own[:slots])[None]
    for bit in bits_of(n_row):
        top = jnp.concatenate([top, permute_row(top, bit)], 0)
    parts = {0: own}
    for bit in bits_of(n_col):
        for q in list(parts):
            parts[q | bit] = permute_col(parts[q], bit)
    gathered = jnp.stack([parts[q] for q in range(n_col)], 0)
    n_bits = len(bits_of(n_row))
    top = top.reshape((2,) * n_bits + top.shape[1:])
    top = top.transpose(tuple(reversed(range(n_bits))) + tuple(range(n_bits, n_bits + 3)))
    top = top.reshape(groups, n_col, slots, strip, tile)
    top = relative_order(top, group, groups).transpose(2, 0, 1, 3, 4).reshape(slab_tiles, tile, tile)
    gathered = gathered.transpose(0, 2, 1, 3).reshape(tile, tiles * tile)

    strips = inverse.reshape(tile, n_col, strip).transpose(1, 0, 2)
    inv_col = relative_order(strips, col, n_col).transpose(1, 0, 2).reshape(tile, tile)
    inv_row = relative_order(strips, rho, n_col).transpose(1, 0, 2).reshape(tile, tile)
    mat = dot(inv_col, inv_row, ((0,), (0,)), highest)

    slab_rows = slab.reshape(tiles * tile, slab_tiles * tile)
    cot_rows = cotangent.reshape(tiles * tile, slab_tiles * tile)
    q_sum = dot(gathered, cot_rows, ((1,), (0,)))
    q_round = q_sum.astype(BF16)

    def split_dot(a32, b16, dims):
        hi = a32.astype(BF16)
        lo = (a32 - hi.astype(F32)).astype(BF16)
        return dot(hi, b16, dims) + dot(lo, b16, dims)

    e_part = -split_dot(mat, q_round, ((0,), (0,)))
    e_part = e_part.reshape(n_col, strip, slots, groups, tile).transpose(3, 0, 2, 1, 4)
    e_part = relative_order(e_part, group, groups)
    e_part = e_part.reshape(n_row, slots, strip, tile).astype(BF16)
    for bit in bits_of(n_row):
        e_part = e_part.reshape((2, bit) + e_part.shape[1:])
        e_part = (e_part[0].astype(F32) + permute_row(e_part[1], bit).astype(F32)).astype(BF16)
    e_own = transpose(e_part[0])

    top_flat = top.transpose(1, 0, 2).reshape(tile, slab_tiles * tile)
    w = split_dot(mat, top_flat, ((1,), (0,))).astype(BF16)
    product = dot(gathered, w, ((0,), (0,)))
    updated = (slab_rows.astype(F32) - product).astype(BF16)
    h = -dot(w, cot_rows, ((1,), (1,)))
    h = h.reshape(n_col, strip, tiles, tile).transpose(0, 2, 1, 3)

    z_rows = dot(q_round, top_flat, ((1,), (1,)))
    to_natural_row = relative_order(
        z_rows.reshape(tile, n_col, strip).transpose(1, 0, 2), rho, n_col
    ).transpose(1, 0, 2).reshape(tile, tile)
    z_nat = relative_order(
        to_natural_row.reshape(n_col, strip, tile), col, n_col
    ).reshape(tile, tile)
    z_both = z_nat + z_nat.T
    gi = -dot(z_both, inverse, ((1,), (1,)), highest)
    gi = relative_order(gi.reshape(n_col, strip, tile), col, n_col)

    sums = jnp.concatenate([h, gi[:, None]], 1).astype(BF16)
    for bit in reversed(bits_of(n_col)):
        sums = sums.reshape((sums.shape[0] // 2, 2) + sums.shape[1:])
        sums = (sums[:, 0].astype(F32) + permute_col(sums[:, 1], bit).astype(F32))
        if sums.shape[0] > 1:
            sums = sums.astype(BF16)
    sums = sums[0]
    grad_panel = sums[:tiles]
    grad_panel = jnp.concatenate([grad_panel[:slots] + e_own.astype(F32), grad_panel[slots:]], 0)
    gi_sum = sums[tiles]
    for bit in bits_of(n_row):
        gi_sum = gi_sum + permute_row(gi_sum, bit)
    return (
        updated.reshape(slab.shape),
        grad_panel.transpose(0, 2, 1).reshape(panel.shape),
        gi_sum.T,
    )


def solution(mesh):
    in_specs = (
        P(None, "row", None, "col"),
        P(None, "row", None, None, "col", None),
        P(None, "row", None, None, "col", None),
        P(),
    )
    out_specs = (
        P(None, "row", None, None, "col", None),
        P(None, "row", None, "col"),
        P(None, "col"),
    )
    return jax.shard_map(
        per_device, mesh=mesh, in_specs=in_specs, out_specs=out_specs, check_vma=False
    )
```

```python
import functools

import jax
import jax.numpy as jnp
from jax import lax
from jax.experimental import pallas as pl
from jax.experimental.pallas import tpu as pltpu
from jax.sharding import PartitionSpec as P

BOTH = ("row", "col")
F32 = jnp.float32
BF16 = jnp.bfloat16
LANES = 128
VMEM = pl.BlockSpec(memory_space=pltpu.VMEM)
SMEM = pl.BlockSpec(memory_space=pltpu.SMEM)


def bits_of(count):
    return [1 << b for b in reversed(range(count.bit_length() - 1))]


def reversed_bits(value, count):
    width = count.bit_length() - 1
    place = 0
    for b in range(width):
        place = place + (((value >> b) & 1) << (width - 1 - b))
    return place


def dot(a, b, dims, precision=None):
    return lax.dot_general(a, b, (dims, ((), ())), precision=precision, preferred_element_type=F32)


def whole(shape):
    return pl.BlockSpec(shape, lambda *_: (0,) * len(shape))


def params():
    return pltpu.CompilerParams(vmem_limit_bytes=24 * 2**20)


def cost(flops, nbytes):
    return pl.CostEstimate(flops=flops, bytes_accessed=nbytes, transcendentals=0)


def unmix_kernel(slabs, tile, x_ref, o_ref, wide_ref):
    halves = tile // LANES
    wide_ref[...] = x_ref[...].astype(F32)
    for s in range(slabs):
        for h in range(halves):
            part = wide_ref[pl.ds(h * slabs + s, tile, stride=halves * slabs), :]
            o_ref[:, s * tile + h * LANES : s * tile + (h + 1) * LANES] = part.astype(BF16)


def q_kernel(n_row, n_col, groups, place_ref, *refs):
    parts, (m_ref, g_ref, q_ref, e_ref, pt_ref) = refs[:n_col], refs[n_col:]
    tiles, strip, tile = parts[0].shape
    s = pl.program_id(0)
    row, col = place_ref[0], place_ref[1]
    group, rho = row // n_col, row % n_col

    @pl.when(s == 0)
    def _():
        for q in range(n_col):
            at = pl.multiple_of((col ^ q) * strip, strip)
            for t in range(tiles):
                pt_ref[pl.ds(at, strip), t * tile : (t + 1) * tile] = parts[q][t]

    q_val = dot(pt_ref[...], g_ref[...], ((1,), (0,))).astype(BF16)
    q_ref[0] = q_val
    e_val = -(dot(m_ref[0], q_val, ((1,), (0,))) + dot(m_ref[1], q_val, ((1,), (0,))))
    e_val = e_val.astype(BF16)
    slot, other = s // groups, group ^ (s % groups)
    for r in range(n_col):
        place = reversed_bits(other * n_col + (rho ^ r), n_row)
        e_ref[place, slot] = e_val[r * strip : (r + 1) * strip]


def h_kernel(n_row, n_col, groups, place_ref, top_ref, m_ref, inv_ref, q_ref, g_ref, w_ref, h_ref, top_all):
    slots, strip, tile = top_ref.shape[1:]
    slabs = slots * groups
    t = pl.program_id(0)
    tiles = pl.num_programs(0)
    row, col = place_ref[0], place_ref[1]
    group, rho = row // n_col, row % n_col

    def put(at, value):
        for r in range(n_col):
            h_ref[reversed_bits(col ^ r, n_col), at] = value[r * strip : (r + 1) * strip].astype(BF16)

    @pl.when(t == 0)
    def _():
        for p in range(n_row):
            at = pl.multiple_of((rho ^ (p % n_col)) * strip, strip)
            for slot in range(slots):
                s = slot * groups + (group ^ (p // n_col))
                top_all[s, pl.ds(at, strip), :] = top_ref[reversed_bits(p, n_row), slot]
        z = jnp.zeros((tile, tile), F32)
        for s in range(slabs):
            top = top_all[s]
            w = dot(m_ref[0], top, ((1,), (0,))) + dot(m_ref[1], top, ((1,), (0,)))
            w_ref[:, s * tile : (s + 1) * tile] = w.astype(BF16)
            z = z + dot(top, q_ref[s], ((1,), (1,)))
        z = z + z.T
        put(tiles, -dot(z, inv_ref[...], ((1,), (1,)), lax.Precision.HIGHEST))

    put(t, -dot(w_ref[...], g_ref[...], ((1,), (1,))))


def update_kernel(slabs, tile, pt_ref, w_ref, x_ref, o_ref, wide_ref):
    halves = tile // LANES
    product = dot(pt_ref[...], w_ref[...], ((0,), (0,)))
    for s in range(slabs):
        for h in range(halves):
            part = product[:, s * tile + h * LANES : s * tile + (h + 1) * LANES]
            wide_ref[pl.ds(h * slabs + s, tile, stride=halves * slabs), :] = part
    o_ref[...] = (x_ref[...].astype(F32) - wide_ref[...]).astype(BF16)


def mixed_rows(x):
    tiles, _, tile, slabs, _, _ = x.shape
    x = x.reshape(tiles, tile, slabs, tile // LANES, LANES).transpose(0, 1, 3, 2, 4)
    return x.reshape(-1, LANES)


def per_device(panel, slab, cotangent, inverse):
    tiles, _, tile, strip = panel.shape
    slabs = slab.shape[3]
    n_row = lax.axis_size("row")
    n_col = lax.axis_size("col")
    groups = n_row // n_col
    slots = slabs // groups
    width = slabs * tile
    rows = tiles * tile
    mixed = tile * width // LANES
    place = jnp.stack([lax.axis_index("row"), lax.axis_index("col")]).astype(jnp.int32)

    def permute_row(value, bit):
        return lax.ppermute(value, "row", [(i, i ^ bit) for i in range(n_row)])

    def permute_col(value, bit):
        return lax.ppermute(value, "col", [(i, i ^ bit) for i in range(n_col)])

    def transpose(value):
        pairs = []
        for m in range(groups):
            for a in range(n_col):
                for b in range(n_col):
                    pairs.append(((m * n_col + a) * n_col + b, (m * n_col + b) * n_col + a))
        return lax.ppermute(value, BOTH, pairs)

    own = panel.reshape(tiles, tile, strip).transpose(0, 2, 1).astype(BF16)
    top = transpose(own[:slots])[None]
    parts = {0: own}
    for bit in bits_of(n_col):
        for q in list(parts):
            parts[q | bit] = permute_col(parts[q], bit)
    for bit in bits_of(n_row):
        top = jnp.concatenate([top, permute_row(top, bit)], 0)

    mat = dot(inverse, inverse, ((0,), (0,)), lax.Precision.HIGHEST)
    mat_hi = mat.astype(BF16)
    mat = jnp.stack([mat_hi, (mat - mat_hi.astype(F32)).astype(BF16)])

    cot = pl.pallas_call(
        functools.partial(unmix_kernel, slabs, tile),
        grid=(tiles,),
        in_specs=[pl.BlockSpec((mixed, LANES), lambda t: (t, 0))],
        out_specs=pl.BlockSpec((tile, width), lambda t: (t, 0)),
        out_shape=jax.ShapeDtypeStruct((rows, width), BF16),
        scratch_shapes=[pltpu.VMEM((mixed, LANES), F32)],
        compiler_params=params(),
        cost_estimate=cost(0, 4 * rows * width),
    )(mixed_rows(cotangent))

    q_sum, e_part, panel_all = pl.pallas_call(
        functools.partial(q_kernel, n_row, n_col, groups),
        grid=(slabs,),
        in_specs=[SMEM]
        + [whole((tiles, strip, tile))] * n_col
        + [whole((2, tile, tile)), pl.BlockSpec((rows, tile), lambda s: (0, s))],
        out_specs=[
            pl.BlockSpec((1, tile, tile), lambda s: (s, 0, 0)),
            whole((n_row, slots, strip, tile)),
            whole((tile, rows)),
        ],
        out_shape=[
            jax.ShapeDtypeStruct((slabs, tile, tile), BF16),
            jax.ShapeDtypeStruct((n_row, slots, strip, tile), BF16),
            jax.ShapeDtypeStruct((tile, rows), BF16),
        ],
        compiler_params=params(),
        cost_estimate=cost(2 * rows * width * tile, 2 * rows * (width + tile)),
    )(place, *[parts[q] for q in range(n_col)], mat, cot)

    w, h = pl.pallas_call(
        functools.partial(h_kernel, n_row, n_col, groups),
        grid=(tiles,),
        in_specs=[
            SMEM,
            whole((n_row, slots, strip, tile)),
            whole((2, tile, tile)),
            whole((tile, tile)),
            whole((slabs, tile, tile)),
            pl.BlockSpec((tile, width), lambda t: (t, 0)),
        ],
        out_specs=[whole((tile, width)), whole((n_col, tiles + 1, strip, tile))],
        out_shape=[
            jax.ShapeDtypeStruct((tile, width), BF16),
            jax.ShapeDtypeStruct((n_col, tiles + 1, strip, tile), BF16),
        ],
        scratch_shapes=[pltpu.VMEM((slabs, tile, tile), BF16)],
        compiler_params=params(),
        cost_estimate=cost(2 * rows * width * tile, 2 * rows * (width + tile)),
    )(place, top, mat, inverse, q_sum, cot)

    updated = pl.pallas_call(
        functools.partial(update_kernel, slabs, tile),
        grid=(tiles,),
        in_specs=[
            pl.BlockSpec((tile, tile), lambda t: (0, t)),
            whole((tile, width)),
            pl.BlockSpec((mixed, LANES), lambda t: (t, 0)),
        ],
        out_specs=pl.BlockSpec((mixed, LANES), lambda t: (t, 0)),
        out_shape=jax.ShapeDtypeStruct((tiles * mixed, LANES), BF16),
        scratch_shapes=[pltpu.VMEM((mixed, LANES), F32)],
        compiler_params=params(),
        cost_estimate=cost(2 * rows * width * tile, 4 * rows * width),
    )(panel_all, w, mixed_rows(slab))
    updated = updated.reshape(tiles, tile, tile // LANES, slabs, LANES).transpose(0, 1, 3, 2, 4)

    def halve(value, exchange, bit):
        half = value.shape[0] // 2
        return value[:half].astype(F32) + exchange(value[half:], bit).astype(F32)

    for bit in reversed(bits_of(n_row)):
        e_part = halve(e_part, permute_row, bit).astype(BF16)
    e_own = transpose(e_part[0])

    for bit in reversed(bits_of(n_col)):
        h = halve(h.astype(BF16), permute_col, bit)
    h = h[0]
    grad_panel = jnp.concatenate([h[:slots] + e_own.astype(F32), h[slots:tiles]], 0)
    gi_sum = h[tiles]
    for bit in bits_of(n_row):
        gi_sum = gi_sum + permute_row(gi_sum, bit)
    return (
        updated.reshape(slab.shape),
        grad_panel.transpose(0, 2, 1).reshape(panel.shape),
        gi_sum.T,
    )


def solution(mesh):
    in_specs = (
        P(None, "row", None, "col"),
        P(None, "row", None, None, "col", None),
        P(None, "row", None, None, "col", None),
        P(),
    )
    out_specs = (
        P(None, "row", None, None, "col", None),
        P(None, "row", None, "col"),
        P(None, "col"),
    )
    return jax.shard_map(
        per_device, mesh=mesh, in_specs=in_specs, out_specs=out_specs, check_vma=False
    )
```

```python
import functools

import jax
import jax.numpy as jnp
from jax import lax
from jax.experimental import pallas as pl
from jax.experimental.pallas import tpu as pltpu
from jax.sharding import PartitionSpec as P

BOTH = ("row", "col")
F32 = jnp.float32
BF16 = jnp.bfloat16
LANES = 128
VMEM = pl.BlockSpec(memory_space=pltpu.VMEM)
SMEM = pl.BlockSpec(memory_space=pltpu.SMEM)


def bits_of(count):
    return [1 << b for b in reversed(range(count.bit_length() - 1))]


def reversed_bits(value, count):
    width = count.bit_length() - 1
    place = 0
    for b in range(width):
        place = place + (((value >> b) & 1) << (width - 1 - b))
    return place


def dot(a, b, dims, precision=None):
    return lax.dot_general(a, b, (dims, ((), ())), precision=precision, preferred_element_type=F32)


def whole(shape):
    return pl.BlockSpec(shape, lambda *_: (0,) * len(shape))


def params():
    return pltpu.CompilerParams(vmem_limit_bytes=24 * 2**20)


def cost(flops, nbytes):
    return pl.CostEstimate(flops=flops, bytes_accessed=nbytes, transcendentals=0)


def unmix_kernel(slabs, tile, x_ref, o_ref, wide_ref):
    halves = tile // LANES
    wide_ref[...] = x_ref[...].astype(F32)
    for s in range(slabs):
        for h in range(halves):
            part = wide_ref[pl.ds(h * slabs + s, tile, stride=halves * slabs), :]
            o_ref[:, s * tile + h * LANES : s * tile + (h + 1) * LANES] = part.astype(BF16)


def q_kernel(n_row, n_col, groups, place_ref, *refs):
    parts, (m_ref, g_ref, q_ref, e_ref, pt_ref) = refs[:n_col], refs[n_col:]
    tiles, strip, tile = parts[0].shape
    s = pl.program_id(0)
    row, col = place_ref[0], place_ref[1]
    group, rho = row // n_col, row % n_col

    @pl.when(s == 0)
    def _():
        for q in range(n_col):
            at = pl.multiple_of((col ^ q) * strip, strip)
            for t in range(tiles):
                pt_ref[pl.ds(at, strip), t * tile : (t + 1) * tile] = parts[q][t]

    q_val = dot(pt_ref[...], g_ref[...], ((1,), (0,))).astype(BF16)
    q_ref[0] = q_val
    e_val = -(dot(m_ref[0], q_val, ((1,), (0,))) + dot(m_ref[1], q_val, ((1,), (0,))))
    e_val = e_val.astype(BF16)
    slot, other = s // groups, group ^ (s % groups)
    for r in range(n_col):
        place = reversed_bits(rho ^ r, n_col) * groups + other
        e_ref[place, slot] = e_val[r * strip : (r + 1) * strip]


def w_kernel(n_row, n_col, groups, place_ref, *refs):
    tops, (m_ref, inv_ref, q_ref, w_ref, gi_ref, top_all) = refs[:2], refs[2:]
    slots, strip, tile = tops[0].shape[1:]
    half = tops[0].shape[0]
    slabs = slots * groups
    row, col = place_ref[0], place_ref[1]
    group, rho = row // n_col, row % n_col
    for p in range(n_row):
        at = pl.multiple_of((rho ^ (p % n_col)) * strip, strip)
        place = reversed_bits(p % n_col, n_col) * groups + p // n_col
        for slot in range(slots):
            s = slot * groups + (group ^ (p // n_col))
            top_all[s, pl.ds(at, strip), :] = tops[place // half][place % half, slot]
    z = jnp.zeros((tile, tile), F32)
    for s in range(slabs):
        top = top_all[s]
        w = dot(m_ref[0], top, ((1,), (0,))) + dot(m_ref[1], top, ((1,), (0,)))
        w_ref[:, s * tile : (s + 1) * tile] = w.astype(BF16)
        z = z + dot(top, q_ref[s], ((1,), (1,)))
    z = z + z.T
    gi = -dot(z, inv_ref[...], ((1,), (1,)), lax.Precision.HIGHEST)
    for r in range(n_col):
        gi_ref[col ^ r] = gi[r * strip : (r + 1) * strip].astype(BF16)


def h_kernel(n_col, place_ref, w_ref, g_ref, h_ref):
    strip = h_ref.shape[2]
    t = pl.program_id(0)
    col = place_ref[1]
    h = -dot(w_ref[...], g_ref[...], ((1,), (1,)))
    for r in range(n_col):
        h_ref[reversed_bits(col ^ r, n_col), t] = h[r * strip : (r + 1) * strip].astype(BF16)


def update_kernel(slabs, tile, pt_ref, w_ref, x_ref, o_ref, wide_ref):
    halves = tile // LANES
    product = dot(pt_ref[...], w_ref[...], ((0,), (0,)))
    for s in range(slabs):
        for h in range(halves):
            part = product[:, s * tile + h * LANES : s * tile + (h + 1) * LANES]
            wide_ref[pl.ds(h * slabs + s, tile, stride=halves * slabs), :] = part
    o_ref[...] = (x_ref[...].astype(F32) - wide_ref[...]).astype(BF16)


def mixed_rows(x):
    tiles, _, tile, slabs, _, _ = x.shape
    x = x.reshape(tiles, tile, slabs, tile // LANES, LANES).transpose(0, 1, 3, 2, 4)
    return x.reshape(-1, LANES)


def per_device(panel, slab, cotangent, inverse):
    tiles, _, tile, strip = panel.shape
    slabs = slab.shape[3]
    n_row = lax.axis_size("row")
    n_col = lax.axis_size("col")
    groups = n_row // n_col
    slots = slabs // groups
    width = slabs * tile
    rows = tiles * tile
    mixed = tile * width // LANES
    place = jnp.stack([lax.axis_index("row"), lax.axis_index("col")]).astype(jnp.int32)

    def permute_row(value, bit):
        return lax.ppermute(value, "row", [(i, i ^ bit) for i in range(n_row)])

    def permute_col(value, bit):
        return lax.ppermute(value, "col", [(i, i ^ bit) for i in range(n_col)])

    def transpose(value, across):
        pairs = []
        for m in range(groups):
            for a in range(n_col):
                for b in range(n_col):
                    target = (m ^ across) * n_col + b
                    pairs.append(((m * n_col + a) * n_col + b, target * n_col + a))
        return lax.ppermute(value, BOTH, pairs)

    own = panel.reshape(tiles, tile, strip).transpose(0, 2, 1).astype(BF16)
    high, *lower = bits_of(n_col)
    parts = {0: own, high: permute_col(own, high)}
    if lower:
        parts[1] = permute_col(own, 1)
    tops = [transpose(own[:slots], m) for m in range(groups)]
    mat = dot(inverse, inverse, ((0,), (0,)), lax.Precision.HIGHEST)
    mat_hi = mat.astype(BF16)
    mat = jnp.stack([mat_hi, (mat - mat_hi.astype(F32)).astype(BF16)])

    cot = pl.pallas_call(
        functools.partial(unmix_kernel, slabs, tile),
        grid=(tiles,),
        in_specs=[pl.BlockSpec((mixed, LANES), lambda t: (t, 0))],
        out_specs=pl.BlockSpec((tile, width), lambda t: (t, 0)),
        out_shape=jax.ShapeDtypeStruct((rows, width), BF16),
        scratch_shapes=[pltpu.VMEM((mixed, LANES), F32)],
        compiler_params=params(),
        cost_estimate=cost(0, 4 * rows * width),
    )(mixed_rows(cotangent))

    parts, mat, cot, tops = lax.optimization_barrier((parts, mat, cot, tops))
    top = jnp.stack(tops)
    for bit in lower:
        for q in range(0, n_col, 2 * bit):
            if q | bit not in parts:
                parts[q | bit] = permute_col(parts[q], bit)
    for bit in bits_of(n_col)[:-1]:
        top = jnp.concatenate([top, permute_row(top, bit)], 0)
    tops = [top, permute_row(top, 1)]

    q_sum, e_part, panel_all = pl.pallas_call(
        functools.partial(q_kernel, n_row, n_col, groups),
        grid=(slabs,),
        in_specs=[SMEM]
        + [whole((tiles, strip, tile))] * n_col
        + [whole((2, tile, tile)), pl.BlockSpec((rows, tile), lambda s: (0, s))],
        out_specs=[
            pl.BlockSpec((1, tile, tile), lambda s: (s, 0, 0)),
            whole((n_row, slots, strip, tile)),
            whole((tile, rows)),
        ],
        out_shape=[
            jax.ShapeDtypeStruct((slabs, tile, tile), BF16),
            jax.ShapeDtypeStruct((n_row, slots, strip, tile), BF16),
            jax.ShapeDtypeStruct((tile, rows), BF16),
        ],
        compiler_params=params(),
        cost_estimate=cost(2 * rows * width * tile, 2 * rows * (width + tile)),
    )(place, *[parts[q] for q in range(n_col)], mat, cot)

    w, gi = pl.pallas_call(
        functools.partial(w_kernel, n_row, n_col, groups),
        in_specs=[SMEM] + [VMEM] * 5,
        out_specs=[VMEM, VMEM],
        out_shape=[
            jax.ShapeDtypeStruct((tile, width), BF16),
            jax.ShapeDtypeStruct((n_col, strip, tile), BF16),
        ],
        scratch_shapes=[pltpu.VMEM((slabs, tile, tile), BF16)],
        compiler_params=params(),
        cost_estimate=cost(6 * tile * tile * width, 8 * tile * width),
    )(place, *tops, mat, inverse, q_sum)

    h = pl.pallas_call(
        functools.partial(h_kernel, n_col),
        grid=(tiles,),
        in_specs=[SMEM, whole((tile, width)), pl.BlockSpec((tile, width), lambda t: (t, 0))],
        out_specs=whole((n_col, tiles, strip, tile)),
        out_shape=jax.ShapeDtypeStruct((n_col, tiles, strip, tile), BF16),
        compiler_params=params(),
        cost_estimate=cost(2 * rows * width * tile, 2 * rows * (width + tile)),
    )(place, w, cot)

    def halve(value, exchange, bit):
        half = value.shape[0] // 2
        return value[:half].astype(F32) + exchange(value[half:], bit).astype(F32)

    def sum_all(values):
        values = [v.astype(F32) for v in values]
        while len(values) > 1:
            values = [values[i] + values[i + 1] for i in range(0, len(values), 2)]
        return values[0]

    def row_sum(value, bits):
        steps = [sum(b for k, b in enumerate(bits) if (q >> k) & 1) for q in range(1 << len(bits))]
        return sum_all([value] + [permute_row(value, step) for step in steps[1:]])

    col_bits, row_bits = list(reversed(bits_of(n_col))), list(reversed(bits_of(n_row)))
    e_part = halve(e_part, permute_row, 1).astype(BF16)
    gi = sum_all([gi[0]] + [permute_col(gi[q], q) for q in range(1, n_col)]).astype(BF16)
    e_part, gi, h = lax.optimization_barrier((e_part, gi, h))

    for bit in col_bits[1:]:
        e_part = halve(e_part, permute_row, bit).astype(BF16)
    gi = row_sum(gi, row_bits[1:3]).astype(BF16)
    h = halve(h, permute_col, 1).astype(BF16)
    e_part, gi, h, w = lax.optimization_barrier((e_part, gi, h, w))

    updated = pl.pallas_call(
        functools.partial(update_kernel, slabs, tile),
        grid=(tiles,),
        in_specs=[
            pl.BlockSpec((tile, tile), lambda t: (0, t)),
            whole((tile, width)),
            pl.BlockSpec((mixed, LANES), lambda t: (t, 0)),
        ],
        out_specs=pl.BlockSpec((mixed, LANES), lambda t: (t, 0)),
        out_shape=jax.ShapeDtypeStruct((tiles * mixed, LANES), BF16),
        scratch_shapes=[pltpu.VMEM((mixed, LANES), F32)],
        compiler_params=params(),
        cost_estimate=cost(2 * rows * width * tile, 4 * rows * width),
    )(panel_all, w, mixed_rows(slab))
    updated = updated.reshape(tiles, tile, tile // LANES, slabs, LANES).transpose(0, 1, 3, 2, 4)

    e_own = sum_all([transpose(e_part[m], m) for m in range(groups)])
    gi = row_sum(gi, row_bits[:1])
    for i in range(3, len(row_bits), 2):
        gi = row_sum(gi.astype(BF16), row_bits[i : i + 2])
    for bit in col_bits[1:]:
        h = halve(h.astype(BF16), permute_col, bit)
    h = h[0]
    grad_panel = jnp.concatenate([h[:slots] + e_own, h[slots:]], 0)
    return (
        updated.reshape(slab.shape),
        grad_panel.transpose(0, 2, 1).reshape(panel.shape),
        gi.T,
    )


def solution(mesh):
    in_specs = (
        P(None, "row", None, "col"),
        P(None, "row", None, None, "col", None),
        P(None, "row", None, None, "col", None),
        P(),
    )
    out_specs = (
        P(None, "row", None, None, "col", None),
        P(None, "row", None, "col"),
        P(None, "col"),
    )
    return jax.shard_map(
        per_device, mesh=mesh, in_specs=in_specs, out_specs=out_specs, check_vma=False
    )
```

```python
import functools

import jax
import jax.numpy as jnp
from jax import lax
from jax.experimental import pallas as pl
from jax.experimental.pallas import tpu as pltpu
from jax.sharding import PartitionSpec as P

BOTH = ("row", "col")
F32 = jnp.float32
BF16 = jnp.bfloat16
LANES = 128
VMEM = pl.BlockSpec(memory_space=pltpu.VMEM)
SMEM = pl.BlockSpec(memory_space=pltpu.SMEM)
STREAMED = 58


def bits_of(count):
    return [1 << b for b in reversed(range(count.bit_length() - 1))]


def reversed_bits(value, count):
    width = count.bit_length() - 1
    place = 0
    for b in range(width):
        place = place + (((value >> b) & 1) << (width - 1 - b))
    return place


def dot(a, b, dims, precision=None):
    return lax.dot_general(a, b, (dims, ((), ())), precision=precision, preferred_element_type=F32)


def whole(shape):
    return pl.BlockSpec(shape, lambda *_: (0,) * len(shape))


def params(mib=24):
    return pltpu.CompilerParams(vmem_limit_bytes=mib * 2**20)


def cost(flops, nbytes):
    return pl.CostEstimate(flops=flops, bytes_accessed=nbytes, transcendentals=0)


def unmix_kernel(slabs, tile, x_ref, o_ref, wide_ref):
    halves = tile // LANES
    wide_ref[...] = x_ref[...].astype(F32)
    for s in range(slabs):
        for h in range(halves):
            part = wide_ref[pl.ds(h * slabs + s, tile, stride=halves * slabs), :]
            o_ref[:, s * tile + h * LANES : s * tile + (h + 1) * LANES] = part.astype(BF16)


def q_kernel(n_row, n_col, groups, place_ref, *refs):
    parts, (m_ref, g_ref, q_ref, e_ref, pt_ref) = refs[:n_col], refs[n_col:]
    tiles, strip, tile = parts[0].shape
    s = pl.program_id(0)
    row, col = place_ref[0], place_ref[1]
    group, rho = row // n_col, row % n_col

    @pl.when(s == 0)
    def _():
        for q in range(n_col):
            at = pl.multiple_of((col ^ q) * strip, strip)
            for t in range(tiles):
                pt_ref[pl.ds(at, strip), t * tile : (t + 1) * tile] = parts[q][t]

    q_val = dot(pt_ref[...], g_ref[...], ((1,), (0,))).astype(BF16)
    q_ref[0] = q_val
    e_val = -(dot(m_ref[0], q_val, ((1,), (0,))) + dot(m_ref[1], q_val, ((1,), (0,))))
    e_val = e_val.astype(BF16)
    slot, other = s // groups, group ^ (s % groups)
    for r in range(n_col):
        place = reversed_bits(rho ^ r, n_col) * groups + other
        e_ref[place, slot] = e_val[r * strip : (r + 1) * strip]


def w_kernel(n_row, n_col, groups, place_ref, *refs):
    tops, (m_ref, inv_ref, q_ref, w_ref, gi_ref, top_all) = refs[:2], refs[2:]
    slots, strip, tile = tops[0].shape[1:]
    half = tops[0].shape[0]
    slabs = slots * groups
    row, col = place_ref[0], place_ref[1]
    group, rho = row // n_col, row % n_col
    for p in range(n_row):
        at = pl.multiple_of((rho ^ (p % n_col)) * strip, strip)
        place = reversed_bits(p % n_col, n_col) * groups + p // n_col
        for slot in range(slots):
            s = slot * groups + (group ^ (p // n_col))
            top_all[s, pl.ds(at, strip), :] = tops[place // half][place % half, slot]
    z = jnp.zeros((tile, tile), F32)
    for s in range(slabs):
        top = top_all[s]
        w = dot(m_ref[0], top, ((1,), (0,))) + dot(m_ref[1], top, ((1,), (0,)))
        w_ref[:, s * tile : (s + 1) * tile] = w.astype(BF16)
        z = z + dot(top, q_ref[s], ((1,), (1,)))
    z = z + z.T
    gi = -dot(z, inv_ref[...], ((1,), (1,)), lax.Precision.HIGHEST)
    for r in range(n_col):
        gi_ref[col ^ r] = gi[r * strip : (r + 1) * strip].astype(BF16)


def h_kernel(n_col, place_ref, w_ref, g_ref, h_ref):
    strip = h_ref.shape[2]
    t = pl.program_id(0)
    col = place_ref[1]
    h = -dot(w_ref[...], g_ref[...], ((1,), (1,)))
    for r in range(n_col):
        h_ref[col ^ r, t] = h[r * strip : (r + 1) * strip].astype(BF16)


def update_kernel(slabs, tile, pt_ref, w_ref, x_ref, *refs):
    o_ref, wide_ref = refs[-2:]
    halves = tile // LANES
    product = dot(pt_ref[...], w_ref[...], ((0,), (0,)))
    for s in range(slabs):
        for h in range(halves):
            part = product[:, s * tile + h * LANES : s * tile + (h + 1) * LANES]
            wide_ref[pl.ds(h * slabs + s, tile, stride=halves * slabs), :] = part
    o_ref[...] = (x_ref[...].astype(F32) - wide_ref[...]).astype(BF16)


def mixed_rows(x):
    tiles, _, tile, slabs, _, _ = x.shape
    x = x.reshape(tiles, tile, slabs, tile // LANES, LANES).transpose(0, 1, 3, 2, 4)
    return x.reshape(-1, LANES)


def per_device(panel, slab, cotangent, inverse):
    tiles, _, tile, strip = panel.shape
    slabs = slab.shape[3]
    n_row = lax.axis_size("row")
    n_col = lax.axis_size("col")
    groups = n_row // n_col
    slots = slabs // groups
    width = slabs * tile
    rows = tiles * tile
    mixed = tile * width // LANES
    place = jnp.stack([lax.axis_index("row"), lax.axis_index("col")]).astype(jnp.int32)

    def permute_row(value, bit):
        return lax.ppermute(value, "row", [(i, i ^ bit) for i in range(n_row)])

    def permute_col(value, bit):
        return lax.ppermute(value, "col", [(i, i ^ bit) for i in range(n_col)])

    def transpose(value, across):
        pairs = []
        for m in range(groups):
            for a in range(n_col):
                for b in range(n_col):
                    target = (m ^ across) * n_col + b
                    pairs.append(((m * n_col + a) * n_col + b, target * n_col + a))
        return lax.ppermute(value, BOTH, pairs)

    own = panel.reshape(tiles, tile, strip).transpose(0, 2, 1).astype(BF16)
    high, *lower = bits_of(n_col)
    parts = {0: own, high: permute_col(own, high)}
    if lower:
        parts[1] = permute_col(own, 1)
    tops = [transpose(own[:slots], m) for m in range(groups)]
    mat = dot(inverse, inverse, ((0,), (0,)), lax.Precision.HIGHEST)
    mat_hi = mat.astype(BF16)
    mat = jnp.stack([mat_hi, (mat - mat_hi.astype(F32)).astype(BF16)])

    cot = pl.pallas_call(
        functools.partial(unmix_kernel, slabs, tile),
        grid=(tiles,),
        in_specs=[pl.BlockSpec((mixed, LANES), lambda t: (t, 0))],
        out_specs=pl.BlockSpec((tile, width), lambda t: (t, 0)),
        out_shape=jax.ShapeDtypeStruct((rows, width), BF16),
        scratch_shapes=[pltpu.VMEM((mixed, LANES), F32)],
        compiler_params=params(STREAMED),
        cost_estimate=cost(0, 4 * rows * width),
    )(mixed_rows(cotangent))

    parts, mat, cot, tops = lax.optimization_barrier((parts, mat, cot, tops))
    top = jnp.stack(tops)
    for bit in lower:
        for q in range(0, n_col, 2 * bit):
            if q | bit not in parts:
                parts[q | bit] = permute_col(parts[q], bit)
    for bit in bits_of(n_col)[:-1]:
        top = jnp.concatenate([top, permute_row(top, bit)], 0)
    tops = [top, permute_row(top, 1)]

    q_sum, e_part, panel_all = pl.pallas_call(
        functools.partial(q_kernel, n_row, n_col, groups),
        grid=(slabs,),
        in_specs=[SMEM]
        + [whole((tiles, strip, tile))] * n_col
        + [whole((2, tile, tile)), pl.BlockSpec((rows, tile), lambda s: (0, s))],
        out_specs=[
            pl.BlockSpec((1, tile, tile), lambda s: (s, 0, 0)),
            whole((n_row, slots, strip, tile)),
            whole((tile, rows)),
        ],
        out_shape=[
            jax.ShapeDtypeStruct((slabs, tile, tile), BF16),
            jax.ShapeDtypeStruct((n_row, slots, strip, tile), BF16),
            jax.ShapeDtypeStruct((tile, rows), BF16),
        ],
        compiler_params=params(),
        cost_estimate=cost(2 * rows * width * tile, 2 * rows * (width + tile)),
    )(place, *[parts[q] for q in range(n_col)], mat, cot)

    w, gi = pl.pallas_call(
        functools.partial(w_kernel, n_row, n_col, groups),
        in_specs=[SMEM] + [VMEM] * 5,
        out_specs=[VMEM, VMEM],
        out_shape=[
            jax.ShapeDtypeStruct((tile, width), BF16),
            jax.ShapeDtypeStruct((n_col, strip, tile), BF16),
        ],
        scratch_shapes=[pltpu.VMEM((slabs, tile, tile), BF16)],
        compiler_params=params(),
        cost_estimate=cost(6 * tile * tile * width, 8 * tile * width),
    )(place, *tops, mat, inverse, q_sum)

    h = pl.pallas_call(
        functools.partial(h_kernel, n_col),
        grid=(tiles,),
        in_specs=[SMEM, whole((tile, width)), pl.BlockSpec((tile, width), lambda t: (t, 0))],
        out_specs=whole((n_col, tiles, strip, tile)),
        out_shape=jax.ShapeDtypeStruct((n_col, tiles, strip, tile), BF16),
        compiler_params=params(),
        cost_estimate=cost(2 * rows * width * tile, 2 * rows * (width + tile)),
    )(place, w, cot)

    def update(first, count, previous):
        return pl.pallas_call(
            functools.partial(update_kernel, slabs, tile),
            grid=(count,),
            in_specs=[
                pl.BlockSpec((tile, tile), lambda t: (0, t + first)),
                whole((tile, width)),
                pl.BlockSpec((mixed, LANES), lambda t: (t + first, 0)),
            ]
            + [pl.BlockSpec(memory_space=pl.ANY)] * len(previous),
            out_specs=pl.BlockSpec((mixed, LANES), lambda t: (t + first, 0)),
            out_shape=jax.ShapeDtypeStruct((tiles * mixed, LANES), BF16),
            scratch_shapes=[pltpu.VMEM((mixed, LANES), F32)],
            input_output_aliases={3: 0} if previous else {},
            compiler_params=params(STREAMED),
            cost_estimate=cost(2 * count * tile * width * tile, 4 * count * tile * width),
        )(panel_all, w, mixed_rows(slab), *previous)

    def halve(value, exchange, bit):
        half = value.shape[0] // 2
        return value[:half].astype(F32) + exchange(value[half:], bit).astype(F32)

    def sum_all(values):
        values = [v.astype(F32) for v in values]
        while len(values) > 1:
            values = [values[i] + values[i + 1] for i in range(0, len(values), 2)]
        return values[0]

    def row_sum(value, bits):
        steps = [sum(b for k, b in enumerate(bits) if (q >> k) & 1) for q in range(1 << len(bits))]
        return sum_all([value] + [permute_row(value, step) for step in steps[1:]])

    col_bits, row_bits = list(reversed(bits_of(n_col))), list(reversed(bits_of(n_row)))
    e_part = halve(e_part, permute_row, 1).astype(BF16)
    gi = sum_all([gi[0]] + [permute_col(gi[q], q) for q in range(1, n_col)]).astype(BF16)
    e_part, gi, h, w = lax.optimization_barrier((e_part, gi, h, w))

    others = [permute_col(h[q], q) for q in range(n_col - 1, 0, -1)]
    for bit in col_bits[1:]:
        e_part = halve(e_part, permute_row, bit).astype(BF16)
    gi = row_sum(gi, row_bits[:1]).astype(BF16)
    half = tiles // 2
    updated = update(0, half, [])
    others[-1], e_part, gi, updated, w = lax.optimization_barrier((others[-1], e_part, gi, updated, w))

    e_own = sum_all([transpose(e_part[m], m) for m in range(groups)])
    gi = row_sum(gi, row_bits[1:2])
    e_own, gi, updated, w = lax.optimization_barrier((e_own, gi, updated, w))

    updated = update(half, tiles - half, [updated])
    for bit in row_bits[2:]:
        gi = row_sum(gi.astype(BF16), [bit])
    others, updated, gi = lax.optimization_barrier((others, updated, gi))
    h = sum_all([h[0]] + others[::-1])
    grad_panel = jnp.concatenate([h[:slots] + e_own, h[slots:]], 0)
    updated = updated.reshape(tiles, tile, tile // LANES, slabs, LANES).transpose(0, 1, 3, 2, 4)
    return (
        updated.reshape(slab.shape),
        grad_panel.transpose(0, 2, 1).reshape(panel.shape),
        gi.T,
    )


def solution(mesh):
    in_specs = (
        P(None, "row", None, "col"),
        P(None, "row", None, None, "col", None),
        P(None, "row", None, None, "col", None),
        P(),
    )
    out_specs = (
        P(None, "row", None, None, "col", None),
        P(None, "row", None, "col"),
        P(None, "col"),
    )
    return jax.shard_map(
        per_device, mesh=mesh, in_specs=in_specs, out_specs=out_specs, check_vma=False
    )
```

```python
import functools

import jax
import jax.numpy as jnp
from jax import lax
from jax.experimental import pallas as pl
from jax.experimental.pallas import tpu as pltpu
from jax.sharding import PartitionSpec as P

BOTH = ("row", "col")
F32 = jnp.float32
BF16 = jnp.bfloat16
LANES = 128
VMEM = pl.BlockSpec(memory_space=pltpu.VMEM)
SMEM = pl.BlockSpec(memory_space=pltpu.SMEM)


def bits_of(count):
    return [1 << b for b in reversed(range(count.bit_length() - 1))]


def reversed_bits(value, count):
    width = count.bit_length() - 1
    place = 0
    for b in range(width):
        place = place + (((value >> b) & 1) << (width - 1 - b))
    return place


def dot(a, b, dims, precision=None):
    return lax.dot_general(a, b, (dims, ((), ())), precision=precision, preferred_element_type=F32)


def whole(shape):
    return pl.BlockSpec(shape, lambda *_: (0,) * len(shape))


def params():
    return pltpu.CompilerParams(vmem_limit_bytes=24 * 2**20)


def cost(flops, nbytes):
    return pl.CostEstimate(flops=flops, bytes_accessed=nbytes, transcendentals=0)


def unmix_kernel(slabs, tile, x_ref, o_ref, wide_ref):
    halves = tile // LANES
    wide_ref[...] = x_ref[...].astype(F32)
    for s in range(slabs):
        for h in range(halves):
            part = wide_ref[pl.ds(h * slabs + s, tile, stride=halves * slabs), :]
            o_ref[:, s * tile + h * LANES : s * tile + (h + 1) * LANES] = part.astype(BF16)


def q_kernel(n_row, n_col, groups, place_ref, *refs):
    parts, (m_ref, g_ref, q_ref, e_ref, pt_ref) = refs[:n_col], refs[n_col:]
    tiles, strip, tile = parts[0].shape
    s = pl.program_id(0)
    row, col = place_ref[0], place_ref[1]
    group, rho = row // n_col, (row % n_col) ^ (n_col // 2)

    @pl.when(s == 0)
    def _():
        for q in range(n_col):
            at = pl.multiple_of((col ^ q) * strip, strip)
            for t in range(tiles):
                pt_ref[pl.ds(at, strip), t * tile : (t + 1) * tile] = parts[q][t]

    q_val = dot(pt_ref[...], g_ref[...], ((1,), (0,))).astype(BF16)
    q_ref[0] = q_val
    e_val = -(dot(m_ref[0], q_val, ((1,), (0,))) + dot(m_ref[1], q_val, ((1,), (0,))))
    e_val = e_val.astype(BF16)
    slot, other = s // groups, group ^ (s % groups)
    for r in range(n_col):
        place = reversed_bits(rho ^ r, n_col) * groups + other
        e_ref[place, slot] = e_val[r * strip : (r + 1) * strip]


def w_kernel(n_row, n_col, groups, place_ref, *refs):
    tops, (m_ref, inv_ref, q_ref, w_ref, gi_ref, top_all) = refs[:2], refs[2:]
    slots, strip, tile = tops[0].shape[1:]
    half = tops[0].shape[0]
    slabs = slots * groups
    row, col = place_ref[0], place_ref[1]
    group, rho = row // n_col, (row % n_col) ^ (n_col // 2)
    for p in range(n_row):
        at = pl.multiple_of((rho ^ (p % n_col)) * strip, strip)
        place = reversed_bits(p % n_col, n_col) * groups + p // n_col
        for slot in range(slots):
            s = slot * groups + (group ^ (p // n_col))
            top_all[s, pl.ds(at, strip), :] = tops[place // half][place % half, slot]
    z = jnp.zeros((tile, tile), F32)
    for s in range(slabs):
        top = top_all[s]
        w = dot(m_ref[0], top, ((1,), (0,))) + dot(m_ref[1], top, ((1,), (0,)))
        w_ref[:, s * tile : (s + 1) * tile] = w.astype(BF16)
        z = z + dot(top, q_ref[s], ((1,), (1,)))
    z = z + z.T
    gi = -dot(z, inv_ref[...], ((1,), (1,)), lax.Precision.HIGHEST)
    for r in range(n_col):
        gi_ref[col ^ r] = gi[r * strip : (r + 1) * strip].astype(BF16)


def h_kernel(n_col, place_ref, w_ref, g_ref, h_ref):
    strip = h_ref.shape[2]
    t = pl.program_id(0)
    col = place_ref[1]
    h = -dot(w_ref[...], g_ref[...], ((1,), (1,)))
    for r in range(n_col):
        h_ref[col ^ r, t] = h[r * strip : (r + 1) * strip].astype(BF16)


def update_kernel(slabs, tile, pt_ref, w_ref, x_ref, *refs):
    o_ref, wide_ref = refs[-2:]
    halves = tile // LANES
    product = dot(pt_ref[...], w_ref[...], ((0,), (0,)))
    for s in range(slabs):
        for h in range(halves):
            part = product[:, s * tile + h * LANES : s * tile + (h + 1) * LANES]
            wide_ref[pl.ds(h * slabs + s, tile, stride=halves * slabs), :] = part
    o_ref[...] = (x_ref[...].astype(F32) - wide_ref[...]).astype(BF16)


def mixed_rows(x):
    tiles, _, tile, slabs, _, _ = x.shape
    x = x.reshape(tiles, tile, slabs, tile // LANES, LANES).transpose(0, 1, 3, 2, 4)
    return x.reshape(-1, LANES)


def per_device(panel, slab, cotangent, inverse):
    tiles, _, tile, strip = panel.shape
    slabs = slab.shape[3]
    n_row = lax.axis_size("row")
    n_col = lax.axis_size("col")
    groups = n_row // n_col
    slots = slabs // groups
    width = slabs * tile
    rows = tiles * tile
    mixed = tile * width // LANES
    place = jnp.stack([lax.axis_index("row"), lax.axis_index("col")]).astype(jnp.int32)

    def permute_row(value, bit):
        return lax.ppermute(value, "row", [(i, i ^ bit) for i in range(n_row)])

    def permute_col(value, bit):
        return lax.ppermute(value, "col", [(i, i ^ bit) for i in range(n_col)])

    far = n_col // 2

    def transpose(value, across, back=False):
        pairs = []
        for m in range(groups):
            for a in range(n_col):
                for b in range(n_col):
                    here = (m * n_col + a) * n_col + b
                    there = ((m ^ across) * n_col + (b ^ far)) * n_col + a
                    pairs.append((there, here) if back else (here, there))
        return lax.ppermute(value, BOTH, pairs)

    own = panel.reshape(tiles, tile, strip).transpose(0, 2, 1).astype(BF16)
    high, *lower = bits_of(n_col)
    parts = {0: own, high: permute_col(own, high)}
    tops = [transpose(own[:slots], m) for m in range(groups)]
    mat = dot(inverse, inverse, ((0,), (0,)), lax.Precision.HIGHEST)
    mat_hi = mat.astype(BF16)
    mat = jnp.stack([mat_hi, (mat - mat_hi.astype(F32)).astype(BF16)])
    tops, mat, own = lax.optimization_barrier((tops, mat, own))

    top = jnp.stack(tops)
    for bit in bits_of(n_col)[:-1]:
        top = jnp.concatenate([top, permute_row(top, bit)], 0)
    if lower:
        parts[1] = permute_col(own, 1)
    cot = pl.pallas_call(
        functools.partial(unmix_kernel, slabs, tile),
        grid=(tiles,),
        in_specs=[pl.BlockSpec((mixed, LANES), lambda t: (t, 0))],
        out_specs=pl.BlockSpec((tile, width), lambda t: (t, 0)),
        out_shape=jax.ShapeDtypeStruct((rows, width), BF16),
        scratch_shapes=[pltpu.VMEM((mixed, LANES), F32)],
        compiler_params=params(),
        cost_estimate=cost(0, 4 * rows * width),
    )(mixed_rows(cotangent))

    top, parts, cot = lax.optimization_barrier((top, parts, cot))

    for bit in lower:
        for q in range(0, n_col, 2 * bit):
            if q | bit not in parts:
                parts[q | bit] = permute_col(parts[q], bit)
    tops = [top, permute_row(top, 1)]

    q_sum, e_part, panel_all = pl.pallas_call(
        functools.partial(q_kernel, n_row, n_col, groups),
        grid=(slabs,),
        in_specs=[SMEM]
        + [whole((tiles, strip, tile))] * n_col
        + [whole((2, tile, tile)), pl.BlockSpec((rows, tile), lambda s: (0, s))],
        out_specs=[
            pl.BlockSpec((1, tile, tile), lambda s: (s, 0, 0)),
            whole((n_row, slots, strip, tile)),
            whole((tile, rows)),
        ],
        out_shape=[
            jax.ShapeDtypeStruct((slabs, tile, tile), BF16),
            jax.ShapeDtypeStruct((n_row, slots, strip, tile), BF16),
            jax.ShapeDtypeStruct((tile, rows), BF16),
        ],
        compiler_params=params(),
        cost_estimate=cost(2 * rows * width * tile, 2 * rows * (width + tile)),
    )(place, *[parts[q] for q in range(n_col)], mat, cot)

    w, gi = pl.pallas_call(
        functools.partial(w_kernel, n_row, n_col, groups),
        in_specs=[SMEM] + [VMEM] * 5,
        out_specs=[VMEM, VMEM],
        out_shape=[
            jax.ShapeDtypeStruct((tile, width), BF16),
            jax.ShapeDtypeStruct((n_col, strip, tile), BF16),
        ],
        scratch_shapes=[pltpu.VMEM((slabs, tile, tile), BF16)],
        compiler_params=params(),
        cost_estimate=cost(6 * tile * tile * width, 8 * tile * width),
    )(place, *tops, mat, inverse, q_sum)

    h = pl.pallas_call(
        functools.partial(h_kernel, n_col),
        grid=(tiles,),
        in_specs=[SMEM, whole((tile, width)), pl.BlockSpec((tile, width), lambda t: (t, 0))],
        out_specs=whole((n_col, tiles, strip, tile)),
        out_shape=jax.ShapeDtypeStruct((n_col, tiles, strip, tile), BF16),
        compiler_params=params(),
        cost_estimate=cost(2 * rows * width * tile, 2 * rows * (width + tile)),
    )(place, w, cot)

    def update(first, count, previous):
        return pl.pallas_call(
            functools.partial(update_kernel, slabs, tile),
            grid=(count,),
            in_specs=[
                pl.BlockSpec((tile, tile), lambda t: (0, t + first)),
                whole((tile, width)),
                pl.BlockSpec((mixed, LANES), lambda t: (t + first, 0)),
            ]
            + [pl.BlockSpec(memory_space=pl.ANY)] * len(previous),
            out_specs=pl.BlockSpec((mixed, LANES), lambda t: (t + first, 0)),
            out_shape=jax.ShapeDtypeStruct((tiles * mixed, LANES), BF16),
            scratch_shapes=[pltpu.VMEM((mixed, LANES), F32)],
            input_output_aliases={3: 0} if previous else {},
            compiler_params=params(),
            cost_estimate=cost(2 * count * tile * width * tile, 4 * count * tile * width),
        )(panel_all, w, mixed_rows(slab), *previous)

    def halve(value, exchange, bit):
        half = value.shape[0] // 2
        return value[:half].astype(F32) + exchange(value[half:], bit).astype(F32)

    def sum_all(values):
        values = [v.astype(F32) for v in values]
        while len(values) > 1:
            values = [values[i] + values[i + 1] for i in range(0, len(values), 2)]
        return values[0]

    def row_sum(value, bits):
        steps = [sum(b for k, b in enumerate(bits) if (q >> k) & 1) for q in range(1 << len(bits))]
        return sum_all([value] + [permute_row(value, step) for step in steps[1:]])

    col_bits, row_bits = list(reversed(bits_of(n_col))), list(reversed(bits_of(n_row)))
    e_part = halve(e_part, permute_row, 1).astype(BF16)
    gi = sum_all([gi[0]] + [permute_col(gi[q], q) for q in range(1, n_col)]).astype(BF16)
    e_part, gi, h, w = lax.optimization_barrier((e_part, gi, h, w))

    others = [permute_col(h[q], q) for q in range(n_col - 1, 0, -1)]
    for bit in col_bits[1:]:
        e_part = halve(e_part, permute_row, bit).astype(BF16)
    gi = row_sum(gi, row_bits[:1]).astype(BF16)
    others[-1], e_part, gi, w = lax.optimization_barrier((others[-1], e_part, gi, w))

    e_own = sum_all([transpose(e_part[m], m, back=True) for m in range(groups)])
    gi = row_sum(gi, row_bits[1:2])
    most = tiles * 5 // 8
    updated = update(0, most, [])
    e_own, gi, updated, w = lax.optimization_barrier((e_own, gi, updated, w))

    updated = update(most, tiles - most, [updated])
    for bit in row_bits[2:]:
        gi = row_sum(gi.astype(BF16), [bit])
    others, updated, gi = lax.optimization_barrier((others, updated, gi))
    h = sum_all([h[0]] + others[::-1])
    grad_panel = jnp.concatenate([h[:slots] + e_own, h[slots:]], 0)
    updated = updated.reshape(tiles, tile, tile // LANES, slabs, LANES).transpose(0, 1, 3, 2, 4)
    return (
        updated.reshape(slab.shape),
        grad_panel.transpose(0, 2, 1).reshape(panel.shape),
        gi.T,
    )


def solution(mesh):
    in_specs = (
        P(None, "row", None, "col"),
        P(None, "row", None, None, "col", None),
        P(None, "row", None, None, "col", None),
        P(),
    )
    out_specs = (
        P(None, "row", None, None, "col", None),
        P(None, "row", None, "col"),
        P(None, "col"),
    )
    return jax.shard_map(
        per_device, mesh=mesh, in_specs=in_specs, out_specs=out_specs, check_vma=False
    )
```

```python
import functools

import jax
import jax.numpy as jnp
from jax import lax
from jax.experimental import pallas as pl
from jax.experimental.pallas import tpu as pltpu
from jax.sharding import PartitionSpec as P

BOTH = ("row", "col")
F32 = jnp.float32
BF16 = jnp.bfloat16
LANES = 128
VMEM = pl.BlockSpec(memory_space=pltpu.VMEM)
SMEM = pl.BlockSpec(memory_space=pltpu.SMEM)


def bits_of(count):
    return [1 << b for b in reversed(range(count.bit_length() - 1))]


def reversed_bits(value, count):
    width = count.bit_length() - 1
    place = 0
    for b in range(width):
        place = place + (((value >> b) & 1) << (width - 1 - b))
    return place


def dot(a, b, dims, precision=None):
    return lax.dot_general(a, b, (dims, ((), ())), precision=precision, preferred_element_type=F32)


def whole(shape):
    return pl.BlockSpec(shape, lambda *_: (0,) * len(shape))


def params():
    return pltpu.CompilerParams(vmem_limit_bytes=24 * 2**20)


def cost(flops, nbytes):
    return pl.CostEstimate(flops=flops, bytes_accessed=nbytes, transcendentals=0)


def unmix_kernel(slabs, tile, inv_ref, x_ref, o_ref, m_ref, wide_ref):
    @pl.when(pl.program_id(0) == 0)
    def _():
        mat = dot(inv_ref[...], inv_ref[...], ((0,), (0,)), lax.Precision.HIGHEST)
        high = mat.astype(BF16)
        m_ref[0] = high
        m_ref[1] = (mat - high.astype(F32)).astype(BF16)

    halves = tile // LANES
    wide_ref[...] = x_ref[...].astype(F32)
    for s in range(slabs):
        for h in range(halves):
            part = wide_ref[pl.ds(h * slabs + s, tile, stride=halves * slabs), :]
            o_ref[:, s * tile + h * LANES : s * tile + (h + 1) * LANES] = part.astype(BF16)


def q_kernel(n_row, n_col, groups, place_ref, *refs):
    parts, (m_ref, g_ref, q_ref, e_ref, pt_ref) = refs[:n_col], refs[n_col:]
    tiles, strip, tile = parts[0].shape
    s = pl.program_id(0)
    row, col = place_ref[0], place_ref[1]
    group, rho = row // n_col, (row % n_col) ^ (n_col // 2)

    @pl.when(s == 0)
    def _():
        for q in range(n_col):
            at = pl.multiple_of((col ^ q) * strip, strip)
            for t in range(tiles):
                pt_ref[pl.ds(at, strip), t * tile : (t + 1) * tile] = parts[q][t]

    q_val = dot(pt_ref[...], g_ref[...], ((1,), (0,))).astype(BF16)
    q_ref[0] = q_val
    e_val = -(dot(m_ref[0], q_val, ((1,), (0,))) + dot(m_ref[1], q_val, ((1,), (0,))))
    e_val = e_val.astype(BF16)
    slot, other = s // groups, group ^ (s % groups)
    for r in range(n_col):
        place = reversed_bits(rho ^ r, n_col) * groups + other
        e_ref[place, slot] = e_val[r * strip : (r + 1) * strip]


def w_kernel(n_row, n_col, groups, place_ref, *refs):
    tops, (m_ref, inv_ref, q_ref, w_ref, gi_ref, top_all) = refs[:2], refs[2:]
    slots, strip, tile = tops[0].shape[1:]
    half = tops[0].shape[0]
    slabs = slots * groups
    row, col = place_ref[0], place_ref[1]
    group, rho = row // n_col, (row % n_col) ^ (n_col // 2)
    for p in range(n_row):
        at = pl.multiple_of((rho ^ (p % n_col)) * strip, strip)
        place = reversed_bits(p % n_col, n_col) * groups + p // n_col
        for slot in range(slots):
            s = slot * groups + (group ^ (p // n_col))
            top_all[s, pl.ds(at, strip), :] = tops[place // half][place % half, slot]
    z = jnp.zeros((tile, tile), F32)
    for s in range(slabs):
        top = top_all[s]
        w = dot(m_ref[0], top, ((1,), (0,))) + dot(m_ref[1], top, ((1,), (0,)))
        w_ref[:, s * tile : (s + 1) * tile] = w.astype(BF16)
        z = z + dot(top, q_ref[s], ((1,), (1,)))
    z = z + z.T
    gi = -dot(z, inv_ref[...], ((1,), (1,)), lax.Precision.HIGHEST)
    for r in range(n_col):
        gi_ref[col ^ r] = gi[r * strip : (r + 1) * strip].astype(BF16)


def h_kernel(n_col, place_ref, w_ref, g_ref, h_ref):
    strip = h_ref.shape[2]
    t = pl.program_id(0)
    col = place_ref[1]
    h = -dot(w_ref[...], g_ref[...], ((1,), (1,)))
    for r in range(n_col):
        h_ref[reversed_bits(col ^ r, n_col), t] = h[r * strip : (r + 1) * strip].astype(BF16)


def update_kernel(slabs, tile, pt_ref, w_ref, x_ref, *refs):
    o_ref, wide_ref = refs[-2:]
    halves = tile // LANES
    product = dot(pt_ref[...], w_ref[...], ((0,), (0,)))
    for s in range(slabs):
        for h in range(halves):
            part = product[:, s * tile + h * LANES : s * tile + (h + 1) * LANES]
            wide_ref[pl.ds(h * slabs + s, tile, stride=halves * slabs), :] = part
    o_ref[...] = (x_ref[...].astype(F32) - wide_ref[...]).astype(BF16)


def mixed_rows(x):
    tiles, _, tile, slabs, _, _ = x.shape
    x = x.reshape(tiles, tile, slabs, tile // LANES, LANES).transpose(0, 1, 3, 2, 4)
    return x.reshape(-1, LANES)


def per_device(panel, slab, cotangent, inverse):
    tiles, _, tile, strip = panel.shape
    slabs = slab.shape[3]
    n_row = lax.axis_size("row")
    n_col = lax.axis_size("col")
    groups = n_row // n_col
    slots = slabs // groups
    width = slabs * tile
    rows = tiles * tile
    mixed = tile * width // LANES
    place = jnp.stack([lax.axis_index("row"), lax.axis_index("col")]).astype(jnp.int32)

    def permute_row(value, bit):
        return lax.ppermute(value, "row", [(i, i ^ bit) for i in range(n_row)])

    def permute_col(value, bit):
        return lax.ppermute(value, "col", [(i, i ^ bit) for i in range(n_col)])

    far = n_col // 2

    def transpose(value, across, back=False):
        pairs = []
        for m in range(groups):
            for a in range(n_col):
                for b in range(n_col):
                    here = (m * n_col + a) * n_col + b
                    there = ((m ^ across) * n_col + (b ^ far)) * n_col + a
                    pairs.append((there, here) if back else (here, there))
        return lax.ppermute(value, BOTH, pairs)

    own = panel.reshape(tiles, tile, strip).transpose(0, 2, 1).astype(BF16)
    high, *lower = bits_of(n_col)
    parts = {0: own, high: permute_col(own, high)}
    tops = [transpose(own[:slots], m) for m in range(groups)]
    tops, own = lax.optimization_barrier((tops, own))

    top = jnp.stack(tops)
    for bit in bits_of(n_col)[:-1]:
        top = jnp.concatenate([top, permute_row(top, bit)], 0)
    if lower:
        parts[1] = permute_col(own, 1)
    cot, mat = pl.pallas_call(
        functools.partial(unmix_kernel, slabs, tile),
        grid=(tiles,),
        in_specs=[whole((tile, tile)), pl.BlockSpec((mixed, LANES), lambda t: (t, 0))],
        out_specs=[pl.BlockSpec((tile, width), lambda t: (t, 0)), whole((2, tile, tile))],
        out_shape=[
            jax.ShapeDtypeStruct((rows, width), BF16),
            jax.ShapeDtypeStruct((2, tile, tile), BF16),
        ],
        scratch_shapes=[pltpu.VMEM((mixed, LANES), F32)],
        compiler_params=params(),
        cost_estimate=cost(0, 4 * rows * width),
    )(inverse, mixed_rows(cotangent))

    top, parts, mat = lax.optimization_barrier((top, parts, mat))

    for bit in lower:
        for q in range(0, n_col, 2 * bit):
            if q | bit not in parts:
                parts[q | bit] = permute_col(parts[q], bit)
    tops = [top, permute_row(top, 1)]

    q_sum, e_part, panel_all = pl.pallas_call(
        functools.partial(q_kernel, n_row, n_col, groups),
        grid=(slabs,),
        in_specs=[SMEM]
        + [whole((tiles, strip, tile))] * n_col
        + [whole((2, tile, tile)), pl.BlockSpec((rows, tile), lambda s: (0, s))],
        out_specs=[
            pl.BlockSpec((1, tile, tile), lambda s: (s, 0, 0)),
            whole((n_row, slots, strip, tile)),
            whole((tile, rows)),
        ],
        out_shape=[
            jax.ShapeDtypeStruct((slabs, tile, tile), BF16),
            jax.ShapeDtypeStruct((n_row, slots, strip, tile), BF16),
            jax.ShapeDtypeStruct((tile, rows), BF16),
        ],
        compiler_params=params(),
        cost_estimate=cost(2 * rows * width * tile, 2 * rows * (width + tile)),
    )(place, *[parts[q] for q in range(n_col)], mat, cot)

    w, gi = pl.pallas_call(
        functools.partial(w_kernel, n_row, n_col, groups),
        in_specs=[SMEM] + [VMEM] * 5,
        out_specs=[VMEM, VMEM],
        out_shape=[
            jax.ShapeDtypeStruct((tile, width), BF16),
            jax.ShapeDtypeStruct((n_col, strip, tile), BF16),
        ],
        scratch_shapes=[pltpu.VMEM((slabs, tile, tile), BF16)],
        compiler_params=params(),
        cost_estimate=cost(tile, tile),
    )(place, *tops, mat, inverse, q_sum)

    h = pl.pallas_call(
        functools.partial(h_kernel, n_col),
        grid=(tiles,),
        in_specs=[SMEM, whole((tile, width)), pl.BlockSpec((tile, width), lambda t: (t, 0))],
        out_specs=whole((n_col, tiles, strip, tile)),
        out_shape=jax.ShapeDtypeStruct((n_col, tiles, strip, tile), BF16),
        compiler_params=params(),
        cost_estimate=cost(tile, tile),
    )(place, w, cot)

    def update(first, count, previous):
        return pl.pallas_call(
            functools.partial(update_kernel, slabs, tile),
            grid=(count,),
            in_specs=[
                pl.BlockSpec((tile, tile), lambda t: (0, t + first)),
                whole((tile, width)),
                pl.BlockSpec((mixed, LANES), lambda t: (t + first, 0)),
            ]
            + [pl.BlockSpec(memory_space=pl.ANY)] * len(previous),
            out_specs=pl.BlockSpec((mixed, LANES), lambda t: (t + first, 0)),
            out_shape=jax.ShapeDtypeStruct((tiles * mixed, LANES), BF16),
            scratch_shapes=[pltpu.VMEM((mixed, LANES), F32)],
            input_output_aliases={3: 0} if previous else {},
            compiler_params=params(),
            cost_estimate=cost(2 * count * tile * width * tile, 4 * count * tile * width),
        )(panel_all, w, mixed_rows(slab), *previous)

    def halve(value, exchange, bit):
        half = value.shape[0] // 2
        return value[:half].astype(F32) + exchange(value[half:], bit).astype(F32)

    def sum_all(values):
        values = [v.astype(F32) for v in values]
        while len(values) > 1:
            values = [values[i] + values[i + 1] for i in range(0, len(values), 2)]
        return values[0]

    def row_sum(value, bits):
        steps = [sum(b for k, b in enumerate(bits) if (q >> k) & 1) for q in range(1 << len(bits))]
        return sum_all([value] + [permute_row(value, step) for step in steps[1:]])

    col_bits, row_bits = list(reversed(bits_of(n_col))), list(reversed(bits_of(n_row)))
    e_part = halve(e_part, permute_row, 1).astype(BF16)
    gi = sum_all([gi[0]] + [permute_col(gi[q], q) for q in range(1, n_col)]).astype(BF16)
    e_part, gi, h, w = lax.optimization_barrier((e_part, gi, h, w))

    h = halve(h, permute_col, 1).astype(BF16)
    for bit in col_bits[1:]:
        e_part = halve(e_part, permute_row, bit).astype(BF16)
    gi = row_sum(gi, row_bits[:1]).astype(BF16)
    h, e_part, gi, w = lax.optimization_barrier((h, e_part, gi, w))

    for bit in col_bits[1:]:
        h = halve(h.astype(BF16), permute_col, bit)

    e_own = sum_all([transpose(e_part[m], m, back=True) for m in range(groups)])
    gi = row_sum(gi, row_bits[1:2])
    most = tiles * 5 // 8
    updated = update(0, most, [])
    e_own, gi, updated, w = lax.optimization_barrier((e_own, gi, updated, w))

    updated = update(most, tiles - most, [updated])
    for bit in row_bits[2:]:
        gi = row_sum(gi.astype(BF16), [bit])
    h, updated, gi = lax.optimization_barrier((h[0], updated, gi))
    grad_panel = jnp.concatenate([h[:slots] + e_own, h[slots:]], 0)
    updated = updated.reshape(tiles, tile, tile // LANES, slabs, LANES).transpose(0, 1, 3, 2, 4)
    return (
        updated.reshape(slab.shape),
        grad_panel.transpose(0, 2, 1).reshape(panel.shape),
        gi.T,
    )


def solution(mesh):
    in_specs = (
        P(None, "row", None, "col"),
        P(None, "row", None, None, "col", None),
        P(None, "row", None, None, "col", None),
        P(),
    )
    out_specs = (
        P(None, "row", None, None, "col", None),
        P(None, "row", None, "col"),
        P(None, "col"),
    )
    return jax.shard_map(
        per_device, mesh=mesh, in_specs=in_specs, out_specs=out_specs, check_vma=False
    )
```

```python
import functools

import jax
import jax.numpy as jnp
from jax import lax
from jax.experimental import pallas as pl
from jax.experimental.pallas import tpu as pltpu
from jax.sharding import PartitionSpec as P

BOTH = ("row", "col")
F32 = jnp.float32
BF16 = jnp.bfloat16
LANES = 128
VMEM = pl.BlockSpec(memory_space=pltpu.VMEM)
SMEM = pl.BlockSpec(memory_space=pltpu.SMEM)


def bits_of(count):
    return [1 << b for b in reversed(range(count.bit_length() - 1))]


def reversed_bits(value, count):
    width = count.bit_length() - 1
    place = 0
    for b in range(width):
        place = place + (((value >> b) & 1) << (width - 1 - b))
    return place


def dot(a, b, dims, precision=None):
    return lax.dot_general(a, b, (dims, ((), ())), precision=precision, preferred_element_type=F32)


def whole(shape):
    return pl.BlockSpec(shape, lambda *_: (0,) * len(shape))


def params():
    return pltpu.CompilerParams(vmem_limit_bytes=12 * 2**20)


def cost(flops, nbytes):
    return pl.CostEstimate(flops=flops, bytes_accessed=nbytes, transcendentals=0)


def unmix_kernel(slabs, tile, inv_ref, x_ref, o_ref, m_ref, wide_ref):
    @pl.when(pl.program_id(0) == 0)
    def _():
        mat = dot(inv_ref[...], inv_ref[...], ((0,), (0,)), lax.Precision.HIGHEST)
        high = mat.astype(BF16)
        m_ref[0] = high
        m_ref[1] = (mat - high.astype(F32)).astype(BF16)

    halves = tile // LANES
    wide_ref[...] = x_ref[...].astype(F32)
    for s in range(slabs):
        for h in range(halves):
            part = wide_ref[pl.ds(h * slabs + s, tile, stride=halves * slabs), :]
            o_ref[:, s * tile + h * LANES : s * tile + (h + 1) * LANES] = part.astype(BF16)


def q_kernel(n_row, n_col, groups, place_ref, *refs):
    parts, (m_ref, g_ref, q_ref, e_ref, pt_ref) = refs[:n_col], refs[n_col:]
    tiles, strip, tile = parts[0].shape
    s = pl.program_id(0)
    row, col = place_ref[0], place_ref[1]
    group, rho = row // n_col, (row % n_col) ^ (n_col // 2)

    @pl.when(s == 0)
    def _():
        for q in range(n_col):
            at = pl.multiple_of((col ^ q) * strip, strip)
            for t in range(tiles):
                pt_ref[pl.ds(at, strip), t * tile : (t + 1) * tile] = parts[q][t]

    q_val = dot(pt_ref[...], g_ref[...], ((1,), (0,))).astype(BF16)
    q_ref[0] = q_val
    e_val = -(dot(m_ref[0], q_val, ((1,), (0,))) + dot(m_ref[1], q_val, ((1,), (0,))))
    e_val = e_val.astype(BF16)
    slot, other = s // groups, group ^ (s % groups)
    for r in range(n_col):
        place = reversed_bits(rho ^ r, n_col) * groups + other
        e_ref[place, slot] = e_val[r * strip : (r + 1) * strip]


def w_kernel(n_row, n_col, groups, place_ref, *refs):
    tops, (m_ref, inv_ref, q_ref, w_ref, gi_ref, top_all) = refs[:2], refs[2:]
    slots, strip, tile = tops[0].shape[1:]
    half = tops[0].shape[0]
    slabs = slots * groups
    row, col = place_ref[0], place_ref[1]
    group, rho = row // n_col, (row % n_col) ^ (n_col // 2)
    for p in range(n_row):
        at = pl.multiple_of((rho ^ (p % n_col)) * strip, strip)
        place = reversed_bits(p % n_col, n_col) * groups + p // n_col
        for slot in range(slots):
            s = slot * groups + (group ^ (p // n_col))
            top_all[s, pl.ds(at, strip), :] = tops[place // half][place % half, slot]
    z = jnp.zeros((tile, tile), F32)
    for s in range(slabs):
        top = top_all[s]
        w = dot(m_ref[0], top, ((1,), (0,))) + dot(m_ref[1], top, ((1,), (0,)))
        w_ref[:, s * tile : (s + 1) * tile] = w.astype(BF16)
        z = z + dot(top, q_ref[s], ((1,), (1,)))
    z = z + z.T
    gi = -dot(z, inv_ref[...], ((1,), (1,)), lax.Precision.HIGHEST)
    for r in range(n_col):
        gi_ref[col ^ r] = gi[r * strip : (r + 1) * strip].astype(BF16)


def h_kernel(n_col, place_ref, w_ref, g_ref, h_ref):
    strip = h_ref.shape[2]
    t = pl.program_id(0)
    col = place_ref[1]
    h = -dot(w_ref[...], g_ref[...], ((1,), (1,)))
    for r in range(n_col):
        h_ref[reversed_bits(col ^ r, n_col), t] = h[r * strip : (r + 1) * strip].astype(BF16)


def update_kernel(slabs, tile, pt_ref, w_ref, x_ref, *refs):
    o_ref, wide_ref = refs[-2:]
    halves = tile // LANES
    product = dot(pt_ref[...], w_ref[...], ((0,), (0,)))
    for s in range(slabs):
        for h in range(halves):
            part = product[:, s * tile + h * LANES : s * tile + (h + 1) * LANES]
            wide_ref[pl.ds(h * slabs + s, tile, stride=halves * slabs), :] = part
    o_ref[...] = (x_ref[...].astype(F32) - wide_ref[...]).astype(BF16)


def mixed_rows(x):
    tiles, _, tile, slabs, _, _ = x.shape
    x = x.reshape(tiles, tile, slabs, tile // LANES, LANES).transpose(0, 1, 3, 2, 4)
    return x.reshape(-1, LANES)


def per_device(panel, slab, cotangent, inverse):
    tiles, _, tile, strip = panel.shape
    slabs = slab.shape[3]
    n_row = lax.axis_size("row")
    n_col = lax.axis_size("col")
    groups = n_row // n_col
    slots = slabs // groups
    width = slabs * tile
    rows = tiles * tile
    mixed = tile * width // LANES
    place = jnp.stack([lax.axis_index("row"), lax.axis_index("col")]).astype(jnp.int32)

    def permute_row(value, bit):
        return lax.ppermute(value, "row", [(i, i ^ bit) for i in range(n_row)])

    def permute_col(value, bit):
        return lax.ppermute(value, "col", [(i, i ^ bit) for i in range(n_col)])

    far = n_col // 2

    def transpose(value, across, back=False):
        pairs = []
        for m in range(groups):
            for a in range(n_col):
                for b in range(n_col):
                    here = (m * n_col + a) * n_col + b
                    there = ((m ^ across) * n_col + (b ^ far)) * n_col + a
                    pairs.append((there, here) if back else (here, there))
        return lax.ppermute(value, BOTH, pairs)

    own = panel.reshape(tiles, tile, strip).transpose(0, 2, 1).astype(BF16)
    high, *lower = bits_of(n_col)
    parts = {0: own, high: permute_col(own, high)}
    tops = [transpose(own[:slots], m) for m in range(groups)]
    cot, mat = pl.pallas_call(
        functools.partial(unmix_kernel, slabs, tile),
        grid=(tiles,),
        in_specs=[whole((tile, tile)), pl.BlockSpec((mixed, LANES), lambda t: (t, 0))],
        out_specs=[pl.BlockSpec((tile, width), lambda t: (t, 0)), whole((2, tile, tile))],
        out_shape=[
            jax.ShapeDtypeStruct((rows, width), BF16),
            jax.ShapeDtypeStruct((2, tile, tile), BF16),
        ],
        scratch_shapes=[pltpu.VMEM((mixed, LANES), F32)],
        compiler_params=params(),
        cost_estimate=cost(0, 4 * rows * width),
    )(inverse, mixed_rows(cotangent))

    tops, own, mat = lax.optimization_barrier((tops, own, mat))

    top = jnp.stack(tops)
    for bit in bits_of(n_col)[:-1]:
        top = jnp.concatenate([top, permute_row(top, bit)], 0)
    if lower:
        parts[1] = permute_col(own, 1)
    top, parts = lax.optimization_barrier((top, parts))

    for bit in lower:
        for q in range(0, n_col, 2 * bit):
            if q | bit not in parts:
                parts[q | bit] = permute_col(parts[q], bit)
    tops = [top, permute_row(top, 1)]

    q_sum, e_part, panel_all = pl.pallas_call(
        functools.partial(q_kernel, n_row, n_col, groups),
        grid=(slabs,),
        in_specs=[SMEM]
        + [whole((tiles, strip, tile))] * n_col
        + [whole((2, tile, tile)), pl.BlockSpec((rows, tile), lambda s: (0, s))],
        out_specs=[
            pl.BlockSpec((1, tile, tile), lambda s: (s, 0, 0)),
            whole((n_row, slots, strip, tile)),
            whole((tile, rows)),
        ],
        out_shape=[
            jax.ShapeDtypeStruct((slabs, tile, tile), BF16),
            jax.ShapeDtypeStruct((n_row, slots, strip, tile), BF16),
            jax.ShapeDtypeStruct((tile, rows), BF16),
        ],
        compiler_params=params(),
        cost_estimate=cost(2 * rows * width * tile, 2 * rows * (width + tile)),
    )(place, *[parts[q] for q in range(n_col)], mat, cot)

    w, gi = pl.pallas_call(
        functools.partial(w_kernel, n_row, n_col, groups),
        in_specs=[SMEM] + [VMEM] * 5,
        out_specs=[VMEM, VMEM],
        out_shape=[
            jax.ShapeDtypeStruct((tile, width), BF16),
            jax.ShapeDtypeStruct((n_col, strip, tile), BF16),
        ],
        scratch_shapes=[pltpu.VMEM((slabs, tile, tile), BF16)],
        compiler_params=params(),
        cost_estimate=cost(tile, tile),
    )(place, *tops, mat, inverse, q_sum)

    h = pl.pallas_call(
        functools.partial(h_kernel, n_col),
        grid=(tiles,),
        in_specs=[SMEM, whole((tile, width)), pl.BlockSpec((tile, width), lambda t: (t, 0))],
        out_specs=whole((n_col, tiles, strip, tile)),
        out_shape=jax.ShapeDtypeStruct((n_col, tiles, strip, tile), BF16),
        compiler_params=params(),
        cost_estimate=cost(tile, tile),
    )(place, w, cot)

    def update(first, count, previous):
        return pl.pallas_call(
            functools.partial(update_kernel, slabs, tile),
            grid=(count,),
            in_specs=[
                pl.BlockSpec((tile, tile), lambda t: (0, t + first)),
                whole((tile, width)),
                pl.BlockSpec((mixed, LANES), lambda t: (t + first, 0)),
            ]
            + [pl.BlockSpec(memory_space=pl.ANY)] * len(previous),
            out_specs=pl.BlockSpec((mixed, LANES), lambda t: (t + first, 0)),
            out_shape=jax.ShapeDtypeStruct((tiles * mixed, LANES), BF16),
            scratch_shapes=[pltpu.VMEM((mixed, LANES), F32)],
            input_output_aliases={3: 0} if previous else {},
            compiler_params=params(),
            cost_estimate=cost(2 * count * tile * width * tile, 4 * count * tile * width),
        )(panel_all, w, mixed_rows(slab), *previous)

    def halve(value, exchange, bit):
        half = value.shape[0] // 2
        return value[:half].astype(F32) + exchange(value[half:], bit).astype(F32)

    def sum_all(values):
        values = [v.astype(F32) for v in values]
        while len(values) > 1:
            values = [values[i] + values[i + 1] for i in range(0, len(values), 2)]
        return values[0]

    def row_sum(value, bits):
        steps = [sum(b for k, b in enumerate(bits) if (q >> k) & 1) for q in range(1 << len(bits))]
        return sum_all([value] + [permute_row(value, step) for step in steps[1:]])

    col_bits, row_bits = list(reversed(bits_of(n_col))), list(reversed(bits_of(n_row)))
    e_part = halve(e_part, permute_row, 1).astype(BF16)
    gi = sum_all([gi[0]] + [permute_col(gi[q], q) for q in range(1, n_col)]).astype(BF16)
    e_part, gi, h, w = lax.optimization_barrier((e_part, gi, h, w))

    h = halve(h, permute_col, 1).astype(BF16)
    for bit in col_bits[1:]:
        e_part = halve(e_part, permute_row, bit).astype(BF16)
    gi = row_sum(gi, row_bits[:1]).astype(BF16)
    h, e_part, gi, w = lax.optimization_barrier((h, e_part, gi, w))

    for bit in col_bits[1:]:
        h = halve(h.astype(BF16), permute_col, bit)

    e_own = sum_all([transpose(e_part[m], m, back=True) for m in range(groups)])
    gi = row_sum(gi, row_bits[1:2])
    most = tiles * 5 // 8
    updated = update(0, most, [])
    e_own, gi, updated, w = lax.optimization_barrier((e_own, gi, updated, w))

    updated = update(most, tiles - most, [updated])
    for bit in row_bits[2:]:
        gi = row_sum(gi.astype(BF16), [bit])
    h, updated, gi = lax.optimization_barrier((h[0], updated, gi))
    grad_panel = jnp.concatenate([h[:slots] + e_own, h[slots:]], 0)
    updated = updated.reshape(tiles, tile, tile // LANES, slabs, LANES).transpose(0, 1, 3, 2, 4)
    return (
        updated.reshape(slab.shape),
        grad_panel.transpose(0, 2, 1).reshape(panel.shape),
        gi.T,
    )


def solution(mesh):
    in_specs = (
        P(None, "row", None, "col"),
        P(None, "row", None, None, "col", None),
        P(None, "row", None, None, "col", None),
        P(),
    )
    out_specs = (
        P(None, "row", None, None, "col", None),
        P(None, "row", None, "col"),
        P(None, "col"),
    )
    return jax.shard_map(
        per_device, mesh=mesh, in_specs=in_specs, out_specs=out_specs, check_vma=False
    )
```

```python
import functools

import jax
import jax.numpy as jnp
from jax import lax
from jax.experimental import pallas as pl
from jax.experimental.pallas import tpu as pltpu
from jax.sharding import PartitionSpec as P

BOTH = ("row", "col")
F32 = jnp.float32
BF16 = jnp.bfloat16
LANES = 128
VMEM = pl.BlockSpec(memory_space=pltpu.VMEM)
SMEM = pl.BlockSpec(memory_space=pltpu.SMEM)
STREAMED = 58
ANY = pl.BlockSpec(memory_space=pl.ANY)


def bits_of(count):
    return [1 << b for b in reversed(range(count.bit_length() - 1))]


def reversed_bits(value, count):
    width = count.bit_length() - 1
    place = 0
    for b in range(width):
        place = place + (((value >> b) & 1) << (width - 1 - b))
    return place


def dot(a, b, dims, precision=None):
    return lax.dot_general(a, b, (dims, ((), ())), precision=precision, preferred_element_type=F32)


def whole(shape):
    return pl.BlockSpec(shape, lambda *_: (0,) * len(shape))


def params(mib=24):
    return pltpu.CompilerParams(vmem_limit_bytes=mib * 2**20)


def cost(flops, nbytes):
    return pl.CostEstimate(flops=flops, bytes_accessed=nbytes, transcendentals=0)


def unmix_kernel(slabs, tile, inv_ref, x_ref, o_ref, m_ref, wide_ref, ins, outs, in_sems, out_sems):
    step, steps = pl.program_id(0), ins.shape[0]
    size = ins.shape[1]

    def copy_in(t):
        at = pl.multiple_of(t * size, size)
        return pltpu.make_async_copy(x_ref.at[pl.ds(at, size)], ins.at[t], in_sems.at[t])

    def copy_out(t):
        at = pl.multiple_of(t * tile, tile)
        return pltpu.make_async_copy(outs.at[t], o_ref.at[pl.ds(at, tile)], out_sems.at[t])

    @pl.when(step == 0)
    def _():
        for t in range(steps):
            copy_in(t).start()
        mat = dot(inv_ref[...], inv_ref[...], ((0,), (0,)), lax.Precision.HIGHEST)
        high = mat.astype(BF16)
        m_ref[0] = high
        m_ref[1] = (mat - high.astype(F32)).astype(BF16)

    copy_in(step).wait()
    halves = tile // LANES
    wide_ref[...] = ins[step].astype(F32)
    for s in range(slabs):
        for h in range(halves):
            part = wide_ref[pl.ds(h * slabs + s, tile, stride=halves * slabs), :]
            outs[step, :, s * tile + h * LANES : s * tile + (h + 1) * LANES] = part.astype(BF16)
    copy_out(step).start()

    @pl.when(step == steps - 1)
    def _():
        for t in range(steps):
            copy_out(t).wait()


def q_kernel(n_row, n_col, groups, place_ref, *refs):
    parts, (m_ref, g_ref, q_ref, e_ref, pt_ref, ins, sems) = refs[:n_col], refs[n_col:]
    tiles, strip, tile = parts[0].shape
    s = pl.program_id(0)
    row, col = place_ref[0], place_ref[1]
    group, rho = row // n_col, (row % n_col) ^ (n_col // 2)

    def copy_in(at):
        columns = pl.ds(pl.multiple_of(at * tile, tile), tile)
        return pltpu.make_async_copy(g_ref.at[:, columns], ins.at[at], sems.at[at])

    @pl.when(s == 0)
    def _():
        for at in range(ins.shape[0]):
            copy_in(at).start()
        for q in range(n_col):
            at = pl.multiple_of((col ^ q) * strip, strip)
            for t in range(tiles):
                pt_ref[pl.ds(at, strip), t * tile : (t + 1) * tile] = parts[q][t]

    copy_in(s).wait()
    q_ref[s] = dot(pt_ref[...], ins[s], ((1,), (0,))).astype(BF16)

    @pl.when(s == pl.num_programs(0) - 1)
    def _():
        for at in range(q_ref.shape[0]):
            q_val = q_ref[at]
            e_val = -(dot(m_ref[0], q_val, ((1,), (0,))) + dot(m_ref[1], q_val, ((1,), (0,))))
            e_val = e_val.astype(BF16)
            slot, other = at // groups, group ^ (at % groups)
            for r in range(n_col):
                place = reversed_bits(rho ^ r, n_col) * groups + other
                e_ref[place, slot] = e_val[r * strip : (r + 1) * strip]


def w_kernel(n_row, n_col, groups, place_ref, *refs):
    tops, (m_ref, inv_ref, q_ref, w_ref, gi_ref, top_all) = refs[:2], refs[2:]
    slots, strip, tile = tops[0].shape[1:]
    half = tops[0].shape[0]
    slabs = slots * groups
    row, col = place_ref[0], place_ref[1]
    group, rho = row // n_col, (row % n_col) ^ (n_col // 2)
    for p in range(n_row):
        at = pl.multiple_of((rho ^ (p % n_col)) * strip, strip)
        place = reversed_bits(p % n_col, n_col) * groups + p // n_col
        for slot in range(slots):
            s = slot * groups + (group ^ (p // n_col))
            top_all[s, pl.ds(at, strip), :] = tops[place // half][place % half, slot]
    z = jnp.zeros((tile, tile), F32)
    for s in range(slabs):
        top = top_all[s]
        w = dot(m_ref[0], top, ((1,), (0,))) + dot(m_ref[1], top, ((1,), (0,)))
        w_ref[:, s * tile : (s + 1) * tile] = w.astype(BF16)
        z = z + dot(top, q_ref[s], ((1,), (1,)))
    z = z + z.T
    gi = -dot(z, inv_ref[...], ((1,), (1,)), lax.Precision.HIGHEST)
    for r in range(n_col):
        gi_ref[col ^ r] = gi[r * strip : (r + 1) * strip].astype(BF16)


def h_kernel(n_col, place_ref, w_ref, g_ref, h_ref):
    strip = h_ref.shape[2]
    t = pl.program_id(0)
    col = place_ref[1]
    h = -dot(w_ref[...], g_ref[...], ((1,), (1,)))
    for r in range(n_col):
        h_ref[reversed_bits(col ^ r, n_col), t] = h[r * strip : (r + 1) * strip].astype(BF16)


def update_kernel(slabs, tile, pt_ref, w_ref, x_ref, *refs):
    o_ref, wide_ref = refs[-2:]
    halves = tile // LANES
    product = dot(pt_ref[...], w_ref[...], ((0,), (0,)))
    for s in range(slabs):
        for h in range(halves):
            part = product[:, s * tile + h * LANES : s * tile + (h + 1) * LANES]
            wide_ref[pl.ds(h * slabs + s, tile, stride=halves * slabs), :] = part
    o_ref[...] = (x_ref[...].astype(F32) - wide_ref[...]).astype(BF16)


def mixed_rows(x):
    tiles, _, tile, slabs, _, _ = x.shape
    x = x.reshape(tiles, tile, slabs, tile // LANES, LANES).transpose(0, 1, 3, 2, 4)
    return x.reshape(-1, LANES)


def per_device(panel, slab, cotangent, inverse):
    tiles, _, tile, strip = panel.shape
    slabs = slab.shape[3]
    n_row = lax.axis_size("row")
    n_col = lax.axis_size("col")
    groups = n_row // n_col
    slots = slabs // groups
    width = slabs * tile
    rows = tiles * tile
    mixed = tile * width // LANES
    place = jnp.stack([lax.axis_index("row"), lax.axis_index("col")]).astype(jnp.int32)

    def permute_row(value, bit):
        return lax.ppermute(value, "row", [(i, i ^ bit) for i in range(n_row)])

    def permute_col(value, bit):
        return lax.ppermute(value, "col", [(i, i ^ bit) for i in range(n_col)])

    far = n_col // 2

    def transpose(value, across, back=False):
        pairs = []
        for m in range(groups):
            for a in range(n_col):
                for b in range(n_col):
                    here = (m * n_col + a) * n_col + b
                    there = ((m ^ across) * n_col + (b ^ far)) * n_col + a
                    pairs.append((there, here) if back else (here, there))
        return lax.ppermute(value, BOTH, pairs)

    own = panel.reshape(tiles, tile, strip).transpose(0, 2, 1).astype(BF16)
    high, *lower = bits_of(n_col)
    parts = {0: own, high: permute_col(own, high)}
    tops = [transpose(own[:slots], m) for m in range(groups)]
    cot, mat = pl.pallas_call(
        functools.partial(unmix_kernel, slabs, tile),
        grid=(tiles,),
        in_specs=[whole((tile, tile)), ANY],
        out_specs=[ANY, whole((2, tile, tile))],
        out_shape=[
            jax.ShapeDtypeStruct((rows, width), BF16),
            jax.ShapeDtypeStruct((2, tile, tile), BF16),
        ],
        scratch_shapes=[
            pltpu.VMEM((mixed, LANES), F32),
            pltpu.VMEM((tiles, mixed, LANES), BF16),
            pltpu.VMEM((tiles, tile, width), BF16),
            pltpu.SemaphoreType.DMA((tiles,)),
            pltpu.SemaphoreType.DMA((tiles,)),
        ],
        compiler_params=params(STREAMED),
        cost_estimate=cost(0, 4 * rows * width),
    )(inverse, mixed_rows(cotangent))

    tops, own, mat = lax.optimization_barrier((tops, own, mat))

    top = jnp.stack(tops)
    for bit in bits_of(n_col)[:-1]:
        top = jnp.concatenate([top, permute_row(top, bit)], 0)
    if lower:
        parts[1] = permute_col(own, 1)
    top, parts = lax.optimization_barrier((top, parts))

    for bit in lower:
        for q in range(0, n_col, 2 * bit):
            if q | bit not in parts:
                parts[q | bit] = permute_col(parts[q], bit)
    tops = [top, permute_row(top, 1)]

    q_sum, e_part, panel_all = pl.pallas_call(
        functools.partial(q_kernel, n_row, n_col, groups),
        grid=(slabs,),
        in_specs=[SMEM]
        + [whole((tiles, strip, tile))] * n_col
        + [whole((2, tile, tile)), ANY],
        out_specs=[
            whole((slabs, tile, tile)),
            whole((n_row, slots, strip, tile)),
            whole((tile, rows)),
        ],
        out_shape=[
            jax.ShapeDtypeStruct((slabs, tile, tile), BF16),
            jax.ShapeDtypeStruct((n_row, slots, strip, tile), BF16),
            jax.ShapeDtypeStruct((tile, rows), BF16),
        ],
        scratch_shapes=[
            pltpu.VMEM((slabs, rows, tile), BF16),
            pltpu.SemaphoreType.DMA((slabs,)),
        ],
        compiler_params=params(STREAMED - 10),
        cost_estimate=cost(2 * rows * width * tile, 2 * rows * (width + tile)),
    )(place, *[parts[q] for q in range(n_col)], mat, cot)

    w, gi = pl.pallas_call(
        functools.partial(w_kernel, n_row, n_col, groups),
        in_specs=[SMEM] + [VMEM] * 5,
        out_specs=[VMEM, VMEM],
        out_shape=[
            jax.ShapeDtypeStruct((tile, width), BF16),
            jax.ShapeDtypeStruct((n_col, strip, tile), BF16),
        ],
        scratch_shapes=[pltpu.VMEM((slabs, tile, tile), BF16)],
        compiler_params=params(),
        cost_estimate=cost(tile, tile),
    )(place, *tops, mat, inverse, q_sum)

    def h_part(first, count):
        return pl.pallas_call(
            functools.partial(h_kernel, n_col),
            grid=(count,),
            in_specs=[
                SMEM,
                whole((tile, width)),
                pl.BlockSpec((tile, width), lambda t: (t + first, 0)),
            ],
            out_specs=whole((n_col, count, strip, tile)),
            out_shape=jax.ShapeDtypeStruct((n_col, count, strip, tile), BF16),
            compiler_params=params(),
            cost_estimate=cost(tile, tile),
        )(place, w, cot)

    def update(first, count, previous):
        return pl.pallas_call(
            functools.partial(update_kernel, slabs, tile),
            grid=(count,),
            in_specs=[
                pl.BlockSpec((tile, tile), lambda t: (0, t + first)),
                whole((tile, width)),
                pl.BlockSpec((mixed, LANES), lambda t: (t + first, 0)),
            ]
            + [ANY] * len(previous),
            out_specs=pl.BlockSpec((mixed, LANES), lambda t: (t + first, 0)),
            out_shape=jax.ShapeDtypeStruct((tiles * mixed, LANES), BF16),
            scratch_shapes=[pltpu.VMEM((mixed, LANES), F32)],
            input_output_aliases={3: 0} if previous else {},
            compiler_params=params(),
            cost_estimate=cost(2 * count * tile * width * tile, 4 * count * tile * width),
        )(panel_all, w, mixed_rows(slab), *previous)

    def halve(value, exchange, bit):
        half = value.shape[0] // 2
        return value[:half].astype(F32) + exchange(value[half:], bit).astype(F32)

    def sum_all(values):
        values = [v.astype(F32) for v in values]
        while len(values) > 1:
            values = [values[i] + values[i + 1] for i in range(0, len(values), 2)]
        return values[0]

    def row_sum(value, bits):
        steps = [sum(b for k, b in enumerate(bits) if (q >> k) & 1) for q in range(1 << len(bits))]
        return sum_all([value] + [permute_row(value, step) for step in steps[1:]])

    col_bits, row_bits = list(reversed(bits_of(n_col))), list(reversed(bits_of(n_row)))
    half = tiles // 2
    some = tiles * 3 // 8
    e_part = halve(e_part, permute_row, 1).astype(BF16)
    gi = sum_all([gi[0]] + [permute_col(gi[q], q) for q in range(1, n_col)]).astype(BF16)
    h_low = h_part(0, half)
    e_part, gi, h_low, w = lax.optimization_barrier((e_part, gi, h_low, w))

    gi = row_sum(gi, row_bits[:1]).astype(BF16)
    h_low = halve(h_low, permute_col, 1).astype(BF16)
    h_high = h_part(half, tiles - half)
    e_part, gi, h_low, h_high, w = lax.optimization_barrier((e_part, gi, h_low, h_high, w))

    for bit in col_bits[1:]:
        e_part = halve(e_part, permute_row, bit).astype(BF16)
    h_high = halve(h_high, permute_col, 1).astype(BF16)
    gi = row_sum(gi, row_bits[1:2])
    for bit in col_bits[1:]:
        h_low = halve(h_low.astype(BF16), permute_col, bit)
    updated = update(0, some, [])
    e_part, gi, h_high, updated, w = lax.optimization_barrier((e_part, gi, h_high, updated, w))

    for bit in col_bits[1:]:
        h_high = halve(h_high.astype(BF16), permute_col, bit)
    e_own = sum_all([transpose(e_part[m], m, back=True) for m in range(groups)])
    for bit in row_bits[2:]:
        gi = row_sum(gi.astype(BF16), [bit])
    updated = update(some, tiles - some, [updated])
    h_low, h_high, e_own, gi, updated = lax.optimization_barrier((h_low, h_high, e_own, gi, updated))
    h = jnp.concatenate([h_low[0], h_high[0]], 0)
    grad_panel = jnp.concatenate([h[:slots] + e_own, h[slots:]], 0)
    updated = updated.reshape(tiles, tile, tile // LANES, slabs, LANES).transpose(0, 1, 3, 2, 4)
    return (
        updated.reshape(slab.shape),
        grad_panel.transpose(0, 2, 1).reshape(panel.shape),
        gi.T,
    )


def solution(mesh):
    in_specs = (
        P(None, "row", None, "col"),
        P(None, "row", None, None, "col", None),
        P(None, "row", None, None, "col", None),
        P(),
    )
    out_specs = (
        P(None, "row", None, None, "col", None),
        P(None, "row", None, "col"),
        P(None, "col"),
    )
    return jax.shard_map(
        per_device, mesh=mesh, in_specs=in_specs, out_specs=out_specs, check_vma=False
    )
```

```python
import functools

import jax
import jax.numpy as jnp
from jax import lax
from jax.experimental import pallas as pl
from jax.experimental.pallas import tpu as pltpu
from jax.sharding import PartitionSpec as P

BOTH = ("row", "col")
F32 = jnp.float32
BF16 = jnp.bfloat16
LANES = 128
VMEM = pl.BlockSpec(memory_space=pltpu.VMEM)
SMEM = pl.BlockSpec(memory_space=pltpu.SMEM)
STREAMED = 58
ANY = pl.BlockSpec(memory_space=pl.ANY)


def bits_of(count):
    return [1 << b for b in reversed(range(count.bit_length() - 1))]


def reversed_bits(value, count):
    width = count.bit_length() - 1
    place = 0
    for b in range(width):
        place = place + (((value >> b) & 1) << (width - 1 - b))
    return place


def dot(a, b, dims, precision=None):
    return lax.dot_general(a, b, (dims, ((), ())), precision=precision, preferred_element_type=F32)


def whole(shape):
    return pl.BlockSpec(shape, lambda *_: (0,) * len(shape))


def params(mib=24):
    return pltpu.CompilerParams(vmem_limit_bytes=mib * 2**20)


def cost(flops, nbytes):
    return pl.CostEstimate(flops=flops, bytes_accessed=nbytes, transcendentals=0)


def unmix_kernel(slabs, tile, first, *refs):
    if first:
        x_ref, _, o_ref, wide_ref, ins, outs, in_sems, out_sems = refs
    else:
        inv_ref, x_ref, o_ref, m_ref, wide_ref, ins, outs, in_sems, out_sems = refs
    step, steps = pl.program_id(0), ins.shape[0]
    size = ins.shape[1]

    def copy_in(t):
        at = pl.multiple_of((first + t) * size, size)
        return pltpu.make_async_copy(x_ref.at[pl.ds(at, size)], ins.at[t], in_sems.at[t])

    def copy_out(t):
        at = pl.multiple_of((first + t) * tile, tile)
        return pltpu.make_async_copy(outs.at[t], o_ref.at[pl.ds(at, tile)], out_sems.at[t])

    @pl.when(step == 0)
    def _():
        for t in range(steps):
            copy_in(t).start()
        if not first:
            mat = dot(inv_ref[...], inv_ref[...], ((0,), (0,)), lax.Precision.HIGHEST)
            high = mat.astype(BF16)
            m_ref[0] = high
            m_ref[1] = (mat - high.astype(F32)).astype(BF16)

    copy_in(step).wait()
    halves = tile // LANES
    wide_ref[...] = ins[step].astype(F32)
    for s in range(slabs):
        for h in range(halves):
            part = wide_ref[pl.ds(h * slabs + s, tile, stride=halves * slabs), :]
            outs[step, :, s * tile + h * LANES : s * tile + (h + 1) * LANES] = part.astype(BF16)
    copy_out(step).start()

    @pl.when(step == steps - 1)
    def _():
        for t in range(steps):
            copy_out(t).wait()


def q_kernel(n_row, n_col, groups, place_ref, *refs):
    parts, (m_any, g_ref, q_ref, e_ref, pt_ref, ins, m_ref, sems) = refs[:n_col], refs[n_col:]
    copy_m = pltpu.make_async_copy(m_any, m_ref, sems.at[ins.shape[0]])
    tiles, strip, tile = parts[0].shape
    s = pl.program_id(0)
    row, col = place_ref[0], place_ref[1]
    group, rho = row // n_col, (row % n_col) ^ (n_col // 2)

    def copy_in(at):
        columns = pl.ds(pl.multiple_of(at * tile, tile), tile)
        return pltpu.make_async_copy(g_ref.at[:, columns], ins.at[at], sems.at[at])

    @pl.when(s == 0)
    def _():
        for at in range(ins.shape[0]):
            copy_in(at).start()
        copy_m.start()
        for q in range(n_col):
            at = pl.multiple_of((col ^ q) * strip, strip)
            for t in range(tiles):
                pt_ref[pl.ds(at, strip), t * tile : (t + 1) * tile] = parts[q][t]

    copy_in(s).wait()
    q_ref[s] = dot(pt_ref[...], ins[s], ((1,), (0,))).astype(BF16)

    @pl.when(s == pl.num_programs(0) - 1)
    def _():
        copy_m.wait()
        for at in range(q_ref.shape[0]):
            q_val = q_ref[at]
            e_val = -(dot(m_ref[0], q_val, ((1,), (0,))) + dot(m_ref[1], q_val, ((1,), (0,))))
            e_val = e_val.astype(BF16)
            slot, other = at // groups, group ^ (at % groups)
            for r in range(n_col):
                e_ref[rho ^ r, other, slot] = e_val[r * strip : (r + 1) * strip]


def w_kernel(n_row, n_col, groups, place_ref, *refs):
    tops, (m_ref, inv_ref, q_ref, w_ref, gi_ref, top_all) = refs[:n_col], refs[n_col:]
    slots, strip, tile = tops[0].shape[1:]
    slabs = slots * groups
    row, col = place_ref[0], place_ref[1]
    group, rho = row // n_col, (row % n_col) ^ (n_col // 2)
    for p in range(n_row):
        at = pl.multiple_of((rho ^ (p % n_col)) * strip, strip)
        for slot in range(slots):
            s = slot * groups + (group ^ (p // n_col))
            top_all[s, pl.ds(at, strip), :] = tops[p % n_col][p // n_col, slot]
    z = jnp.zeros((tile, tile), F32)
    for s in range(slabs):
        top = top_all[s]
        w = dot(m_ref[0], top, ((1,), (0,))) + dot(m_ref[1], top, ((1,), (0,)))
        w_ref[:, s * tile : (s + 1) * tile] = w.astype(BF16)
        z = z + dot(top, q_ref[s], ((1,), (1,)))
    z = z + z.T
    gi = -dot(z, inv_ref[...], ((1,), (1,)), lax.Precision.HIGHEST)
    for r in range(n_col):
        gi_ref[reversed_bits(col ^ r, n_col)] = gi[r * strip : (r + 1) * strip].astype(BF16)


def h_kernel(n_col, place_ref, w_ref, g_ref, h_ref):
    strip = h_ref.shape[2]
    t = pl.program_id(0)
    col = place_ref[1]
    h = -dot(w_ref[...], g_ref[...], ((1,), (1,)))
    for r in range(n_col):
        h_ref[reversed_bits(col ^ r, n_col), t] = h[r * strip : (r + 1) * strip].astype(BF16)


def update_kernel(slabs, tile, pt_ref, w_ref, x_ref, *refs):
    o_ref, wide_ref = refs[-2:]
    halves = tile // LANES
    product = dot(pt_ref[...], w_ref[...], ((0,), (0,)))
    for s in range(slabs):
        for h in range(halves):
            part = product[:, s * tile + h * LANES : s * tile + (h + 1) * LANES]
            wide_ref[pl.ds(h * slabs + s, tile, stride=halves * slabs), :] = part
    o_ref[...] = (x_ref[...].astype(F32) - wide_ref[...]).astype(BF16)


def mixed_rows(x):
    tiles, _, tile, slabs, _, _ = x.shape
    x = x.reshape(tiles, tile, slabs, tile // LANES, LANES).transpose(0, 1, 3, 2, 4)
    return x.reshape(-1, LANES)


def per_device(panel, slab, cotangent, inverse):
    tiles, _, tile, strip = panel.shape
    slabs = slab.shape[3]
    n_row = lax.axis_size("row")
    n_col = lax.axis_size("col")
    groups = n_row // n_col
    slots = slabs // groups
    width = slabs * tile
    rows = tiles * tile
    mixed = tile * width // LANES
    place = jnp.stack([lax.axis_index("row"), lax.axis_index("col")]).astype(jnp.int32)

    def permute_row(value, bit):
        return lax.ppermute(value, "row", [(i, i ^ bit) for i in range(n_row)])

    def permute_col(value, bit):
        return lax.ppermute(value, "col", [(i, i ^ bit) for i in range(n_col)])

    far = n_col // 2

    def transpose(value, across, back=False):
        pairs = []
        for m in range(groups):
            for a in range(n_col):
                for b in range(n_col):
                    here = (m * n_col + a) * n_col + b
                    there = ((m ^ across) * n_col + (b ^ far)) * n_col + a
                    pairs.append((there, here) if back else (here, there))
        return lax.ppermute(value, BOTH, pairs)

    own = panel.reshape(tiles, tile, strip).transpose(0, 2, 1).astype(BF16)
    def unmix(first, count, *args):
        outs = [ANY] if first else [ANY, whole((2, tile, tile))]
        shapes = [
            jax.ShapeDtypeStruct((rows, width), BF16),
            jax.ShapeDtypeStruct((2, tile, tile), BF16),
        ]
        return pl.pallas_call(
            functools.partial(unmix_kernel, slabs, tile, first),
            grid=(count,),
            in_specs=[ANY, ANY] if first else [whole((tile, tile)), ANY],
            out_specs=outs,
            out_shape=shapes[: len(outs)],
            scratch_shapes=[
                pltpu.VMEM((mixed, LANES), F32),
                pltpu.VMEM((count, mixed, LANES), BF16),
                pltpu.VMEM((count, tile, width), BF16),
                pltpu.SemaphoreType.DMA((count,)),
                pltpu.SemaphoreType.DMA((count,)),
            ],
            input_output_aliases={1: 0} if first else {},
            compiler_params=params(STREAMED),
            cost_estimate=cost(0, 4 * count * tile * width),
        )(*args)

    high, *lower = bits_of(n_col)
    half = tiles // 2
    parts = {0: own, high: permute_col(own, high)}
    if lower:
        parts[1] = permute_col(own, 1)
    tops = [transpose(own[:slots], m) for m in range(groups)]
    cot, mat = unmix(0, half, inverse, mixed_rows(cotangent))
    tops, parts, mat = lax.optimization_barrier((tops, parts, mat))

    top = jnp.stack(tops)
    tops = [top] + [permute_row(top, q) for q in range(1, n_col)]
    for bit in lower:
        for q in range(0, n_col, 2 * bit):
            if q | bit not in parts:
                parts[q | bit] = permute_col(parts[q], bit)
    (cot,) = unmix(half, tiles - half, mixed_rows(cotangent), cot)

    q_sum, e_part, panel_all = pl.pallas_call(
        functools.partial(q_kernel, n_row, n_col, groups),
        grid=(slabs,),
        in_specs=[SMEM]
        + [whole((tiles, strip, tile))] * n_col
        + [ANY, ANY],
        out_specs=[
            whole((slabs, tile, tile)),
            whole((n_col, groups, slots, strip, tile)),
            whole((tile, rows)),
        ],
        out_shape=[
            jax.ShapeDtypeStruct((slabs, tile, tile), BF16),
            jax.ShapeDtypeStruct((n_col, groups, slots, strip, tile), BF16),
            jax.ShapeDtypeStruct((tile, rows), BF16),
        ],
        scratch_shapes=[
            pltpu.VMEM((slabs, rows, tile), BF16),
            pltpu.VMEM((2, tile, tile), BF16),
            pltpu.SemaphoreType.DMA((slabs + 1,)),
        ],
        compiler_params=params(STREAMED - 10),
        cost_estimate=cost(2 * rows * width * tile, 2 * rows * (width + tile)),
    )(place, *[parts[q] for q in range(n_col)], mat, cot)

    w, gi = pl.pallas_call(
        functools.partial(w_kernel, n_row, n_col, groups),
        in_specs=[SMEM] + [VMEM] * (n_col + 3),
        out_specs=[VMEM, VMEM],
        out_shape=[
            jax.ShapeDtypeStruct((tile, width), BF16),
            jax.ShapeDtypeStruct((n_col, strip, tile), BF16),
        ],
        scratch_shapes=[pltpu.VMEM((slabs, tile, tile), BF16)],
        compiler_params=params(),
        cost_estimate=cost(tile, tile),
    )(place, *tops, mat, inverse, q_sum)

    def h_part(first, count):
        return pl.pallas_call(
            functools.partial(h_kernel, n_col),
            grid=(count,),
            in_specs=[
                SMEM,
                whole((tile, width)),
                pl.BlockSpec((tile, width), lambda t: (t + first, 0)),
            ],
            out_specs=whole((n_col, count, strip, tile)),
            out_shape=jax.ShapeDtypeStruct((n_col, count, strip, tile), BF16),
            compiler_params=params(),
            cost_estimate=cost(2 * count * tile * width * tile, 4 * count * tile * width),
        )(place, w, cot)

    def update(first, count, previous):
        return pl.pallas_call(
            functools.partial(update_kernel, slabs, tile),
            grid=(count,),
            in_specs=[
                pl.BlockSpec((tile, tile), lambda t: (0, t + first)),
                whole((tile, width)),
                pl.BlockSpec((mixed, LANES), lambda t: (t + first, 0)),
            ]
            + [ANY] * len(previous),
            out_specs=pl.BlockSpec((mixed, LANES), lambda t: (t + first, 0)),
            out_shape=jax.ShapeDtypeStruct((tiles * mixed, LANES), BF16),
            scratch_shapes=[pltpu.VMEM((mixed, LANES), F32)],
            input_output_aliases={3: 0} if previous else {},
            compiler_params=params(),
            cost_estimate=cost(2 * count * tile * width * tile, 4 * count * tile * width),
        )(panel_all, w, mixed_rows(slab), *previous)

    def halve(value, exchange, bit):
        half = value.shape[0] // 2
        return value[:half].astype(F32) + exchange(value[half:], bit).astype(F32)

    def sum_all(values):
        values = [v.astype(F32) for v in values]
        while len(values) > 1:
            values = [values[i] + values[i + 1] for i in range(0, len(values), 2)]
        return values[0]

    def row_sum(value, bits):
        steps = [sum(b for k, b in enumerate(bits) if (q >> k) & 1) for q in range(1 << len(bits))]
        return sum_all([value] + [permute_row(value, step) for step in steps[1:]])

    col_bits, row_bits = list(reversed(bits_of(n_col))), list(reversed(bits_of(n_row)))
    some = tiles * 3 // 8
    e_part = sum_all([e_part[0]] + [permute_row(e_part[q], q) for q in range(1, n_col)]).astype(BF16)
    gi = halve(gi, permute_col, 1).astype(BF16)
    h_low = h_part(0, half)
    e_part, gi, h_low, w = lax.optimization_barrier((e_part, gi, h_low, w))

    e_own = sum_all([transpose(e_part[m], m, back=True) for m in range(groups)])
    for bit in col_bits[1:]:
        gi = halve(gi, permute_col, bit).astype(BF16)
    h_low = halve(h_low, permute_col, 1).astype(BF16)
    h_high = h_part(half, tiles - half)
    e_own, gi, h_low, h_high, w = lax.optimization_barrier((e_own, gi[0], h_low, h_high, w))

    h_high = halve(h_high, permute_col, 1).astype(BF16)
    gi = row_sum(gi, row_bits[:2])
    for bit in col_bits[1:]:
        h_low = halve(h_low.astype(BF16), permute_col, bit)
    updated = update(0, some, [])
    gi, h_high, updated, w = lax.optimization_barrier((gi, h_high, updated, w))

    for bit in col_bits[1:]:
        h_high = halve(h_high.astype(BF16), permute_col, bit)
    for bit in row_bits[2:]:
        gi = row_sum(gi.astype(BF16), [bit])
    updated = update(some, tiles - some, [updated])
    h_low, h_high, gi, updated = lax.optimization_barrier((h_low, h_high, gi, updated))
    h = jnp.concatenate([h_low[0], h_high[0]], 0)
    grad_panel = jnp.concatenate([h[:slots] + e_own, h[slots:]], 0)
    updated = updated.reshape(tiles, tile, tile // LANES, slabs, LANES).transpose(0, 1, 3, 2, 4)
    return (
        updated.reshape(slab.shape),
        grad_panel.transpose(0, 2, 1).reshape(panel.shape),
        gi.T,
    )


def solution(mesh):
    in_specs = (
        P(None, "row", None, "col"),
        P(None, "row", None, None, "col", None),
        P(None, "row", None, None, "col", None),
        P(),
    )
    out_specs = (
        P(None, "row", None, None, "col", None),
        P(None, "row", None, "col"),
        P(None, "col"),
    )
    return jax.shard_map(
        per_device, mesh=mesh, in_specs=in_specs, out_specs=out_specs, check_vma=False
    )
```

```python
import functools

import jax
import jax.numpy as jnp
from jax import lax
from jax.experimental import pallas as pl
from jax.experimental.pallas import tpu as pltpu
from jax.sharding import PartitionSpec as P

BOTH = ("row", "col")
F32 = jnp.float32
BF16 = jnp.bfloat16
LANES = 128
VMEM = pl.BlockSpec(memory_space=pltpu.VMEM)
SMEM = pl.BlockSpec(memory_space=pltpu.SMEM)
STREAMED = 58
ANY = pl.BlockSpec(memory_space=pl.ANY)


def bits_of(count):
    return [1 << b for b in reversed(range(count.bit_length() - 1))]


def reversed_bits(value, count):
    width = count.bit_length() - 1
    place = 0
    for b in range(width):
        place = place + (((value >> b) & 1) << (width - 1 - b))
    return place


def dot(a, b, dims, precision=None):
    return lax.dot_general(a, b, (dims, ((), ())), precision=precision, preferred_element_type=F32)


def whole(shape):
    return pl.BlockSpec(shape, lambda *_: (0,) * len(shape))


def params(mib=24):
    return pltpu.CompilerParams(vmem_limit_bytes=mib * 2**20)


def cost(flops, nbytes):
    return pl.CostEstimate(flops=flops, bytes_accessed=nbytes, transcendentals=0)


def unmix_kernel(slabs, tile, x_ref, o_ref, token_ref, wide_ref, ins, outs, in_sems, out_sems):
    step, steps = pl.program_id(0), ins.shape[0]
    size = ins.shape[1]

    def copy_in(t):
        at = pl.multiple_of(t * size, size)
        return pltpu.make_async_copy(x_ref.at[pl.ds(at, size)], ins.at[t], in_sems.at[t])

    def copy_out(t):
        at = pl.multiple_of(t * tile, tile)
        return pltpu.make_async_copy(outs.at[t], o_ref.at[pl.ds(at, tile)], out_sems.at[t])

    @pl.when(step == 0)
    def _():
        for t in range(steps):
            copy_in(t).start()
        token_ref[...] = jnp.zeros_like(token_ref)

    copy_in(step).wait()
    halves = tile // LANES
    wide_ref[...] = ins[step].astype(F32)
    for s in range(slabs):
        for h in range(halves):
            part = wide_ref[pl.ds(h * slabs + s, tile, stride=halves * slabs), :]
            outs[step, :, s * tile + h * LANES : s * tile + (h + 1) * LANES] = part.astype(BF16)
    copy_out(step).start()

    @pl.when(step == steps - 1)
    def _():
        for t in range(steps):
            copy_out(t).wait()


def q_kernel(n_row, n_col, groups, place_ref, *refs):
    parts, (inv_ref, g_ref, q_ref, e_ref, pt_ref, m_ref, ins, sems) = refs[:n_col], refs[n_col:]
    tiles, strip, tile = parts[0].shape
    s = pl.program_id(0)
    row, col = place_ref[0], place_ref[1]
    group, rho = row // n_col, (row % n_col) ^ (n_col // 2)

    def copy_in(at):
        columns = pl.ds(pl.multiple_of(at * tile, tile), tile)
        return pltpu.make_async_copy(g_ref.at[:, columns], ins.at[at], sems.at[at])

    @pl.when(s == 0)
    def _():
        for at in range(ins.shape[0]):
            copy_in(at).start()
        mat = dot(inv_ref[...], inv_ref[...], ((0,), (0,)), lax.Precision.HIGHEST)
        high = mat.astype(BF16)
        m_ref[0] = high
        m_ref[1] = (mat - high.astype(F32)).astype(BF16)
        for q in range(n_col):
            at = pl.multiple_of((col ^ q) * strip, strip)
            for t in range(tiles):
                pt_ref[pl.ds(at, strip), t * tile : (t + 1) * tile] = parts[q][t]

    copy_in(s).wait()
    q_ref[s] = dot(pt_ref[...], ins[s], ((1,), (0,))).astype(BF16)

    @pl.when(s == pl.num_programs(0) - 1)
    def _():
        for at in range(q_ref.shape[0]):
            q_val = q_ref[at]
            e_val = -(dot(m_ref[0], q_val, ((1,), (0,))) + dot(m_ref[1], q_val, ((1,), (0,))))
            e_val = e_val.astype(BF16)
            slot, other = at // groups, group ^ (at % groups)
            for r in range(n_col):
                e_ref[reversed_bits(rho ^ r, n_col), other, slot] = e_val[r * strip : (r + 1) * strip]


def w_kernel(n_row, n_col, groups, place_ref, *refs):
    tops, (m_ref, inv_ref, q_ref, _, w_ref, wt_ref, gi_ref, top_all) = refs[:n_col], refs[n_col:]
    slots, strip, tile = tops[0].shape[1:]
    slabs = slots * groups
    row, col = place_ref[0], place_ref[1]
    group, rho = row // n_col, (row % n_col) ^ (n_col // 2)
    for p in range(n_row):
        at = pl.multiple_of((rho ^ (p % n_col)) * strip, strip)
        for slot in range(slots):
            s = slot * groups + (group ^ (p // n_col))
            top_all[s, pl.ds(at, strip), :] = tops[p % n_col][p // n_col, slot]
    z = jnp.zeros((tile, tile), F32)
    for s in range(slabs):
        top = top_all[s]
        w = dot(m_ref[0], top, ((1,), (0,))) + dot(m_ref[1], top, ((1,), (0,)))
        w = w.astype(BF16)
        w_ref[:, s * tile : (s + 1) * tile] = w
        wt_ref[s * tile : (s + 1) * tile, :] = w.T
        z = z + dot(top, q_ref[s], ((1,), (1,)))
    z = z + z.T
    gi = -dot(z, inv_ref[...], ((1,), (1,)), lax.Precision.HIGHEST)
    for r in range(n_col):
        gi_ref[col ^ r] = gi[r * strip : (r + 1) * strip].astype(BF16)


def h_kernel(n_col, place_ref, wt_ref, g_ref, h_ref):
    strip = h_ref.shape[2]
    t = pl.program_id(0)
    col = place_ref[1]
    h = -dot(g_ref[...], wt_ref[...], ((1,), (0,)))
    h = h.astype(BF16).T
    for r in range(n_col):
        h_ref[reversed_bits(col ^ r, n_col), t] = h[r * strip : (r + 1) * strip]


def update_kernel(slabs, tile, pt_ref, w_ref, x_ref, *refs):
    o_ref, wide_ref = refs[-2:]
    halves = tile // LANES
    product = dot(pt_ref[...], w_ref[...], ((0,), (0,)))
    for s in range(slabs):
        for h in range(halves):
            part = product[:, s * tile + h * LANES : s * tile + (h + 1) * LANES]
            wide_ref[pl.ds(h * slabs + s, tile, stride=halves * slabs), :] = part
    o_ref[...] = (x_ref[...].astype(F32) - wide_ref[...]).astype(BF16)


def mixed_rows(x):
    tiles, _, tile, slabs, _, _ = x.shape
    x = x.reshape(tiles, tile, slabs, tile // LANES, LANES).transpose(0, 1, 3, 2, 4)
    return x.reshape(-1, LANES)


def per_device(panel, slab, cotangent, inverse):
    tiles, _, tile, strip = panel.shape
    slabs = slab.shape[3]
    n_row = lax.axis_size("row")
    n_col = lax.axis_size("col")
    groups = n_row // n_col
    slots = slabs // groups
    width = slabs * tile
    rows = tiles * tile
    mixed = tile * width // LANES
    place = jnp.stack([lax.axis_index("row"), lax.axis_index("col")]).astype(jnp.int32)

    def permute_row(value, bit):
        return lax.ppermute(value, "row", [(i, i ^ bit) for i in range(n_row)])

    def permute_col(value, bit):
        return lax.ppermute(value, "col", [(i, i ^ bit) for i in range(n_col)])

    far = n_col // 2

    def transpose(value, across, back=False):
        pairs = []
        for m in range(groups):
            for a in range(n_col):
                for b in range(n_col):
                    here = (m * n_col + a) * n_col + b
                    there = ((m ^ across) * n_col + (b ^ far)) * n_col + a
                    pairs.append((there, here) if back else (here, there))
        return lax.ppermute(value, BOTH, pairs)

    own = panel.reshape(tiles, tile, strip).transpose(0, 2, 1).astype(BF16)
    high, *lower = bits_of(n_col)
    half = tiles // 2
    parts = {0: own, high: permute_col(own, high)}
    if lower:
        parts[1] = permute_col(own, 1)
    tops = [transpose(own[:slots], m) for m in range(groups)]
    cot, token = pl.pallas_call(
        functools.partial(unmix_kernel, slabs, tile),
        grid=(tiles,),
        in_specs=[ANY],
        out_specs=[ANY, whole((8, LANES))],
        out_shape=[
            jax.ShapeDtypeStruct((rows, width), BF16),
            jax.ShapeDtypeStruct((8, LANES), F32),
        ],
        scratch_shapes=[
            pltpu.VMEM((mixed, LANES), F32),
            pltpu.VMEM((tiles, mixed, LANES), BF16),
            pltpu.VMEM((tiles, tile, width), BF16),
            pltpu.SemaphoreType.DMA((tiles,)),
            pltpu.SemaphoreType.DMA((tiles,)),
        ],
        compiler_params=params(STREAMED),
        cost_estimate=cost(0, 4 * rows * width),
    )(mixed_rows(cotangent))

    tops, parts, token = lax.optimization_barrier((tops, parts, token))

    top = jnp.stack(tops)
    tops = [top] + [permute_row(top, q) for q in range(1, n_col)]
    for bit in lower:
        for q in range(0, n_col, 2 * bit):
            if q | bit not in parts:
                parts[q | bit] = permute_col(parts[q], bit)

    q_sum, e_part, panel_all, mat = pl.pallas_call(
        functools.partial(q_kernel, n_row, n_col, groups),
        grid=(slabs,),
        in_specs=[SMEM]
        + [whole((tiles, strip, tile))] * n_col
        + [whole((tile, tile)), ANY],
        out_specs=[
            whole((slabs, tile, tile)),
            whole((n_col, groups, slots, strip, tile)),
            whole((tile, rows)),
            whole((2, tile, tile)),
        ],
        out_shape=[
            jax.ShapeDtypeStruct((slabs, tile, tile), BF16),
            jax.ShapeDtypeStruct((n_col, groups, slots, strip, tile), BF16),
            jax.ShapeDtypeStruct((tile, rows), BF16),
            jax.ShapeDtypeStruct((2, tile, tile), BF16),
        ],
        scratch_shapes=[
            pltpu.VMEM((slabs, rows, tile), BF16),
            pltpu.SemaphoreType.DMA((slabs,)),
        ],
        compiler_params=params(STREAMED - 10),
        cost_estimate=cost(2 * rows * width * tile, 2 * rows * (width + tile)),
    )(place, *[parts[q] for q in range(n_col)], inverse, cot)

    w, w_flip, gi = pl.pallas_call(
        functools.partial(w_kernel, n_row, n_col, groups),
        in_specs=[SMEM] + [VMEM] * (n_col + 3) + [ANY],
        out_specs=[VMEM, VMEM, VMEM],
        out_shape=[
            jax.ShapeDtypeStruct((tile, width), BF16),
            jax.ShapeDtypeStruct((width, tile), BF16),
            jax.ShapeDtypeStruct((n_col, strip, tile), BF16),
        ],
        scratch_shapes=[pltpu.VMEM((slabs, tile, tile), BF16)],
        compiler_params=params(),
        cost_estimate=cost(tile, tile),
    )(place, *tops, mat, inverse, q_sum, token)

    def h_part(first, count):
        return pl.pallas_call(
            functools.partial(h_kernel, n_col),
            grid=(count,),
            in_specs=[
                SMEM,
                whole((width, tile)),
                pl.BlockSpec((tile, width), lambda t: (t + first, 0)),
            ],
            out_specs=whole((n_col, count, strip, tile)),
            out_shape=jax.ShapeDtypeStruct((n_col, count, strip, tile), BF16),
            compiler_params=params(),
            cost_estimate=cost(tile, tile),
        )(place, w_flip, cot)

    def update(first, count, previous):
        return pl.pallas_call(
            functools.partial(update_kernel, slabs, tile),
            grid=(count,),
            in_specs=[
                pl.BlockSpec((tile, tile), lambda t: (0, t + first)),
                whole((tile, width)),
                pl.BlockSpec((mixed, LANES), lambda t: (t + first, 0)),
            ]
            + [ANY] * len(previous),
            out_specs=pl.BlockSpec((mixed, LANES), lambda t: (t + first, 0)),
            out_shape=jax.ShapeDtypeStruct((tiles * mixed, LANES), BF16),
            scratch_shapes=[pltpu.VMEM((mixed, LANES), F32)],
            input_output_aliases={3: 0} if previous else {},
            compiler_params=params(),
            cost_estimate=cost(2 * count * tile * width * tile, 4 * count * tile * width),
        )(panel_all, w, mixed_rows(slab), *previous)

    def halve(value, exchange, bit):
        half = value.shape[0] // 2
        return value[:half].astype(F32) + exchange(value[half:], bit).astype(F32)

    def sum_all(values):
        values = [v.astype(F32) for v in values]
        while len(values) > 1:
            values = [values[i] + values[i + 1] for i in range(0, len(values), 2)]
        return values[0]

    def row_sum(value, bits):
        steps = [sum(b for k, b in enumerate(bits) if (q >> k) & 1) for q in range(1 << len(bits))]
        return sum_all([value] + [permute_row(value, step) for step in steps[1:]])

    col_bits, row_bits = list(reversed(bits_of(n_col))), list(reversed(bits_of(n_row)))
    some = tiles // 2
    e_part = halve(e_part, permute_row, 1).astype(BF16)
    gi = sum_all([gi[0]] + [permute_col(gi[q], q) for q in range(1, n_col)]).astype(BF16)
    h_low = h_part(0, half)
    e_part, gi, h_low, w, w_flip = lax.optimization_barrier((e_part, gi, h_low, w, w_flip))

    gi = row_sum(gi, row_bits[:1]).astype(BF16)
    h_low = halve(h_low, permute_col, 1).astype(BF16)
    h_high = h_part(half, tiles - half)
    e_part, gi, h_low, h_high, w = lax.optimization_barrier((e_part, gi, h_low, h_high, w))

    for bit in col_bits[1:]:
        e_part = halve(e_part, permute_row, bit).astype(BF16)
    h_high = halve(h_high, permute_col, 1).astype(BF16)
    gi = row_sum(gi, row_bits[1:2])
    for bit in col_bits[1:]:
        h_low = halve(h_low.astype(BF16), permute_col, bit)
    updated = update(0, some, [])
    e_part, gi, h_high, updated, w = lax.optimization_barrier((e_part, gi, h_high, updated, w))

    for bit in col_bits[1:]:
        h_high = halve(h_high.astype(BF16), permute_col, bit)
    e_own = sum_all([transpose(e_part[0, m], m, back=True) for m in range(groups)])
    for bit in row_bits[2:]:
        gi = row_sum(gi.astype(BF16), [bit])
    updated = update(some, tiles - some, [updated])
    h_low, h_high, e_own, gi, updated = lax.optimization_barrier((h_low, h_high, e_own, gi, updated))
    h = jnp.concatenate([h_low[0], h_high[0]], 0)
    grad_panel = jnp.concatenate([h[:slots] + e_own, h[slots:]], 0)
    updated = updated.reshape(tiles, tile, tile // LANES, slabs, LANES).transpose(0, 1, 3, 2, 4)
    return (
        updated.reshape(slab.shape),
        grad_panel.transpose(0, 2, 1).reshape(panel.shape),
        gi.T,
    )


def solution(mesh):
    in_specs = (
        P(None, "row", None, "col"),
        P(None, "row", None, None, "col", None),
        P(None, "row", None, None, "col", None),
        P(),
    )
    out_specs = (
        P(None, "row", None, None, "col", None),
        P(None, "row", None, "col"),
        P(None, "col"),
    )
    return jax.shard_map(
        per_device, mesh=mesh, in_specs=in_specs, out_specs=out_specs, check_vma=False
    )
```

```python
import functools

import jax
import jax.numpy as jnp
from jax import lax
from jax.experimental import pallas as pl
from jax.experimental.pallas import tpu as pltpu
from jax.sharding import PartitionSpec as P

BOTH = ("row", "col")
F32 = jnp.float32
BF16 = jnp.bfloat16
LANES = 128
VMEM = pl.BlockSpec(memory_space=pltpu.VMEM)
SMEM = pl.BlockSpec(memory_space=pltpu.SMEM)
STREAMED = 58
ANY = pl.BlockSpec(memory_space=pl.ANY)


def bits_of(count):
    return [1 << b for b in reversed(range(count.bit_length() - 1))]


def reversed_bits(value, count):
    width = count.bit_length() - 1
    place = 0
    for b in range(width):
        place = place + (((value >> b) & 1) << (width - 1 - b))
    return place


def dot(a, b, dims, precision=None):
    return lax.dot_general(a, b, (dims, ((), ())), precision=precision, preferred_element_type=F32)


def whole(shape):
    return pl.BlockSpec(shape, lambda *_: (0,) * len(shape))


def params(mib=24):
    return pltpu.CompilerParams(vmem_limit_bytes=mib * 2**20)


def cost(flops, nbytes):
    return pl.CostEstimate(flops=flops, bytes_accessed=nbytes, transcendentals=0)


def unmix_kernel(slabs, tile, x_ref, o_ref, token_ref, wide_ref, ins, outs, in_sems, out_sems):
    step, steps = pl.program_id(0), ins.shape[0]
    size = ins.shape[1]

    def copy_in(t):
        at = pl.multiple_of(t * size, size)
        return pltpu.make_async_copy(x_ref.at[pl.ds(at, size)], ins.at[t], in_sems.at[t])

    def copy_out(t):
        at = pl.multiple_of(t * tile, tile)
        return pltpu.make_async_copy(outs.at[t], o_ref.at[pl.ds(at, tile)], out_sems.at[t])

    @pl.when(step == 0)
    def _():
        for t in range(steps):
            copy_in(t).start()
        token_ref[...] = jnp.zeros_like(token_ref)

    copy_in(step).wait()
    halves = tile // LANES
    wide_ref[...] = ins[step].astype(F32)
    for s in range(slabs):
        for h in range(halves):
            part = wide_ref[pl.ds(h * slabs + s, tile, stride=halves * slabs), :]
            outs[step, :, s * tile + h * LANES : s * tile + (h + 1) * LANES] = part.astype(BF16)
    copy_out(step).start()

    @pl.when(step == steps - 1)
    def _():
        for t in range(steps):
            copy_out(t).wait()


def q_kernel(n_row, n_col, groups, place_ref, *refs):
    parts, (inv_ref, g_ref, q_ref, e_ref, pt_ref, m_ref, ins, sems) = refs[:n_col], refs[n_col:]
    tiles, strip, tile = parts[0].shape
    s = pl.program_id(0)
    row, col = place_ref[0], place_ref[1]
    group, rho = row // n_col, (row % n_col) ^ (n_col // 2)

    def copy_in(at):
        columns = pl.ds(pl.multiple_of(at * tile, tile), tile)
        return pltpu.make_async_copy(g_ref.at[:, columns], ins.at[at], sems.at[at])

    @pl.when(s == 0)
    def _():
        for at in range(ins.shape[0]):
            copy_in(at).start()
        mat = dot(inv_ref[...], inv_ref[...], ((0,), (0,)), lax.Precision.HIGHEST)
        high = mat.astype(BF16)
        m_ref[0] = high
        m_ref[1] = (mat - high.astype(F32)).astype(BF16)
        for q in range(n_col):
            at = pl.multiple_of((col ^ q) * strip, strip)
            for t in range(tiles):
                pt_ref[pl.ds(at, strip), t * tile : (t + 1) * tile] = parts[q][t]

    copy_in(s).wait()
    q_ref[s] = dot(pt_ref[...], ins[s], ((1,), (0,))).astype(BF16)

    @pl.when(s == pl.num_programs(0) - 1)
    def _():
        for at in range(q_ref.shape[0]):
            q_val = q_ref[at]
            e_val = -(dot(m_ref[0], q_val, ((1,), (0,))) + dot(m_ref[1], q_val, ((1,), (0,))))
            e_val = e_val.astype(BF16)
            slot, other = at // groups, group ^ (at % groups)
            for r in range(n_col):
                e_ref[reversed_bits(rho ^ r, n_col), other, slot] = e_val[r * strip : (r + 1) * strip]


def w_kernel(n_row, n_col, groups, place_ref, *refs):
    tops, (m_ref, inv_ref, q_ref, _, w_ref, wt_ref, gi_ref, top_all) = refs[:n_col], refs[n_col:]
    slots, strip, tile = tops[0].shape[1:]
    slabs = slots * groups
    row, col = place_ref[0], place_ref[1]
    group, rho = row // n_col, (row % n_col) ^ (n_col // 2)
    for p in range(n_row):
        at = pl.multiple_of((rho ^ (p % n_col)) * strip, strip)
        for slot in range(slots):
            s = slot * groups + (group ^ (p // n_col))
            top_all[s, pl.ds(at, strip), :] = tops[p % n_col][p // n_col, slot]
    z = jnp.zeros((tile, tile), F32)
    for s in range(slabs):
        top = top_all[s]
        w = dot(m_ref[0], top, ((1,), (0,))) + dot(m_ref[1], top, ((1,), (0,)))
        w = w.astype(BF16)
        w_ref[:, s * tile : (s + 1) * tile] = w
        wt_ref[s * tile : (s + 1) * tile, :] = w.T
        z = z + dot(top, q_ref[s], ((1,), (1,)))
    z = z + z.T
    gi = -dot(z, inv_ref[...], ((1,), (1,)), lax.Precision.HIGHEST)
    for r in range(n_col):
        gi_ref[col ^ r] = gi[r * strip : (r + 1) * strip].astype(BF16)


def h_kernel(n_col, place_ref, wt_ref, g_ref, h_ref):
    strip = h_ref.shape[2]
    t = pl.program_id(0)
    col = place_ref[1]
    tile = h_ref.shape[3]
    pair = -dot(g_ref[...], wt_ref[...], ((1,), (0,)))
    pair = pair.astype(BF16)
    for k in range(2):
        h = pair[k * tile : (k + 1) * tile].T
        for r in range(n_col):
            h_ref[reversed_bits(col ^ r, n_col), 2 * t + k] = h[r * strip : (r + 1) * strip]


def update_kernel(slabs, tile, pt_ref, w_ref, x_ref, *refs):
    o_ref, wide_ref = refs[-2:]
    halves = tile // LANES
    product = dot(pt_ref[...], w_ref[...], ((0,), (0,)))
    for s in range(slabs):
        for h in range(halves):
            part = product[:, s * tile + h * LANES : s * tile + (h + 1) * LANES]
            wide_ref[pl.ds(h * slabs + s, tile, stride=halves * slabs), :] = part
    o_ref[...] = (x_ref[...].astype(F32) - wide_ref[...]).astype(BF16)


def mixed_rows(x):
    tiles, _, tile, slabs, _, _ = x.shape
    x = x.reshape(tiles, tile, slabs, tile // LANES, LANES).transpose(0, 1, 3, 2, 4)
    return x.reshape(-1, LANES)


def per_device(panel, slab, cotangent, inverse):
    tiles, _, tile, strip = panel.shape
    slabs = slab.shape[3]
    n_row = lax.axis_size("row")
    n_col = lax.axis_size("col")
    groups = n_row // n_col
    slots = slabs // groups
    width = slabs * tile
    rows = tiles * tile
    mixed = tile * width // LANES
    place = jnp.stack([lax.axis_index("row"), lax.axis_index("col")]).astype(jnp.int32)

    def permute_row(value, bit):
        return lax.ppermute(value, "row", [(i, i ^ bit) for i in range(n_row)])

    def permute_col(value, bit):
        return lax.ppermute(value, "col", [(i, i ^ bit) for i in range(n_col)])

    far = n_col // 2

    def transpose(value, across, back=False):
        pairs = []
        for m in range(groups):
            for a in range(n_col):
                for b in range(n_col):
                    here = (m * n_col + a) * n_col + b
                    there = ((m ^ across) * n_col + (b ^ far)) * n_col + a
                    pairs.append((there, here) if back else (here, there))
        return lax.ppermute(value, BOTH, pairs)

    own = panel.reshape(tiles, tile, strip).transpose(0, 2, 1).astype(BF16)
    high, *lower = bits_of(n_col)
    half = tiles // 2
    tops = [transpose(own[:slots], m) for m in range(groups)]
    parts = {0: own, high: permute_col(own, high)}
    cot, token = pl.pallas_call(
        functools.partial(unmix_kernel, slabs, tile),
        grid=(tiles,),
        in_specs=[ANY],
        out_specs=[ANY, whole((8, LANES))],
        out_shape=[
            jax.ShapeDtypeStruct((rows, width), BF16),
            jax.ShapeDtypeStruct((8, LANES), F32),
        ],
        scratch_shapes=[
            pltpu.VMEM((mixed, LANES), F32),
            pltpu.VMEM((tiles, mixed, LANES), BF16),
            pltpu.VMEM((tiles, tile, width), BF16),
            pltpu.SemaphoreType.DMA((tiles,)),
            pltpu.SemaphoreType.DMA((tiles,)),
        ],
        compiler_params=params(STREAMED),
        cost_estimate=cost(0, 4 * rows * width),
    )(mixed_rows(cotangent))

    tops, own, token = lax.optimization_barrier((tops, own, token))

    if lower:
        parts[1] = permute_col(own, 1)

    top = jnp.stack(tops)
    tops = [top] + [permute_row(top, q) for q in range(1, n_col)]
    parts, token = lax.optimization_barrier((parts, token))
    for bit in lower:
        for q in range(0, n_col, 2 * bit):
            if q | bit not in parts:
                parts[q | bit] = permute_col(parts[q], bit)

    q_sum, e_part, panel_all, mat = pl.pallas_call(
        functools.partial(q_kernel, n_row, n_col, groups),
        grid=(slabs,),
        in_specs=[SMEM]
        + [whole((tiles, strip, tile))] * n_col
        + [whole((tile, tile)), ANY],
        out_specs=[
            whole((slabs, tile, tile)),
            whole((n_col, groups, slots, strip, tile)),
            whole((tile, rows)),
            whole((2, tile, tile)),
        ],
        out_shape=[
            jax.ShapeDtypeStruct((slabs, tile, tile), BF16),
            jax.ShapeDtypeStruct((n_col, groups, slots, strip, tile), BF16),
            jax.ShapeDtypeStruct((tile, rows), BF16),
            jax.ShapeDtypeStruct((2, tile, tile), BF16),
        ],
        scratch_shapes=[
            pltpu.VMEM((slabs, rows, tile), BF16),
            pltpu.SemaphoreType.DMA((slabs,)),
        ],
        compiler_params=params(STREAMED - 10),
        cost_estimate=cost(2 * rows * width * tile, 2 * rows * (width + tile)),
    )(place, *[parts[q] for q in range(n_col)], inverse, cot)

    w, w_flip, gi = pl.pallas_call(
        functools.partial(w_kernel, n_row, n_col, groups),
        in_specs=[SMEM] + [VMEM] * (n_col + 3) + [ANY],
        out_specs=[VMEM, VMEM, VMEM],
        out_shape=[
            jax.ShapeDtypeStruct((tile, width), BF16),
            jax.ShapeDtypeStruct((width, tile), BF16),
            jax.ShapeDtypeStruct((n_col, strip, tile), BF16),
        ],
        scratch_shapes=[pltpu.VMEM((slabs, tile, tile), BF16)],
        compiler_params=params(),
        cost_estimate=cost(tile, tile),
    )(place, *tops, mat, inverse, q_sum, token)

    def h_part(first, count):
        return pl.pallas_call(
            functools.partial(h_kernel, n_col),
            grid=(count // 2,),
            in_specs=[
                SMEM,
                whole((width, tile)),
                pl.BlockSpec((2 * tile, width), lambda t: (t + first // 2, 0)),
            ],
            out_specs=whole((n_col, count, strip, tile)),
            out_shape=jax.ShapeDtypeStruct((n_col, count, strip, tile), BF16),
            compiler_params=params(),
            cost_estimate=cost(tile, tile),
        )(place, w_flip, cot)

    def update(first, count, previous):
        return pl.pallas_call(
            functools.partial(update_kernel, slabs, tile),
            grid=(count,),
            in_specs=[
                pl.BlockSpec((tile, tile), lambda t: (0, t + first)),
                whole((tile, width)),
                pl.BlockSpec((mixed, LANES), lambda t: (t + first, 0)),
            ]
            + [ANY] * len(previous),
            out_specs=pl.BlockSpec((mixed, LANES), lambda t: (t + first, 0)),
            out_shape=jax.ShapeDtypeStruct((tiles * mixed, LANES), BF16),
            scratch_shapes=[pltpu.VMEM((mixed, LANES), F32)],
            input_output_aliases={3: 0} if previous else {},
            compiler_params=params(),
            cost_estimate=cost(2 * count * tile * width * tile, 4 * count * tile * width),
        )(panel_all, w, mixed_rows(slab), *previous)

    def halve(value, exchange, bit):
        half = value.shape[0] // 2
        return value[:half].astype(F32) + exchange(value[half:], bit).astype(F32)

    def sum_all(values):
        values = [v.astype(F32) for v in values]
        while len(values) > 1:
            values = [values[i] + values[i + 1] for i in range(0, len(values), 2)]
        return values[0]

    def row_sum(value, bits):
        steps = [sum(b for k, b in enumerate(bits) if (q >> k) & 1) for q in range(1 << len(bits))]
        return sum_all([value] + [permute_row(value, step) for step in steps[1:]])

    col_bits, row_bits = list(reversed(bits_of(n_col))), list(reversed(bits_of(n_row)))
    some = tiles // 2
    e_part = halve(e_part, permute_row, 1).astype(BF16)
    gi = sum_all([gi[0]] + [permute_col(gi[q], q) for q in range(1, n_col)]).astype(BF16)
    h_low = h_part(0, half)
    e_part, gi, h_low, w, w_flip = lax.optimization_barrier((e_part, gi, h_low, w, w_flip))

    gi = row_sum(gi, row_bits[:1]).astype(BF16)
    h_low = halve(h_low, permute_col, 1).astype(BF16)
    h_high = h_part(half, tiles - half)
    e_part, gi, h_low, h_high, w = lax.optimization_barrier((e_part, gi, h_low, h_high, w))

    for bit in col_bits[1:]:
        e_part = halve(e_part, permute_row, bit).astype(BF16)
    h_high = halve(h_high, permute_col, 1).astype(BF16)
    gi = row_sum(gi, row_bits[1:2])
    for bit in col_bits[1:]:
        h_low = halve(h_low.astype(BF16), permute_col, bit)
    updated = update(0, some, [])
    e_part, gi, h_high, updated, w = lax.optimization_barrier((e_part, gi, h_high, updated, w))

    for bit in col_bits[1:]:
        h_high = halve(h_high.astype(BF16), permute_col, bit)
    e_own = sum_all([transpose(e_part[0, m], m, back=True) for m in range(groups)])
    for bit in row_bits[2:]:
        gi = row_sum(gi.astype(BF16), [bit])
    updated = update(some, tiles - some, [updated])
    h_low, h_high, e_own, gi, updated = lax.optimization_barrier((h_low, h_high, e_own, gi, updated))
    h = jnp.concatenate([h_low[0], h_high[0]], 0)
    grad_panel = jnp.concatenate([h[:slots] + e_own, h[slots:]], 0)
    updated = updated.reshape(tiles, tile, tile // LANES, slabs, LANES).transpose(0, 1, 3, 2, 4)
    return (
        updated.reshape(slab.shape),
        grad_panel.transpose(0, 2, 1).reshape(panel.shape),
        gi.T,
    )


def solution(mesh):
    in_specs = (
        P(None, "row", None, "col"),
        P(None, "row", None, None, "col", None),
        P(None, "row", None, None, "col", None),
        P(),
    )
    out_specs = (
        P(None, "row", None, None, "col", None),
        P(None, "row", None, "col"),
        P(None, "col"),
    )
    return jax.shard_map(
        per_device, mesh=mesh, in_specs=in_specs, out_specs=out_specs, check_vma=False
    )
```

```python
import functools

import jax
import jax.numpy as jnp
from jax import lax
from jax.experimental import pallas as pl
from jax.experimental.pallas import tpu as pltpu
from jax.sharding import PartitionSpec as P

BOTH = ("row", "col")
F32 = jnp.float32
BF16 = jnp.bfloat16
LANES = 128
VMEM = pl.BlockSpec(memory_space=pltpu.VMEM)
SMEM = pl.BlockSpec(memory_space=pltpu.SMEM)
STREAMED = 58
ANY = pl.BlockSpec(memory_space=pl.ANY)


def bits_of(count):
    return [1 << b for b in reversed(range(count.bit_length() - 1))]


def reversed_bits(value, count):
    width = count.bit_length() - 1
    place = 0
    for b in range(width):
        place = place + (((value >> b) & 1) << (width - 1 - b))
    return place


def dot(a, b, dims, precision=None):
    return lax.dot_general(a, b, (dims, ((), ())), precision=precision, preferred_element_type=F32)


def whole(shape):
    return pl.BlockSpec(shape, lambda *_: (0,) * len(shape))


def params(mib=24):
    return pltpu.CompilerParams(vmem_limit_bytes=mib * 2**20)


def cost(flops, nbytes):
    return pl.CostEstimate(flops=flops, bytes_accessed=nbytes, transcendentals=0)


def unmix_kernel(slabs, tile, x_ref, o_ref, token_ref, wide_ref, ins, outs, in_sems, out_sems):
    step, steps = pl.program_id(0), ins.shape[0]
    size = ins.shape[1]

    def copy_in(t):
        at = pl.multiple_of(t * size, size)
        return pltpu.make_async_copy(x_ref.at[pl.ds(at, size)], ins.at[t], in_sems.at[t])

    def copy_out(t):
        at = pl.multiple_of(t * tile, tile)
        return pltpu.make_async_copy(outs.at[t], o_ref.at[pl.ds(at, tile)], out_sems.at[t])

    @pl.when(step == 0)
    def _():
        for t in range(steps):
            copy_in(t).start()
        token_ref[...] = jnp.zeros_like(token_ref)

    copy_in(step).wait()
    halves = tile // LANES
    wide_ref[...] = ins[step].astype(F32)
    for s in range(slabs):
        for h in range(halves):
            part = wide_ref[pl.ds(h * slabs + s, tile, stride=halves * slabs), :]
            outs[step, :, s * tile + h * LANES : s * tile + (h + 1) * LANES] = part.astype(BF16)
    copy_out(step).start()

    @pl.when(step == steps - 1)
    def _():
        for t in range(steps):
            copy_out(t).wait()


def q_kernel(n_row, n_col, groups, place_ref, *refs):
    parts, (inv_ref, g_ref, q_ref, e_ref, pt_ref, m_ref, ins, sems) = refs[:n_col], refs[n_col:]
    tiles, strip, tile = parts[0].shape
    s = pl.program_id(0)
    row, col = place_ref[0], place_ref[1]
    group, rho = row // n_col, (row % n_col) ^ (n_col // 2)

    def copy_in(at):
        columns = pl.ds(pl.multiple_of(at * tile, tile), tile)
        return pltpu.make_async_copy(g_ref.at[:, columns], ins.at[at], sems.at[at])

    @pl.when(s == 0)
    def _():
        for at in range(ins.shape[0]):
            copy_in(at).start()
        mat = dot(inv_ref[...], inv_ref[...], ((0,), (0,)), lax.Precision.HIGHEST)
        high = mat.astype(BF16)
        m_ref[0] = high
        m_ref[1] = (mat - high.astype(F32)).astype(BF16)
        for q in range(n_col):
            at = pl.multiple_of((col ^ q) * strip, strip)
            for t in range(tiles):
                pt_ref[pl.ds(at, strip), t * tile : (t + 1) * tile] = parts[q][t]

    copy_in(s).wait()
    q_ref[:, pl.ds(pl.multiple_of(s * tile, tile), tile)] = dot(pt_ref[...], ins[s], ((1,), (0,))).astype(BF16)

    @pl.when(s == pl.num_programs(0) - 1)
    def _():
        q_val = q_ref[...]
        e_val = -(dot(m_ref[0], q_val, ((1,), (0,))) + dot(m_ref[1], q_val, ((1,), (0,))))
        e_val = e_val.astype(BF16)
        for at in range(ins.shape[0]):
            slot, other = at // groups, group ^ (at % groups)
            for r in range(n_col):
                piece = e_val[r * strip : (r + 1) * strip, at * tile : (at + 1) * tile]
                e_ref[reversed_bits(rho ^ r, n_col), other, slot] = piece


def w_kernel(n_row, n_col, groups, place_ref, *refs):
    tops, (m_ref, inv_ref, q_ref, _, w_ref, wt_ref, gi_ref, top_all) = refs[:n_col], refs[n_col:]
    slots, strip, tile = tops[0].shape[1:]
    slabs = slots * groups
    row, col = place_ref[0], place_ref[1]
    group, rho = row // n_col, (row % n_col) ^ (n_col // 2)
    for p in range(n_row):
        at = pl.multiple_of((rho ^ (p % n_col)) * strip, strip)
        for slot in range(slots):
            s = slot * groups + (group ^ (p // n_col))
            columns = pl.ds(pl.multiple_of(s * tile, tile), tile)
            top_all[pl.ds(at, strip), columns] = tops[p % n_col][p // n_col, slot]
    top = top_all[...]
    w = dot(m_ref[0], top, ((1,), (0,))) + dot(m_ref[1], top, ((1,), (0,)))
    w_ref[...] = w.astype(BF16)
    for s in range(slabs):
        wt_ref[s * tile : (s + 1) * tile, :] = w_ref[:, s * tile : (s + 1) * tile].T
    z = dot(top, q_ref[...], ((1,), (1,)))
    z = z + z.T
    gi = -dot(z, inv_ref[...], ((1,), (1,)), lax.Precision.HIGHEST)
    for r in range(n_col):
        gi_ref[col ^ r] = gi[r * strip : (r + 1) * strip].astype(BF16)


def h_kernel(n_col, place_ref, wt_ref, g_ref, h_ref):
    strip = h_ref.shape[2]
    t = pl.program_id(0)
    col = place_ref[1]
    tile = h_ref.shape[3]
    pair = -dot(g_ref[...], wt_ref[...], ((1,), (0,)))
    pair = pair.astype(BF16)
    for k in range(2):
        h = pair[k * tile : (k + 1) * tile].T
        for r in range(n_col):
            h_ref[reversed_bits(col ^ r, n_col), 2 * t + k] = h[r * strip : (r + 1) * strip]


def update_kernel(slabs, tile, pt_ref, w_ref, x_ref, *refs):
    o_ref, wide_ref = refs[-2:]
    halves = tile // LANES
    for k in range(2):
        product = dot(pt_ref[:, k * tile : (k + 1) * tile], w_ref[...], ((0,), (0,)))
        for s in range(slabs):
            for h in range(halves):
                part = product[:, s * tile + h * LANES : s * tile + (h + 1) * LANES]
                at = (k * tile * halves + h) * slabs + s
                wide_ref[pl.ds(at, tile, stride=halves * slabs), :] = part
    o_ref[...] = (x_ref[...].astype(F32) - wide_ref[...]).astype(BF16)


def mixed_rows(x):
    tiles, _, tile, slabs, _, _ = x.shape
    x = x.reshape(tiles, tile, slabs, tile // LANES, LANES).transpose(0, 1, 3, 2, 4)
    return x.reshape(-1, LANES)


def per_device(panel, slab, cotangent, inverse):
    tiles, _, tile, strip = panel.shape
    slabs = slab.shape[3]
    n_row = lax.axis_size("row")
    n_col = lax.axis_size("col")
    groups = n_row // n_col
    slots = slabs // groups
    width = slabs * tile
    rows = tiles * tile
    mixed = tile * width // LANES
    place = jnp.stack([lax.axis_index("row"), lax.axis_index("col")]).astype(jnp.int32)

    def permute_row(value, bit):
        return lax.ppermute(value, "row", [(i, i ^ bit) for i in range(n_row)])

    def permute_col(value, bit):
        return lax.ppermute(value, "col", [(i, i ^ bit) for i in range(n_col)])

    far = n_col // 2

    def transpose(value, across, back=False):
        pairs = []
        for m in range(groups):
            for a in range(n_col):
                for b in range(n_col):
                    here = (m * n_col + a) * n_col + b
                    there = ((m ^ across) * n_col + (b ^ far)) * n_col + a
                    pairs.append((there, here) if back else (here, there))
        return lax.ppermute(value, BOTH, pairs)

    own = panel.reshape(tiles, tile, strip).transpose(0, 2, 1).astype(BF16)
    high, *lower = bits_of(n_col)
    half = tiles // 2
    tops = [transpose(own[:slots], m) for m in range(groups)]
    parts = {0: own, high: permute_col(own, high)}
    if lower:
        parts[1] = permute_col(own, 1)
    cot, token = pl.pallas_call(
        functools.partial(unmix_kernel, slabs, tile),
        grid=(tiles,),
        in_specs=[ANY],
        out_specs=[ANY, whole((8, LANES))],
        out_shape=[
            jax.ShapeDtypeStruct((rows, width), BF16),
            jax.ShapeDtypeStruct((8, LANES), F32),
        ],
        scratch_shapes=[
            pltpu.VMEM((mixed, LANES), F32),
            pltpu.VMEM((tiles, mixed, LANES), BF16),
            pltpu.VMEM((tiles, tile, width), BF16),
            pltpu.SemaphoreType.DMA((tiles,)),
            pltpu.SemaphoreType.DMA((tiles,)),
        ],
        compiler_params=params(STREAMED),
        cost_estimate=cost(0, 4 * rows * width),
    )(mixed_rows(cotangent))

    tops, parts, token = lax.optimization_barrier((tops, parts, token))


    top = jnp.stack(tops)
    tops = [top] + [permute_row(top, q) for q in range(1, n_col)]
    for bit in lower:
        for q in range(0, n_col, 2 * bit):
            if q | bit not in parts:
                parts[q | bit] = permute_col(parts[q], bit)

    q_sum, e_part, panel_all, mat = pl.pallas_call(
        functools.partial(q_kernel, n_row, n_col, groups),
        grid=(slabs,),
        in_specs=[SMEM]
        + [whole((tiles, strip, tile))] * n_col
        + [whole((tile, tile)), ANY],
        out_specs=[
            whole((tile, width)),
            whole((n_col, groups, slots, strip, tile)),
            whole((tile, rows)),
            whole((2, tile, tile)),
        ],
        out_shape=[
            jax.ShapeDtypeStruct((tile, width), BF16),
            jax.ShapeDtypeStruct((n_col, groups, slots, strip, tile), BF16),
            jax.ShapeDtypeStruct((tile, rows), BF16),
            jax.ShapeDtypeStruct((2, tile, tile), BF16),
        ],
        scratch_shapes=[
            pltpu.VMEM((slabs, rows, tile), BF16),
            pltpu.SemaphoreType.DMA((slabs,)),
        ],
        compiler_params=params(STREAMED - 10),
        cost_estimate=cost(2 * rows * width * tile, 2 * rows * (width + tile)),
    )(place, *[parts[q] for q in range(n_col)], inverse, cot)

    w, w_flip, gi = pl.pallas_call(
        functools.partial(w_kernel, n_row, n_col, groups),
        in_specs=[SMEM] + [VMEM] * (n_col + 3) + [ANY],
        out_specs=[VMEM, VMEM, VMEM],
        out_shape=[
            jax.ShapeDtypeStruct((tile, width), BF16),
            jax.ShapeDtypeStruct((width, tile), BF16),
            jax.ShapeDtypeStruct((n_col, strip, tile), BF16),
        ],
        scratch_shapes=[pltpu.VMEM((tile, width), BF16)],
        compiler_params=params(),
        cost_estimate=cost(tile, tile),
    )(place, *tops, mat, inverse, q_sum, token)

    def h_part(first, count):
        return pl.pallas_call(
            functools.partial(h_kernel, n_col),
            grid=(count // 2,),
            in_specs=[
                SMEM,
                whole((width, tile)),
                pl.BlockSpec((2 * tile, width), lambda t: (t + first // 2, 0)),
            ],
            out_specs=whole((n_col, count, strip, tile)),
            out_shape=jax.ShapeDtypeStruct((n_col, count, strip, tile), BF16),
            compiler_params=params(),
            cost_estimate=cost(tile, tile),
        )(place, w_flip, cot)

    def update(first, count, previous):
        return pl.pallas_call(
            functools.partial(update_kernel, slabs, tile),
            grid=(count // 2,),
            in_specs=[
                pl.BlockSpec((tile, 2 * tile), lambda t: (0, t + first // 2)),
                whole((tile, width)),
                pl.BlockSpec((2 * mixed, LANES), lambda t: (t + first // 2, 0)),
            ]
            + [ANY] * len(previous),
            out_specs=pl.BlockSpec((2 * mixed, LANES), lambda t: (t + first // 2, 0)),
            out_shape=jax.ShapeDtypeStruct((tiles * mixed, LANES), BF16),
            scratch_shapes=[pltpu.VMEM((2 * mixed, LANES), F32)],
            input_output_aliases={3: 0} if previous else {},
            compiler_params=params(),
            cost_estimate=cost(2 * count * tile * width * tile, 4 * count * tile * width),
        )(panel_all, w, mixed_rows(slab), *previous)

    def halve(value, exchange, bit):
        half = value.shape[0] // 2
        return value[:half].astype(F32) + exchange(value[half:], bit).astype(F32)

    def sum_all(values):
        values = [v.astype(F32) for v in values]
        while len(values) > 1:
            values = [values[i] + values[i + 1] for i in range(0, len(values), 2)]
        return values[0]

    def row_sum(value, bits):
        steps = [sum(b for k, b in enumerate(bits) if (q >> k) & 1) for q in range(1 << len(bits))]
        return sum_all([value] + [permute_row(value, step) for step in steps[1:]])

    def halve_both(value, extra, bit):
        half = value.shape[0] // 2
        sent = jnp.concatenate([value[half:].reshape(-1, strip, tile), extra[None]], 0)
        got = permute_row(sent, bit)
        value = value[:half].astype(F32) + got[:-1].reshape(value[:half].shape).astype(F32)
        return value.astype(BF16), sum_all([extra, got[-1]])

    col_bits, row_bits = list(reversed(bits_of(n_col))), list(reversed(bits_of(n_row)))
    some = tiles // 2
    e_part = halve(e_part, permute_row, 1).astype(BF16)
    gi = sum_all([gi[0]] + [permute_col(gi[q], q) for q in range(1, n_col)]).astype(BF16)
    h_low = h_part(0, half)
    e_part, gi, h_low, w, w_flip = lax.optimization_barrier((e_part, gi, h_low, w, w_flip))

    gi = row_sum(gi, row_bits[:1]).astype(BF16)
    h_low = halve(h_low, permute_col, 1).astype(BF16)
    h_high = h_part(half, tiles - half)
    e_part, gi, h_low, h_high, w = lax.optimization_barrier((e_part, gi, h_low, h_high, w))

    for bit in col_bits[1:]:
        e_part, gi = halve_both(e_part, gi.astype(BF16), bit)
    h_high = halve(h_high, permute_col, 1).astype(BF16)
    for bit in col_bits[1:]:
        h_low = halve(h_low.astype(BF16), permute_col, bit)
    updated = update(0, some, [])
    e_part, gi, h_high, updated, w = lax.optimization_barrier((e_part, gi, h_high, updated, w))

    for bit in col_bits[1:]:
        h_high = halve(h_high.astype(BF16), permute_col, bit)
    e_own = sum_all([transpose(e_part[0, m], m, back=True) for m in range(groups)])
    for bit in row_bits[len(col_bits) :]:
        gi = row_sum(gi.astype(BF16), [bit])
    updated = update(some, tiles - some, [updated])
    h_low, h_high, e_own, gi, updated = lax.optimization_barrier((h_low, h_high, e_own, gi, updated))
    h = jnp.concatenate([h_low[0], h_high[0]], 0)
    grad_panel = jnp.concatenate([h[:slots] + e_own, h[slots:]], 0)
    updated = updated.reshape(tiles, tile, tile // LANES, slabs, LANES).transpose(0, 1, 3, 2, 4)
    return (
        updated.reshape(slab.shape),
        grad_panel.transpose(0, 2, 1).reshape(panel.shape),
        gi.T,
    )


def solution(mesh):
    in_specs = (
        P(None, "row", None, "col"),
        P(None, "row", None, None, "col", None),
        P(None, "row", None, None, "col", None),
        P(),
    )
    out_specs = (
        P(None, "row", None, None, "col", None),
        P(None, "row", None, "col"),
        P(None, "col"),
    )
    return jax.shard_map(
        per_device, mesh=mesh, in_specs=in_specs, out_specs=out_specs, check_vma=False
    )
```

```python
import functools

import jax
import jax.numpy as jnp
from jax import lax
from jax.experimental import pallas as pl
from jax.experimental.pallas import tpu as pltpu
from jax.sharding import PartitionSpec as P

BOTH = ("row", "col")
F32 = jnp.float32
BF16 = jnp.bfloat16
LANES = 128
VMEM = pl.BlockSpec(memory_space=pltpu.VMEM)
SMEM = pl.BlockSpec(memory_space=pltpu.SMEM)
STREAMED = 58
ANY = pl.BlockSpec(memory_space=pl.ANY)


def bits_of(count):
    return [1 << b for b in reversed(range(count.bit_length() - 1))]


def reversed_bits(value, count):
    width = count.bit_length() - 1
    place = 0
    for b in range(width):
        place = place + (((value >> b) & 1) << (width - 1 - b))
    return place


def dot(a, b, dims, precision=None):
    return lax.dot_general(a, b, (dims, ((), ())), precision=precision, preferred_element_type=F32)


def whole(shape):
    return pl.BlockSpec(shape, lambda *_: (0,) * len(shape))


def params(mib=24):
    return pltpu.CompilerParams(vmem_limit_bytes=mib * 2**20)


def cost(flops, nbytes):
    return pl.CostEstimate(flops=flops, bytes_accessed=nbytes, transcendentals=0)


def unmix_kernel(slabs, tile, x_ref, o_ref, token_ref, wide_ref, ins, outs, in_sems, out_sems):
    step, steps = pl.program_id(0), ins.shape[0]
    size = ins.shape[1]

    def copy_in(t):
        at = pl.multiple_of(t * size, size)
        return pltpu.make_async_copy(x_ref.at[pl.ds(at, size)], ins.at[t], in_sems.at[t])

    def copy_out(t):
        at = pl.multiple_of(t * tile, tile)
        return pltpu.make_async_copy(outs.at[t], o_ref.at[pl.ds(at, tile)], out_sems.at[t])

    @pl.when(step == 0)
    def _():
        for t in range(steps):
            copy_in(t).start()
        token_ref[...] = jnp.zeros_like(token_ref)

    copy_in(step).wait()
    halves = tile // LANES
    wide_ref[...] = ins[step].astype(F32)
    for s in range(slabs):
        for h in range(halves):
            part = wide_ref[pl.ds(h * slabs + s, tile, stride=halves * slabs), :]
            outs[step, :, s * tile + h * LANES : s * tile + (h + 1) * LANES] = part.astype(BF16)
    copy_out(step).start()

    @pl.when(step == steps - 1)
    def _():
        for t in range(steps):
            copy_out(t).wait()


def q_kernel(n_row, n_col, groups, place_ref, *refs):
    parts, (inv_ref, g_ref, q_ref, e_ref, pt_ref, m_ref, ins, sems) = refs[:n_col], refs[n_col:]
    tiles, strip, tile = parts[0].shape
    s = pl.program_id(0)
    row, col = place_ref[0], place_ref[1]
    group, rho = row // n_col, (row % n_col) ^ (n_col // 2)

    def copy_in(at):
        columns = pl.ds(pl.multiple_of(at * tile, tile), tile)
        return pltpu.make_async_copy(g_ref.at[:, columns], ins.at[at], sems.at[at])

    @pl.when(s == 0)
    def _():
        for at in range(ins.shape[0]):
            copy_in(at).start()
        mat = dot(inv_ref[...], inv_ref[...], ((0,), (0,)), lax.Precision.HIGHEST)
        high = mat.astype(BF16)
        m_ref[0] = high
        m_ref[1] = (mat - high.astype(F32)).astype(BF16)
        for q in range(n_col):
            at = pl.multiple_of((col ^ q) * strip, strip)
            for t in range(tiles):
                pt_ref[pl.ds(at, strip), t * tile : (t + 1) * tile] = parts[q][t]

    copy_in(s).wait()
    q_ref[s] = dot(pt_ref[...], ins[s], ((1,), (0,))).astype(BF16)

    @pl.when(s == pl.num_programs(0) - 1)
    def _():
        for at in range(q_ref.shape[0]):
            q_val = q_ref[at]
            e_val = -(dot(m_ref[0], q_val, ((1,), (0,))) + dot(m_ref[1], q_val, ((1,), (0,))))
            e_val = e_val.astype(BF16)
            slot, other = at // groups, group ^ (at % groups)
            for r in range(n_col):
                e_ref[reversed_bits(rho ^ r, n_col), other, slot] = e_val[r * strip : (r + 1) * strip]


def w_kernel(n_row, n_col, groups, place_ref, *refs):
    tops, (m_ref, inv_ref, q_ref, _, w_ref, wt_ref, gi_ref, top_all) = refs[:n_col], refs[n_col:]
    slots, strip, tile = tops[0].shape[1:]
    slabs = slots * groups
    row, col = place_ref[0], place_ref[1]
    group, rho = row // n_col, (row % n_col) ^ (n_col // 2)
    for p in range(n_row):
        at = pl.multiple_of((rho ^ (p % n_col)) * strip, strip)
        for slot in range(slots):
            s = slot * groups + (group ^ (p // n_col))
            top_all[s, pl.ds(at, strip), :] = tops[p % n_col][p // n_col, slot]
    z = jnp.zeros((tile, tile), F32)
    for s in range(slabs):
        top = top_all[s]
        w = dot(m_ref[0], top, ((1,), (0,))) + dot(m_ref[1], top, ((1,), (0,)))
        w = w.astype(BF16)
        w_ref[:, s * tile : (s + 1) * tile] = w
        wt_ref[s * tile : (s + 1) * tile, :] = w.T
        z = z + dot(top, q_ref[s], ((1,), (1,)))
    z = z + z.T
    gi = -dot(z, inv_ref[...], ((1,), (1,)), lax.Precision.HIGHEST)
    for r in range(n_col):
        gi_ref[col ^ r] = gi[r * strip : (r + 1) * strip].astype(BF16)


def h_kernel(n_col, place_ref, wt_ref, g_ref, h_ref):
    strip = h_ref.shape[2]
    t = pl.program_id(0)
    col = place_ref[1]
    tile = h_ref.shape[3]
    pair = -dot(g_ref[...], wt_ref[...], ((1,), (0,)))
    pair = pair.astype(BF16)
    for k in range(2):
        h = pair[k * tile : (k + 1) * tile].T
        for r in range(n_col):
            h_ref[reversed_bits(col ^ r, n_col), 2 * t + k] = h[r * strip : (r + 1) * strip]


def update_kernel(slabs, tile, pt_ref, w_ref, x_ref, *refs):
    o_ref, wide_ref = refs[-2:]
    halves = tile // LANES
    for k in range(2):
        product = dot(pt_ref[:, k * tile : (k + 1) * tile], w_ref[...], ((0,), (0,)))
        for s in range(slabs):
            for h in range(halves):
                part = product[:, s * tile + h * LANES : s * tile + (h + 1) * LANES]
                at = (k * tile * halves + h) * slabs + s
                wide_ref[pl.ds(at, tile, stride=halves * slabs), :] = part
    o_ref[...] = (x_ref[...].astype(F32) - wide_ref[...]).astype(BF16)


def mixed_rows(x):
    tiles, _, tile, slabs, _, _ = x.shape
    x = x.reshape(tiles, tile, slabs, tile // LANES, LANES).transpose(0, 1, 3, 2, 4)
    return x.reshape(-1, LANES)


def per_device(panel, slab, cotangent, inverse):
    tiles, _, tile, strip = panel.shape
    slabs = slab.shape[3]
    n_row = lax.axis_size("row")
    n_col = lax.axis_size("col")
    groups = n_row // n_col
    slots = slabs // groups
    width = slabs * tile
    rows = tiles * tile
    mixed = tile * width // LANES
    place = jnp.stack([lax.axis_index("row"), lax.axis_index("col")]).astype(jnp.int32)

    def permute_row(value, bit):
        return lax.ppermute(value, "row", [(i, i ^ bit) for i in range(n_row)])

    def permute_col(value, bit):
        return lax.ppermute(value, "col", [(i, i ^ bit) for i in range(n_col)])

    far = n_col // 2

    def transpose(value, across, back=False):
        pairs = []
        for m in range(groups):
            for a in range(n_col):
                for b in range(n_col):
                    here = (m * n_col + a) * n_col + b
                    there = ((m ^ across) * n_col + (b ^ far)) * n_col + a
                    pairs.append((there, here) if back else (here, there))
        return lax.ppermute(value, BOTH, pairs)

    own = panel.reshape(tiles, tile, strip).transpose(0, 2, 1).astype(BF16)
    high, *lower = bits_of(n_col)
    half = tiles // 2
    tops = [transpose(own[:slots], m) for m in range(groups)]
    parts = {0: own, high: permute_col(own, high)}
    if lower:
        parts[1] = permute_col(own, 1)
    cot, token = pl.pallas_call(
        functools.partial(unmix_kernel, slabs, tile),
        grid=(tiles,),
        in_specs=[ANY],
        out_specs=[ANY, whole((8, LANES))],
        out_shape=[
            jax.ShapeDtypeStruct((rows, width), BF16),
            jax.ShapeDtypeStruct((8, LANES), F32),
        ],
        scratch_shapes=[
            pltpu.VMEM((mixed, LANES), F32),
            pltpu.VMEM((tiles, mixed, LANES), BF16),
            pltpu.VMEM((tiles, tile, width), BF16),
            pltpu.SemaphoreType.DMA((tiles,)),
            pltpu.SemaphoreType.DMA((tiles,)),
        ],
        compiler_params=params(STREAMED),
        cost_estimate=cost(0, 4 * rows * width),
    )(mixed_rows(cotangent))

    tops, parts, token = lax.optimization_barrier((tops, parts, token))


    top = jnp.stack(tops)
    tops = [top] + [permute_row(top, q) for q in range(1, n_col)]
    for bit in lower:
        for q in range(0, n_col, 2 * bit):
            if q | bit not in parts:
                parts[q | bit] = permute_col(parts[q], bit)

    q_sum, e_part, panel_all, mat = pl.pallas_call(
        functools.partial(q_kernel, n_row, n_col, groups),
        grid=(slabs,),
        in_specs=[SMEM]
        + [whole((tiles, strip, tile))] * n_col
        + [whole((tile, tile)), ANY],
        out_specs=[
            whole((slabs, tile, tile)),
            whole((n_col, groups, slots, strip, tile)),
            whole((tile, rows)),
            whole((2, tile, tile)),
        ],
        out_shape=[
            jax.ShapeDtypeStruct((slabs, tile, tile), BF16),
            jax.ShapeDtypeStruct((n_col, groups, slots, strip, tile), BF16),
            jax.ShapeDtypeStruct((tile, rows), BF16),
            jax.ShapeDtypeStruct((2, tile, tile), BF16),
        ],
        scratch_shapes=[
            pltpu.VMEM((slabs, rows, tile), BF16),
            pltpu.SemaphoreType.DMA((slabs,)),
        ],
        compiler_params=params(STREAMED - 10),
        cost_estimate=cost(2 * rows * width * tile, 2 * rows * (width + tile)),
    )(place, *[parts[q] for q in range(n_col)], inverse, cot)

    w, w_flip, gi = pl.pallas_call(
        functools.partial(w_kernel, n_row, n_col, groups),
        in_specs=[SMEM] + [VMEM] * (n_col + 3) + [ANY],
        out_specs=[VMEM, VMEM, VMEM],
        out_shape=[
            jax.ShapeDtypeStruct((tile, width), BF16),
            jax.ShapeDtypeStruct((width, tile), BF16),
            jax.ShapeDtypeStruct((n_col, strip, tile), BF16),
        ],
        scratch_shapes=[pltpu.VMEM((slabs, tile, tile), BF16)],
        compiler_params=params(),
        cost_estimate=cost(tile, tile),
    )(place, *tops, mat, inverse, q_sum, token)

    def h_part(first, count, flops):
        return pl.pallas_call(
            functools.partial(h_kernel, n_col),
            grid=(count // 2,),
            in_specs=[
                SMEM,
                whole((width, tile)),
                pl.BlockSpec((2 * tile, width), lambda t: (t + first // 2, 0)),
            ],
            out_specs=whole((n_col, count, strip, tile)),
            out_shape=jax.ShapeDtypeStruct((n_col, count, strip, tile), BF16),
            compiler_params=params(),
            cost_estimate=cost(flops, tile),
        )(place, w_flip, cot)

    def update(first, count, previous):
        return pl.pallas_call(
            functools.partial(update_kernel, slabs, tile),
            grid=(count // 2,),
            in_specs=[
                pl.BlockSpec((tile, 2 * tile), lambda t: (0, t + first // 2)),
                whole((tile, width)),
                pl.BlockSpec((2 * mixed, LANES), lambda t: (t + first // 2, 0)),
            ]
            + [ANY] * len(previous),
            out_specs=pl.BlockSpec((2 * mixed, LANES), lambda t: (t + first // 2, 0)),
            out_shape=jax.ShapeDtypeStruct((tiles * mixed, LANES), BF16),
            scratch_shapes=[pltpu.VMEM((2 * mixed, LANES), F32)],
            input_output_aliases={3: 0} if previous else {},
            compiler_params=params(),
            cost_estimate=cost(first * tile * width * tile, 4 * first * tile * width),
        )(panel_all, w, mixed_rows(slab), *previous)

    def halve(value, exchange, bit):
        half = value.shape[0] // 2
        return value[:half].astype(F32) + exchange(value[half:], bit).astype(F32)

    def sum_all(values):
        values = [v.astype(F32) for v in values]
        while len(values) > 1:
            values = [values[i] + values[i + 1] for i in range(0, len(values), 2)]
        return values[0]

    def row_sum(value, bits):
        steps = [sum(b for k, b in enumerate(bits) if (q >> k) & 1) for q in range(1 << len(bits))]
        return sum_all([value] + [permute_row(value, step) for step in steps[1:]])

    col_bits, row_bits = list(reversed(bits_of(n_col))), list(reversed(bits_of(n_row)))
    some = tiles // 4
    e_part = halve(e_part, permute_row, 1).astype(BF16)
    gi = sum_all([gi[0]] + [permute_col(gi[q], q) for q in range(1, n_col)]).astype(BF16)
    h_low = h_part(0, half, tile)
    e_part, gi, h_low, w, w_flip = lax.optimization_barrier((e_part, gi, h_low, w, w_flip))

    gi = row_sum(gi, row_bits[:1]).astype(BF16)
    h_low = halve(h_low, permute_col, 1).astype(BF16)
    for bit in col_bits[1:]:
        e_part = halve(e_part, permute_row, bit).astype(BF16)
    h_high = h_part(half, tiles - half, tile)
    updated = update(0, some, [])
    e_part, gi, h_low, h_high, updated, w = lax.optimization_barrier(
        (e_part, gi, h_low, h_high, updated, w)
    )

    h_high = halve(h_high, permute_col, 1).astype(BF16)
    e_own = sum_all([transpose(e_part[0, m], m, back=True) for m in range(groups)])
    for bit in col_bits[1:]:
        h_low = halve(h_low.astype(BF16), permute_col, bit)
    gi = row_sum(gi, row_bits[1:2])
    updated = update(some, tiles - 2 * some, [updated])
    e_own, gi, h_high, updated, w = lax.optimization_barrier((e_own, gi, h_high, updated, w))

    for bit in col_bits[1:]:
        h_high = halve(h_high.astype(BF16), permute_col, bit)
    for bit in row_bits[2:]:
        gi = row_sum(gi.astype(BF16), [bit])
    updated = update(tiles - some, some, [updated])
    h_low, h_high, e_own, gi, updated = lax.optimization_barrier((h_low, h_high, e_own, gi, updated))
    h = jnp.concatenate([h_low[0], h_high[0]], 0)
    grad_panel = jnp.concatenate([h[:slots] + e_own, h[slots:]], 0)
    updated = updated.reshape(tiles, tile, tile // LANES, slabs, LANES).transpose(0, 1, 3, 2, 4)
    return (
        updated.reshape(slab.shape),
        grad_panel.transpose(0, 2, 1).reshape(panel.shape),
        gi.T,
    )


def solution(mesh):
    in_specs = (
        P(None, "row", None, "col"),
        P(None, "row", None, None, "col", None),
        P(None, "row", None, None, "col", None),
        P(),
    )
    out_specs = (
        P(None, "row", None, None, "col", None),
        P(None, "row", None, "col"),
        P(None, "col"),
    )
    return jax.shard_map(
        per_device, mesh=mesh, in_specs=in_specs, out_specs=out_specs, check_vma=False
    )
```

```python
import functools

import jax
import jax.numpy as jnp
from jax import lax
from jax.experimental import pallas as pl
from jax.experimental.pallas import tpu as pltpu
from jax.sharding import PartitionSpec as P

BOTH = ("row", "col")
F32 = jnp.float32
BF16 = jnp.bfloat16
LANES = 128
VMEM = pl.BlockSpec(memory_space=pltpu.VMEM)
SMEM = pl.BlockSpec(memory_space=pltpu.SMEM)
STREAMED = 58
ANY = pl.BlockSpec(memory_space=pl.ANY)


def bits_of(count):
    return [1 << b for b in reversed(range(count.bit_length() - 1))]


def reversed_bits(value, count):
    width = count.bit_length() - 1
    place = 0
    for b in range(width):
        place = place + (((value >> b) & 1) << (width - 1 - b))
    return place


def dot(a, b, dims, precision=None):
    return lax.dot_general(a, b, (dims, ((), ())), precision=precision, preferred_element_type=F32)


def whole(shape):
    return pl.BlockSpec(shape, lambda *_: (0,) * len(shape))


def params(mib=24):
    return pltpu.CompilerParams(vmem_limit_bytes=mib * 2**20)


def cost(flops, nbytes):
    return pl.CostEstimate(flops=flops, bytes_accessed=nbytes, transcendentals=0)


def unmix_kernel(slabs, tile, x_ref, o_ref, token_ref, wide_ref, ins, outs, in_sems, out_sems):
    step, steps = pl.program_id(0), ins.shape[0]
    size = ins.shape[1]

    def copy_in(t):
        at = pl.multiple_of(t * size, size)
        return pltpu.make_async_copy(x_ref.at[pl.ds(at, size)], ins.at[t], in_sems.at[t])

    def copy_out(t):
        at = pl.multiple_of(t * tile, tile)
        return pltpu.make_async_copy(outs.at[t], o_ref.at[pl.ds(at, tile)], out_sems.at[t])

    @pl.when(step == 0)
    def _():
        for t in range(steps):
            copy_in(t).start()
        token_ref[...] = jnp.zeros_like(token_ref)

    copy_in(step).wait()
    halves = tile // LANES
    wide_ref[...] = ins[step].astype(F32)
    for s in range(slabs):
        for h in range(halves):
            part = wide_ref[pl.ds(h * slabs + s, tile, stride=halves * slabs), :]
            outs[step, :, s * tile + h * LANES : s * tile + (h + 1) * LANES] = part.astype(BF16)
    copy_out(step).start()

    @pl.when(step == steps - 1)
    def _():
        for t in range(steps):
            copy_out(t).wait()


def q_kernel(n_row, n_col, groups, place_ref, *refs):
    parts, (inv_ref, g_ref, q_ref, e_ref, pt_ref, m_ref, ins, sems) = refs[:n_col], refs[n_col:]
    tiles, strip, tile = parts[0].shape
    s = pl.program_id(0)
    row, col = place_ref[0], place_ref[1]
    group, rho = row // n_col, (row % n_col) ^ (n_col // 2)

    def copy_in(at):
        columns = pl.ds(pl.multiple_of(at * tile, tile), tile)
        return pltpu.make_async_copy(g_ref.at[:, columns], ins.at[at], sems.at[at])

    @pl.when(s == 0)
    def _():
        for at in range(ins.shape[0]):
            copy_in(at).start()
        mat = dot(inv_ref[...], inv_ref[...], ((0,), (0,)), lax.Precision.HIGHEST)
        high = mat.astype(BF16)
        m_ref[0] = high
        m_ref[1] = (mat - high.astype(F32)).astype(BF16)
        for q in range(n_col):
            at = pl.multiple_of((col ^ q) * strip, strip)
            for t in range(tiles):
                pt_ref[pl.ds(at, strip), t * tile : (t + 1) * tile] = parts[q][t]

    copy_in(s).wait()
    q_ref[s] = dot(pt_ref[...], ins[s], ((1,), (0,))).astype(BF16)

    @pl.when(s == pl.num_programs(0) - 1)
    def _():
        for at in range(q_ref.shape[0]):
            q_val = q_ref[at]
            e_val = -(dot(m_ref[0], q_val, ((1,), (0,))) + dot(m_ref[1], q_val, ((1,), (0,))))
            e_val = e_val.astype(BF16)
            slot, other = at // groups, group ^ (at % groups)
            for r in range(n_col):
                e_ref[reversed_bits(rho ^ r, n_col), other, slot] = e_val[r * strip : (r + 1) * strip]


def w_kernel(n_row, n_col, groups, place_ref, *refs):
    tops, (m_ref, inv_ref, q_ref, _, w_ref, wt_ref, gi_ref, top_all) = refs[:n_col], refs[n_col:]
    slots, strip, tile = tops[0].shape[1:]
    slabs = slots * groups
    row, col = place_ref[0], place_ref[1]
    group, rho = row // n_col, (row % n_col) ^ (n_col // 2)
    for p in range(n_row):
        at = pl.multiple_of((rho ^ (p % n_col)) * strip, strip)
        for slot in range(slots):
            s = slot * groups + (group ^ (p // n_col))
            top_all[s, pl.ds(at, strip), :] = tops[p % n_col][p // n_col, slot]
    z = jnp.zeros((tile, tile), F32)
    for s in range(slabs):
        top = top_all[s]
        w = dot(m_ref[0], top, ((1,), (0,))) + dot(m_ref[1], top, ((1,), (0,)))
        w = w.astype(BF16)
        w_ref[:, s * tile : (s + 1) * tile] = w
        wt_ref[s * tile : (s + 1) * tile, :] = w.T
        z = z + dot(top, q_ref[s], ((1,), (1,)))
    z = z + z.T
    gi = -dot(z, inv_ref[...], ((1,), (1,)), lax.Precision.HIGHEST)
    for r in range(n_col):
        gi_ref[col ^ r] = gi[r * strip : (r + 1) * strip].astype(BF16)


def h_kernel(n_col, place_ref, wt_ref, g_ref, h_ref):
    strip = h_ref.shape[2]
    t = pl.program_id(0)
    col = place_ref[1]
    tile = h_ref.shape[3]
    pair = -dot(g_ref[...], wt_ref[...], ((1,), (0,)))
    pair = pair.astype(BF16)
    for k in range(2):
        h = pair[k * tile : (k + 1) * tile].T
        for r in range(n_col):
            h_ref[reversed_bits(col ^ r, n_col), 2 * t + k] = h[r * strip : (r + 1) * strip]


def update_kernel(slabs, tile, pt_ref, w_ref, x_ref, *refs):
    o_ref, wide_ref = refs[-2:]
    halves = tile // LANES
    for k in range(2):
        product = dot(pt_ref[:, k * tile : (k + 1) * tile], w_ref[...], ((0,), (0,)))
        for s in range(slabs):
            for h in range(halves):
                part = product[:, s * tile + h * LANES : s * tile + (h + 1) * LANES]
                at = (k * tile * halves + h) * slabs + s
                wide_ref[pl.ds(at, tile, stride=halves * slabs), :] = part
    o_ref[...] = (x_ref[...].astype(F32) - wide_ref[...]).astype(BF16)


def mixed_rows(x):
    tiles, _, tile, slabs, _, _ = x.shape
    x = x.reshape(tiles, tile, slabs, tile // LANES, LANES).transpose(0, 1, 3, 2, 4)
    return x.reshape(-1, LANES)


def per_device(panel, slab, cotangent, inverse):
    tiles, _, tile, strip = panel.shape
    slabs = slab.shape[3]
    n_row = lax.axis_size("row")
    n_col = lax.axis_size("col")
    groups = n_row // n_col
    slots = slabs // groups
    width = slabs * tile
    rows = tiles * tile
    mixed = tile * width // LANES
    place = jnp.stack([lax.axis_index("row"), lax.axis_index("col")]).astype(jnp.int32)

    def permute_row(value, bit):
        return lax.ppermute(value, "row", [(i, i ^ bit) for i in range(n_row)])

    def permute_col(value, bit):
        return lax.ppermute(value, "col", [(i, i ^ bit) for i in range(n_col)])

    far = n_col // 2

    def transpose(value, across, back=False):
        pairs = []
        for m in range(groups):
            for a in range(n_col):
                for b in range(n_col):
                    here = (m * n_col + a) * n_col + b
                    there = ((m ^ across) * n_col + (b ^ far)) * n_col + a
                    pairs.append((there, here) if back else (here, there))
        return lax.ppermute(value, BOTH, pairs)

    own = panel.reshape(tiles, tile, strip).transpose(0, 2, 1).astype(BF16)
    high, *lower = bits_of(n_col)
    half = tiles // 2
    parts = {0: own, high: permute_col(own, high)}
    if lower:
        parts[1] = permute_col(own, 1)
    tops = [transpose(own[:slots], m) for m in range(groups)]
    cot, token = pl.pallas_call(
        functools.partial(unmix_kernel, slabs, tile),
        grid=(tiles,),
        in_specs=[ANY],
        out_specs=[ANY, whole((8, LANES))],
        out_shape=[
            jax.ShapeDtypeStruct((rows, width), BF16),
            jax.ShapeDtypeStruct((8, LANES), F32),
        ],
        scratch_shapes=[
            pltpu.VMEM((mixed, LANES), F32),
            pltpu.VMEM((tiles, mixed, LANES), BF16),
            pltpu.VMEM((tiles, tile, width), BF16),
            pltpu.SemaphoreType.DMA((tiles,)),
            pltpu.SemaphoreType.DMA((tiles,)),
        ],
        compiler_params=params(STREAMED),
        cost_estimate=cost(0, 4 * rows * width),
    )(mixed_rows(cotangent))

    tops, parts, token = lax.optimization_barrier((tops, parts, token))

    top = jnp.stack(tops)
    tops = [top] + [permute_row(top, q) for q in range(1, n_col)]
    for bit in lower:
        for q in range(0, n_col, 2 * bit):
            if q | bit not in parts:
                parts[q | bit] = permute_col(parts[q], bit)

    q_sum, e_part, panel_all, mat = pl.pallas_call(
        functools.partial(q_kernel, n_row, n_col, groups),
        grid=(slabs,),
        in_specs=[SMEM]
        + [whole((tiles, strip, tile))] * n_col
        + [whole((tile, tile)), ANY],
        out_specs=[
            whole((slabs, tile, tile)),
            whole((n_col, groups, slots, strip, tile)),
            whole((tile, rows)),
            whole((2, tile, tile)),
        ],
        out_shape=[
            jax.ShapeDtypeStruct((slabs, tile, tile), BF16),
            jax.ShapeDtypeStruct((n_col, groups, slots, strip, tile), BF16),
            jax.ShapeDtypeStruct((tile, rows), BF16),
            jax.ShapeDtypeStruct((2, tile, tile), BF16),
        ],
        scratch_shapes=[
            pltpu.VMEM((slabs, rows, tile), BF16),
            pltpu.SemaphoreType.DMA((slabs,)),
        ],
        compiler_params=params(STREAMED - 10),
        cost_estimate=cost(2 * rows * width * tile, 2 * rows * (width + tile)),
    )(place, *[parts[q] for q in range(n_col)], inverse, cot)

    w, w_flip, gi = pl.pallas_call(
        functools.partial(w_kernel, n_row, n_col, groups),
        in_specs=[SMEM] + [VMEM] * (n_col + 3) + [ANY],
        out_specs=[VMEM, VMEM, VMEM],
        out_shape=[
            jax.ShapeDtypeStruct((tile, width), BF16),
            jax.ShapeDtypeStruct((width, tile), BF16),
            jax.ShapeDtypeStruct((n_col, strip, tile), BF16),
        ],
        scratch_shapes=[pltpu.VMEM((slabs, tile, tile), BF16)],
        compiler_params=params(),
        cost_estimate=cost(tile, tile),
    )(place, *tops, mat, inverse, q_sum, token)

    def h_part(first, count):
        return pl.pallas_call(
            functools.partial(h_kernel, n_col),
            grid=(count // 2,),
            in_specs=[
                SMEM,
                whole((width, tile)),
                pl.BlockSpec((2 * tile, width), lambda t: (t + first // 2, 0)),
            ],
            out_specs=whole((n_col, count, strip, tile)),
            out_shape=jax.ShapeDtypeStruct((n_col, count, strip, tile), BF16),
            compiler_params=params(),
            cost_estimate=cost(tile, tile),
        )(place, w_flip, cot)

    def update(first, count, previous):
        return pl.pallas_call(
            functools.partial(update_kernel, slabs, tile),
            grid=(count // 2,),
            in_specs=[
                pl.BlockSpec((tile, 2 * tile), lambda t: (0, t + first // 2)),
                whole((tile, width)),
                pl.BlockSpec((2 * mixed, LANES), lambda t: (t + first // 2, 0)),
            ]
            + [ANY] * len(previous),
            out_specs=pl.BlockSpec((2 * mixed, LANES), lambda t: (t + first // 2, 0)),
            out_shape=jax.ShapeDtypeStruct((tiles * mixed, LANES), BF16),
            scratch_shapes=[pltpu.VMEM((2 * mixed, LANES), F32)],
            input_output_aliases={3: 0} if previous else {},
            compiler_params=params(),
            cost_estimate=cost(2 * count * tile * width * tile, 4 * count * tile * width),
        )(panel_all, w, mixed_rows(slab), *previous)

    def halve(value, exchange, bit):
        half = value.shape[0] // 2
        return value[:half].astype(F32) + exchange(value[half:], bit).astype(F32)

    def sum_all(values):
        values = [v.astype(F32) for v in values]
        while len(values) > 1:
            values = [values[i] + values[i + 1] for i in range(0, len(values), 2)]
        return values[0]

    def row_sum(value, bits):
        steps = [sum(b for k, b in enumerate(bits) if (q >> k) & 1) for q in range(1 << len(bits))]
        return sum_all([value] + [permute_row(value, step) for step in steps[1:]])

    col_bits, row_bits = list(reversed(bits_of(n_col))), list(reversed(bits_of(n_row)))
    some = tiles // 2
    e_part = halve(e_part, permute_row, 1).astype(BF16)
    gi = sum_all([gi[0]] + [permute_col(gi[q], q) for q in range(1, n_col)]).astype(BF16)
    h_low = h_part(0, half)
    e_part, gi, h_low, w, w_flip = lax.optimization_barrier((e_part, gi, h_low, w, w_flip))

    gi = row_sum(gi, row_bits[:1]).astype(BF16)
    h_low = halve(h_low, permute_col, 1).astype(BF16)
    h_high = h_part(half, tiles - half)
    e_part, gi, h_low, h_high, w = lax.optimization_barrier((e_part, gi, h_low, h_high, w))

    for bit in col_bits[1:]:
        e_part = halve(e_part, permute_row, bit).astype(BF16)
    h_high = halve(h_high, permute_col, 1).astype(BF16)
    gi = row_sum(gi, row_bits[1:2])
    for bit in col_bits[1:]:
        h_low = halve(h_low.astype(BF16), permute_col, bit)
    updated = update(0, some, [])
    e_part, gi, h_high, updated, w = lax.optimization_barrier((e_part, gi, h_high, updated, w))

    for bit in col_bits[1:]:
        h_high = halve(h_high.astype(BF16), permute_col, bit)
    e_own = sum_all([transpose(e_part[0, m], m, back=True) for m in range(groups)])
    for bit in row_bits[2:]:
        gi = row_sum(gi.astype(BF16), [bit])
    updated = update(some, tiles - some, [updated])
    h_low, h_high, e_own, gi, updated = lax.optimization_barrier((h_low, h_high, e_own, gi, updated))
    h = jnp.concatenate([h_low[0], h_high[0]], 0)
    grad_panel = jnp.concatenate([h[:slots] + e_own, h[slots:]], 0)
    updated = updated.reshape(tiles, tile, tile // LANES, slabs, LANES).transpose(0, 1, 3, 2, 4)
    return (
        updated.reshape(slab.shape),
        grad_panel.transpose(0, 2, 1).reshape(panel.shape),
        gi.T,
    )


def solution(mesh):
    in_specs = (
        P(None, "row", None, "col"),
        P(None, "row", None, None, "col", None),
        P(None, "row", None, None, "col", None),
        P(),
    )
    out_specs = (
        P(None, "row", None, None, "col", None),
        P(None, "row", None, "col"),
        P(None, "col"),
    )
    return jax.shard_map(
        per_device, mesh=mesh, in_specs=in_specs, out_specs=out_specs, check_vma=False
    )
```

```python
import functools

import jax
import jax.numpy as jnp
from jax import lax
from jax.experimental import pallas as pl
from jax.experimental.pallas import tpu as pltpu
from jax.sharding import PartitionSpec as P

BOTH = ("row", "col")
F32 = jnp.float32
BF16 = jnp.bfloat16
LANES = 128
VMEM = pl.BlockSpec(memory_space=pltpu.VMEM)
SMEM = pl.BlockSpec(memory_space=pltpu.SMEM)
STREAMED = 58
ANY = pl.BlockSpec(memory_space=pl.ANY)


def bits_of(count):
    return [1 << b for b in reversed(range(count.bit_length() - 1))]


def reversed_bits(value, count):
    width = count.bit_length() - 1
    place = 0
    for b in range(width):
        place = place + (((value >> b) & 1) << (width - 1 - b))
    return place


def dot(a, b, dims, precision=None):
    return lax.dot_general(a, b, (dims, ((), ())), precision=precision, preferred_element_type=F32)


def whole(shape):
    return pl.BlockSpec(shape, lambda *_: (0,) * len(shape))


def params(mib=24):
    return pltpu.CompilerParams(vmem_limit_bytes=mib * 2**20)


def cost(flops, nbytes):
    return pl.CostEstimate(flops=flops, bytes_accessed=nbytes, transcendentals=0)


def unmix_kernel(slabs, tile, x_ref, o_ref, token_ref, wide_ref, ins, outs, in_sems, out_sems):
    step, steps = pl.program_id(0), ins.shape[0]
    size = ins.shape[1]

    def copy_in(t):
        at = pl.multiple_of(t * size, size)
        return pltpu.make_async_copy(x_ref.at[pl.ds(at, size)], ins.at[t], in_sems.at[t])

    def copy_out(t):
        at = pl.multiple_of(t * tile, tile)
        return pltpu.make_async_copy(outs.at[t], o_ref.at[pl.ds(at, tile)], out_sems.at[t])

    @pl.when(step == 0)
    def _():
        for t in range(steps):
            copy_in(t).start()
        token_ref[...] = jnp.zeros_like(token_ref)

    copy_in(step).wait()
    halves = tile // LANES
    wide_ref[...] = ins[step].astype(F32)
    for s in range(slabs):
        for h in range(halves):
            part = wide_ref[pl.ds(h * slabs + s, tile, stride=halves * slabs), :]
            outs[step, :, s * tile + h * LANES : s * tile + (h + 1) * LANES] = part.astype(BF16)
    copy_out(step).start()

    @pl.when(step == steps - 1)
    def _():
        for t in range(steps):
            copy_out(t).wait()


def q_kernel(n_row, n_col, groups, place_ref, *refs):
    parts, (inv_ref, g_ref, q_ref, e_ref, pt_ref, m_ref, ins, sems) = refs[:n_col], refs[n_col:]
    tiles, strip, tile = parts[0].shape
    s = pl.program_id(0)
    row, col = place_ref[0], place_ref[1]
    group, rho = row // n_col, (row % n_col) ^ (n_col // 2)

    def copy_in(at):
        columns = pl.ds(pl.multiple_of(at * tile, tile), tile)
        return pltpu.make_async_copy(g_ref.at[:, columns], ins.at[at], sems.at[at])

    @pl.when(s == 0)
    def _():
        for at in range(ins.shape[0]):
            copy_in(at).start()
        mat = dot(inv_ref[...], inv_ref[...], ((0,), (0,)), lax.Precision.HIGHEST)
        high = mat.astype(BF16)
        m_ref[0] = high
        m_ref[1] = (mat - high.astype(F32)).astype(BF16)
        for q in range(n_col):
            at = pl.multiple_of((col ^ q) * strip, strip)
            for t in range(tiles):
                pt_ref[pl.ds(at, strip), t * tile : (t + 1) * tile] = parts[q][t]

    copy_in(s).wait()
    q_ref[s] = dot(pt_ref[...], ins[s], ((1,), (0,))).astype(BF16)

    @pl.when(s == pl.num_programs(0) - 1)
    def _():
        for at in range(q_ref.shape[0]):
            q_val = q_ref[at]
            e_val = -(dot(m_ref[0], q_val, ((1,), (0,))) + dot(m_ref[1], q_val, ((1,), (0,))))
            e_val = e_val.astype(BF16)
            slot, other = at // groups, group ^ (at % groups)
            for r in range(n_col):
                e_ref[reversed_bits(rho ^ r, n_col), other, slot] = e_val[r * strip : (r + 1) * strip]


def w_kernel(n_row, n_col, groups, place_ref, *refs):
    tops, (m_ref, inv_ref, q_ref, _, w_ref, wt_ref, gi_ref, top_all) = refs[:n_col], refs[n_col:]
    slots, strip, tile = tops[0].shape[1:]
    slabs = slots * groups
    row, col = place_ref[0], place_ref[1]
    group, rho = row // n_col, (row % n_col) ^ (n_col // 2)
    for p in range(n_row):
        at = pl.multiple_of((rho ^ (p % n_col)) * strip, strip)
        for slot in range(slots):
            s = slot * groups + (group ^ (p // n_col))
            top_all[s, pl.ds(at, strip), :] = tops[p % n_col][p // n_col, slot]
    z = jnp.zeros((tile, tile), F32)
    for s in range(slabs):
        top = top_all[s]
        w = dot(m_ref[0], top, ((1,), (0,))) + dot(m_ref[1], top, ((1,), (0,)))
        w = w.astype(BF16)
        w_ref[:, s * tile : (s + 1) * tile] = w
        wt_ref[s * tile : (s + 1) * tile, :] = w.T
        z = z + dot(top, q_ref[s], ((1,), (1,)))
    z = z + z.T
    gi = -dot(z, inv_ref[...], ((1,), (1,)), lax.Precision.HIGHEST)
    for r in range(n_col):
        gi_ref[col ^ r] = gi[r * strip : (r + 1) * strip].astype(BF16)


def h_kernel(n_col, place_ref, wt_ref, g_ref, h_ref):
    strip = h_ref.shape[2]
    t = pl.program_id(0)
    col = place_ref[1]
    tile = h_ref.shape[3]
    pair = -dot(g_ref[...], wt_ref[...], ((1,), (0,)))
    pair = pair.astype(BF16)
    for k in range(2):
        h = pair[k * tile : (k + 1) * tile].T
        for r in range(n_col):
            h_ref[reversed_bits(col ^ r, n_col), 2 * t + k] = h[r * strip : (r + 1) * strip]


def update_kernel(slabs, tile, pt_ref, w_ref, x_ref, *refs):
    o_ref, wide_ref = refs[-2:]
    halves = tile // LANES
    for k in range(2):
        product = dot(pt_ref[:, k * tile : (k + 1) * tile], w_ref[...], ((0,), (0,)))
        for s in range(slabs):
            for h in range(halves):
                part = product[:, s * tile + h * LANES : s * tile + (h + 1) * LANES]
                at = (k * tile * halves + h) * slabs + s
                wide_ref[pl.ds(at, tile, stride=halves * slabs), :] = part
    o_ref[...] = (x_ref[...].astype(F32) - wide_ref[...]).astype(BF16)


def mixed_rows(x):
    tiles, _, tile, slabs, _, _ = x.shape
    x = x.reshape(tiles, tile, slabs, tile // LANES, LANES).transpose(0, 1, 3, 2, 4)
    return x.reshape(-1, LANES)


def per_device(panel, slab, cotangent, inverse):
    tiles, _, tile, strip = panel.shape
    slabs = slab.shape[3]
    n_row = lax.axis_size("row")
    n_col = lax.axis_size("col")
    groups = n_row // n_col
    slots = slabs // groups
    width = slabs * tile
    rows = tiles * tile
    mixed = tile * width // LANES
    place = jnp.stack([lax.axis_index("row"), lax.axis_index("col")]).astype(jnp.int32)

    def permute_row(value, bit):
        return lax.ppermute(value, "row", [(i, i ^ bit) for i in range(n_row)])

    def permute_col(value, bit):
        return lax.ppermute(value, "col", [(i, i ^ bit) for i in range(n_col)])

    far = n_col // 2

    def transpose(value, across, back=False):
        pairs = []
        for m in range(groups):
            for a in range(n_col):
                for b in range(n_col):
                    here = (m * n_col + a) * n_col + b
                    there = ((m ^ across) * n_col + (b ^ far)) * n_col + a
                    pairs.append((there, here) if back else (here, there))
        return lax.ppermute(value, BOTH, pairs)

    own = panel.reshape(tiles, tile, strip).transpose(0, 2, 1).astype(BF16)
    high, *lower = bits_of(n_col)
    half = tiles // 2
    parts = {0: own, high: permute_col(own, high)}
    if lower:
        parts[1] = permute_col(own, 1)
    tops = [transpose(own[:slots], m) for m in range(groups)]
    cot, token = pl.pallas_call(
        functools.partial(unmix_kernel, slabs, tile),
        grid=(tiles,),
        in_specs=[ANY],
        out_specs=[ANY, whole((8, LANES))],
        out_shape=[
            jax.ShapeDtypeStruct((rows, width), BF16),
            jax.ShapeDtypeStruct((8, LANES), F32),
        ],
        scratch_shapes=[
            pltpu.VMEM((mixed, LANES), F32),
            pltpu.VMEM((tiles, mixed, LANES), BF16),
            pltpu.VMEM((tiles, tile, width), BF16),
            pltpu.SemaphoreType.DMA((tiles,)),
            pltpu.SemaphoreType.DMA((tiles,)),
        ],
        compiler_params=params(STREAMED),
        cost_estimate=cost(0, 4 * rows * width),
    )(mixed_rows(cotangent))

    tops, parts, token = lax.optimization_barrier((tops, parts, token))

    top = jnp.stack(tops)
    tops = [top] + [permute_row(top, q) for q in range(1, n_col)]
    for bit in lower:
        for q in range(0, n_col, 2 * bit):
            if q | bit not in parts:
                parts[q | bit] = permute_col(parts[q], bit)

    q_sum, e_part, panel_all, mat = pl.pallas_call(
        functools.partial(q_kernel, n_row, n_col, groups),
        grid=(slabs,),
        in_specs=[SMEM]
        + [whole((tiles, strip, tile))] * n_col
        + [whole((tile, tile)), ANY],
        out_specs=[
            whole((slabs, tile, tile)),
            whole((n_col, groups, slots, strip, tile)),
            whole((tile, rows)),
            whole((2, tile, tile)),
        ],
        out_shape=[
            jax.ShapeDtypeStruct((slabs, tile, tile), BF16),
            jax.ShapeDtypeStruct((n_col, groups, slots, strip, tile), BF16),
            jax.ShapeDtypeStruct((tile, rows), BF16),
            jax.ShapeDtypeStruct((2, tile, tile), BF16),
        ],
        scratch_shapes=[
            pltpu.VMEM((slabs, rows, tile), BF16),
            pltpu.SemaphoreType.DMA((slabs,)),
        ],
        compiler_params=params(STREAMED - 10),
        cost_estimate=cost(2 * rows * width * tile, 2 * rows * (width + tile)),
    )(place, *[parts[q] for q in range(n_col)], inverse, cot)

    w, w_flip, gi = pl.pallas_call(
        functools.partial(w_kernel, n_row, n_col, groups),
        in_specs=[SMEM] + [VMEM] * (n_col + 3) + [ANY],
        out_specs=[VMEM, VMEM, VMEM],
        out_shape=[
            jax.ShapeDtypeStruct((tile, width), BF16),
            jax.ShapeDtypeStruct((width, tile), BF16),
            jax.ShapeDtypeStruct((n_col, strip, tile), BF16),
        ],
        scratch_shapes=[pltpu.VMEM((slabs, tile, tile), BF16)],
        compiler_params=params(),
        cost_estimate=cost(tile, tile),
    )(place, *tops, mat, inverse, q_sum, token)

    def h_part(first, count):
        return pl.pallas_call(
            functools.partial(h_kernel, n_col),
            grid=(count // 2,),
            in_specs=[
                SMEM,
                whole((width, tile)),
                pl.BlockSpec((2 * tile, width), lambda t: (t + first // 2, 0)),
            ],
            out_specs=whole((n_col, count, strip, tile)),
            out_shape=jax.ShapeDtypeStruct((n_col, count, strip, tile), BF16),
            compiler_params=params(),
            cost_estimate=cost(tile, tile),
        )(place, w_flip, cot)

    def update(first, count, previous):
        return pl.pallas_call(
            functools.partial(update_kernel, slabs, tile),
            grid=(count // 2,),
            in_specs=[
                pl.BlockSpec((tile, 2 * tile), lambda t: (0, t + first // 2)),
                whole((tile, width)),
                pl.BlockSpec((2 * mixed, LANES), lambda t: (t + first // 2, 0)),
            ]
            + [ANY] * len(previous),
            out_specs=pl.BlockSpec((2 * mixed, LANES), lambda t: (t + first // 2, 0)),
            out_shape=jax.ShapeDtypeStruct((tiles * mixed, LANES), BF16),
            scratch_shapes=[pltpu.VMEM((2 * mixed, LANES), F32)],
            input_output_aliases={3: 0} if previous else {},
            compiler_params=params(),
            cost_estimate=cost(2 * count * tile * width * tile, 4 * count * tile * width),
        )(panel_all, w, mixed_rows(slab), *previous)

    def halve(value, exchange, bit):
        half = value.shape[0] // 2
        return value[:half].astype(F32) + exchange(value[half:], bit).astype(F32)

    def sum_all(values):
        values = [v.astype(F32) for v in values]
        while len(values) > 1:
            values = [values[i] + values[i + 1] for i in range(0, len(values), 2)]
        return values[0]

    def row_sum(value, bits):
        steps = [sum(b for k, b in enumerate(bits) if (q >> k) & 1) for q in range(1 << len(bits))]
        return sum_all([value] + [permute_row(value, step) for step in steps[1:]])

    col_bits, row_bits = list(reversed(bits_of(n_col))), list(reversed(bits_of(n_row)))
    some = tiles * 3 // 4
    e_part = halve(e_part, permute_row, 1).astype(BF16)
    gi = sum_all([gi[0]] + [permute_col(gi[q], q) for q in range(1, n_col)]).astype(BF16)
    h_low = h_part(0, half)
    e_part, gi, h_low, w, w_flip = lax.optimization_barrier((e_part, gi, h_low, w, w_flip))

    gi = row_sum(gi, row_bits[:1]).astype(BF16)
    h_low = halve(h_low, permute_col, 1).astype(BF16)
    h_high = h_part(half, tiles - half)
    e_part, gi, h_low, h_high, w = lax.optimization_barrier((e_part, gi, h_low, h_high, w))

    for bit in col_bits[1:]:
        e_part = halve(e_part, permute_row, bit).astype(BF16)
    h_high = halve(h_high, permute_col, 1).astype(BF16)
    gi = row_sum(gi, row_bits[1:2])
    for bit in col_bits[1:]:
        h_low = halve(h_low.astype(BF16), permute_col, bit)
    updated = update(0, some, [])
    e_part, gi, h_high, updated, w = lax.optimization_barrier((e_part, gi, h_high, updated, w))

    for bit in col_bits[1:]:
        h_high = halve(h_high.astype(BF16), permute_col, bit)
    e_own = sum_all([transpose(e_part[0, m], m, back=True) for m in range(groups)])
    for bit in row_bits[2:]:
        gi = row_sum(gi.astype(BF16), [bit])
    updated = update(some, tiles - some, [updated])
    h_low, h_high, e_own, gi, updated = lax.optimization_barrier((h_low, h_high, e_own, gi, updated))
    h = jnp.concatenate([h_low[0], h_high[0]], 0)
    grad_panel = jnp.concatenate([h[:slots] + e_own, h[slots:]], 0)
    updated = updated.reshape(tiles, tile, tile // LANES, slabs, LANES).transpose(0, 1, 3, 2, 4)
    return (
        updated.reshape(slab.shape),
        grad_panel.transpose(0, 2, 1).reshape(panel.shape),
        gi.T,
    )


def solution(mesh):
    in_specs = (
        P(None, "row", None, "col"),
        P(None, "row", None, None, "col", None),
        P(None, "row", None, None, "col", None),
        P(),
    )
    out_specs = (
        P(None, "row", None, None, "col", None),
        P(None, "row", None, "col"),
        P(None, "col"),
    )
    return jax.shard_map(
        per_device, mesh=mesh, in_specs=in_specs, out_specs=out_specs, check_vma=False
    )
```
